32 devices in a mesh: groups: 2 (over x), section: 1, expert: 16 (over z, y, core).
Axes of the slice: x: 2, y: 2, z: 4, core: 2. Of those that a mesh axis runs over, the one named last changes fastest.
Arguments:
- inputs: bfloat16 [2, 512, 2048], P(None, ('groups', 'expert')), parts along dimension 1, may hold values from -6 to 6
- routes: int32 [2, 2, 512, 8], P('section', None, ('groups', 'expert')), parts along dimension 2, may hold values from 0 to 15, all different within a row; in each aligned block of 16 rows (0 to 15, 16 to 31, ..., all dimensions but the last counted through in order) at most 16 rows name the same one
- norm_gain: float32 [2, 2048], P('section'), may hold values from 0.1 to 1.9
- w_gate_up: bfloat16 [2, 16, 2048, 1536], P('section', 'expert'), may hold values from -0.125 to 0.125
- w_down: bfloat16 [2, 16, 768, 2048], P('section', 'expert'), may hold values from -0.4375 to 0.4375
Outputs:
- outputs: bfloat16 [2, 2, 512, 2048], P('section', None, ('groups', 'expert')), parts along dimension 2
The draws below stay inside these ranges and needn't reach their ends.
There are 2 independent parts, one for each index of `groups`. The reference program is written for one: setup_inputs(seed, part) draws one part's arguments, and reference() takes and returns one part's arrays. A program takes and returns all parts, laid end to end along the dimension named above; an argument that names none is the same for every part. Nothing has to cross between parts.
Inputs may be any that keep to these rules, and one draw needn't show every extreme that they name: `routes`: the 8 entries of a row differ. In each aligned block of 16 rows (the rows of one index of expert in one micro-batch of one layer) no expert is named by more than 16 rows, and some block reaches 16.
All inputs are finite; a program needn't handle non-finite values.
Results may differ from the reference program's by a relative error of at most 0.0055.
Values may be sent and summed in bfloat16 or wider, within the bound.
No kernel may reach another device: no remote copies, remote signals or barrier semaphores. Data moves between devices by JAX's collectives and lax.ppermute only.
A program may use at most 64 MiB of HBM per device.

```python
import math
import jax
import jax.numpy as jnp
import numpy as np
from jax import lax

D = 2048
F = 768
TOP = 8
MB = 2
TOK_MB = 16
EXPERTS = 16
TOKENS = 256
CAP = 16


def block_levels(own_key, extent, cuts, least, largest):
    level = 1.0
    for position, shards_of in cuts:
        steps = jax.random.uniform(jax.random.fold_in(jax.random.fold_in(own_key, 6), position), (shards_of,), jnp.float32, least / len(cuts), largest / len(cuts))
        level = level * jnp.repeat(jnp.exp(steps), extent[position] // shards_of).reshape((-1,) + (1,) * (len(extent) - 1 - position))
    return level


def deal_out(stream_key, own, number, rows, number_of, top, most, skew):
    order = jax.random.permutation(stream_key, number_of)
    crowded, usual = load_shares(number_of, rows * top, most, skew, True), load_shares(number_of, rows * top, most, skew, False)
    places = jnp.arange(number_of)

    def named(tallies, rotation):
        used = int((tallies > 0).sum())
        fixed = max(1, used // 4)
        moved = fixed + (places - fixed + rotation * (used - fixed)) % max(1, number_of - fixed)
        return jnp.zeros((number_of,), jnp.int32).at[order[jnp.where(places < fixed, places, moved)]].set(jnp.asarray(tallies, jnp.int32))

    tallies = jnp.where(number % 4 == 0, named(crowded, number // 4), named(usual, number - number // 4 - 1))
    mixed = jax.random.permutation(jax.random.fold_in(own, 3), number_of)
    giver, sink = mixed[0:number_of // 2 * 2:2], mixed[1:number_of // 2 * 2:2]
    slack = jnp.minimum(tallies[giver] - 1, most - tallies[sink]) // 2
    slack = jnp.where((giver == order[0]) | (sink == order[0]) | (tallies[sink] == 0), 0, jnp.maximum(slack, 0))
    moved = jax.random.randint(jax.random.fold_in(own, 4), (number_of // 2,), 0, 1 << 20) % (slack + 1)
    tallies = tallies.at[giver].add(-moved).at[sink].add(moved)
    items = jnp.searchsorted(jnp.cumsum(tallies), jnp.arange(rows * top), side="right").astype(jnp.int32)
    listing = items.reshape(top, rows).T
    listing = listing[jax.random.permutation(jax.random.fold_in(own, 1), rows)]
    rotation = jax.random.randint(jax.random.fold_in(own, 2), (rows, 1), 0, top)
    return jnp.take_along_axis(listing, (jnp.arange(top)[None, :] + rotation) % top, axis=1)


def load_shares(amount, total, most, skew, full):
    weights = [(1 << 20) // math.isqrt(grade ** skew) + 1 for grade in range(1, amount + 1)]
    largest = most if full else min(most, max(-(-total // amount), total * weights[0] // sum(weights)))
    least = 1 if total - largest >= amount - 1 else 0
    given, spare = [largest] + [least] * (amount - 1), total - largest - least * (amount - 1)
    while spare > 0:
        candidates = [i for i in range(1, amount) if given[i] < largest] or [i for i in range(1, amount) if given[i] < most]
        pool, budget = sum([weights[i] for i in candidates]), spare
        for i in candidates:
            addition = min(most - given[i], max(1, budget * weights[i] // pool), spare)
            given[i] = given[i] + addition
            spare = spare - addition
    return np.array(given)


def gaussian(stream_key, extent, deviation, bound, split=(), held_as=jnp.bfloat16):
    level = block_levels(stream_key, extent, split, -0.22, 0.18) if split else 1.0
    drawn = jax.random.normal(stream_key, extent, jnp.float32) * deviation * level
    return jnp.minimum(jnp.maximum(drawn, -bound), bound).astype(held_as)


def setup_inputs(seed: int = 0, part: int = 0) -> dict:
    splits = jax.random.split(jax.random.key(seed), 6)
    part_splits = jax.random.split(jax.random.fold_in(splits[5], part), 6)
    inputs = gaussian(part_splits[0], (MB, TOKENS, D), 1.0, 6.0, ((1, 16),))
    routes_keys = jax.random.split(jax.random.fold_in(part_splits[1], 1), 2 * MB * TOKENS // TOK_MB)
    routes_turns = jax.random.permutation(jax.random.fold_in(part_splits[1], 3), 2 * MB * TOKENS // TOK_MB)
    routes = jax.vmap(lambda own, number: deal_out(jax.random.fold_in(part_splits[1], 2), own, number, TOK_MB, EXPERTS, TOP, CAP, 2))(routes_keys, routes_turns).reshape((2, MB, TOKENS, TOP))
    norm_gain = jnp.clip(1.0 + 0.18 * jax.random.normal(splits[2], (2, D), jnp.float32), 0.1, 1.9)
    w_gate_up = gaussian(splits[3], (2, EXPERTS, D, 2 * F), D ** -0.5, 0.125, ((1, 16),))
    w_down = gaussian(splits[4], (2, EXPERTS, F, D), (F // 4) ** -0.5, 0.4375, ((1, 16),))
    return dict(inputs=inputs, routes=routes, norm_gain=norm_gain, w_gate_up=w_gate_up, w_down=w_down)


eps = 1e-06

def expert_ffn(rows, gate_up, down_proj):
    joined = jnp.dot(rows.astype(jnp.float32), gate_up.astype(jnp.float32))
    hidden = (jax.nn.silu(joined[:, :F]) * joined[:, F:]).astype(jnp.bfloat16)
    return jnp.dot(hidden.astype(jnp.float32), down_proj.astype(jnp.float32)).astype(jnp.bfloat16)

def moe_layer(current, layer_routes, gain_row, gate_up, down_proj):
    widened = current.astype(jnp.float32)
    scale_inv = lax.rsqrt(lax.optimization_barrier(jnp.mean(widened * widened, axis=-1, keepdims=True)) + eps)
    normed = (widened * scale_inv * gain_row).astype(jnp.bfloat16)
    flat_routes = layer_routes.reshape(-1).astype(jnp.int32)
    expert_ids = jnp.arange(EXPERTS, dtype=jnp.int32)
    onehot = (flat_routes[:, None] == expert_ids[None, :]).astype(jnp.int32)
    before = jnp.cumsum(onehot, axis=0) - onehot
    rank_of = lax.optimization_barrier(jnp.sum(before * onehot, axis=1))
    room = EXPERTS * CAP
    target = (flat_routes * room + rank_of).astype(jnp.int32)
    source = jnp.repeat(normed, TOP, axis=0)
    buffer = jnp.zeros((EXPERTS * room, D), jnp.bfloat16).at[target].set(source)
    results = lax.map(lambda packed: expert_ffn(packed[0], packed[1], packed[2]), (buffer.reshape(EXPERTS, room, D), gate_up, down_proj))
    picked = results.reshape(EXPERTS * room, D)[target].reshape(TOKENS, TOP, D).astype(jnp.float32)
    combined = lax.optimization_barrier(jnp.sum(picked, axis=1)) * 0.125
    return (widened + combined).astype(jnp.bfloat16)

def reference(inputs, routes, norm_gain, w_gate_up, w_down):
    first_layer = []
    for batch_no in range(MB):
        first_layer.append(moe_layer(inputs[batch_no], routes[0, batch_no], norm_gain[0], w_gate_up[0], w_down[0]))
    second_layer = []
    for batch_no in range(MB):
        second_layer.append(moe_layer(first_layer[batch_no], routes[1, batch_no], norm_gain[1], w_gate_up[1], w_down[1]))
    return jnp.stack([jnp.stack(first_layer), jnp.stack(second_layer)])
```

```python
import jax
import jax.numpy as jnp
from jax import lax
from jax.experimental import pallas as pl
from jax.experimental.pallas import tpu as pltpu
from jax.sharding import PartitionSpec as P

eps = 1e-06
LANES = 128


def from_behind(value, axis, steps):
    count = lax.axis_size(axis)
    initial, last = (max(0, -steps), min(count, count - steps))
    return lax.ppermute(value, axis, [(source, source + steps) for source in range(initial, last)])


def levels(count):
    found, stride = [], 1
    for _ in range(2):
        radix = 2 if (count // stride) % 2 == 0 else 1
        found.append((stride, radix))
        stride *= radix
    found.append((stride, count // stride))
    return found


def swap(value, level, step, back=False):
    count = lax.axis_size("expert")
    stride, radix = level

    def partner(index):
        digit = index // stride % radix
        if radix & (radix - 1) == 0:
            other = digit ^ step
        else:
            other = (digit + (step if back else radix - step)) % radix
        return index + (other - digit) * stride

    return lax.ppermute(value, "expert", [(i, partner(i)) for i in range(count)])


def gather_rows(rows):
    for level in levels(lax.axis_size("expert"))[::-1]:
        if level[1] > 1:
            rows = jnp.concatenate([rows] + [swap(rows, level, k) for k in range(1, level[1])])
    return rows


def return_rows(mine, other):
    first, second, third = levels(lax.axis_size("expert"))
    total = mine
    if first[1] > 1:
        total = total + swap(other, first, 1, True).astype(jnp.float32)
    for level in (second, third):
        radix = level[1]
        part = total.shape[0] // radix
        arrived = [
            swap(total[k * part : (k + 1) * part].astype(jnp.bfloat16), level, k, True)
            for k in range(1, radix)
        ]
        total = total[:part]
        for piece in arrived:
            total = total + piece.astype(jnp.float32)
    return total


def expert_kernel(column_ref, rows_ref, routed_ref, gate_up_ref, down_ref, mine_ref, other_ref):
    hidden_size, features = down_ref.shape
    rows = rows_ref[...]
    places = lax.broadcasted_iota(jnp.int32, routed_ref.shape, 1)
    routed = jnp.where(places == column_ref[0], routed_ref[...].astype(jnp.float32), 0.0)
    share = jnp.sum(routed, axis=1, keepdims=True)
    gate = jnp.dot(rows, gate_up_ref[:, :hidden_size], preferred_element_type=jnp.float32)
    up = jnp.dot(rows, gate_up_ref[:, hidden_size:], preferred_element_type=jnp.float32)
    hidden = (gate / (1.0 + jnp.exp(-gate)) * up).astype(jnp.bfloat16)
    done = jnp.dot(hidden, down_ref[...], preferred_element_type=jnp.float32) * share
    half = mine_ref.shape[0]
    mine_ref[...] = done[:half]
    if half < rows.shape[0]:
        other_ref[...] = done[half:].astype(jnp.bfloat16)
    else:
        other_ref[...] = jnp.zeros_like(other_ref)


def run_expert(rows, routed, column, gate_up, down_proj):
    count, features = rows.shape
    half = count // levels(lax.axis_size("expert"))[0][1]
    vmem = pl.BlockSpec(memory_space=pltpu.VMEM)
    return pl.pallas_call(
        expert_kernel,
        out_shape=(
            jax.ShapeDtypeStruct((half, features), jnp.float32),
            jax.ShapeDtypeStruct((half, features), jnp.bfloat16),
        ),
        in_specs=[pl.BlockSpec(memory_space=pltpu.SMEM)] + [vmem] * 4,
        out_specs=(vmem, vmem),
        compiler_params=pltpu.CompilerParams(vmem_limit_bytes=48 * 2**20),
    )(column, rows, routed, gate_up, down_proj)


def norm_rows(current, gain_row):
    widened = current.astype(jnp.float32)
    scale_inv = lax.rsqrt(jnp.mean(widened * widened, axis=-1, keepdims=True) + eps)
    return (widened * scale_inv * gain_row).astype(jnp.bfloat16)


def route_columns(routes, experts):
    layers, batches, tokens, _ = routes.shape
    ids = jnp.arange(experts, dtype=jnp.int32)
    named = jnp.any(routes[..., None] == ids, axis=3).astype(jnp.bfloat16)
    flat = named.transpose(2, 0, 1, 3).reshape(tokens, layers * batches * experts)
    return jnp.pad(flat, ((0, 0), (0, -flat.shape[1] % LANES)))


def moe_layer(current, rows, routed, column, gate_up, down_proj):
    mine, other = run_expert(rows, routed, column, gate_up, down_proj)
    combined = return_rows(mine, other) * 0.125
    return (current.astype(jnp.float32) + combined).astype(jnp.bfloat16)


def on_device(inputs, routes, norm_gain, w_gate_up, w_down):
    experts = lax.axis_size("expert")
    sections = lax.axis_size("section")
    me = lax.axis_index("expert")
    batches, tokens, features = inputs.shape
    columns = route_columns(routes, experts)

    def column_of(layer_no, batch_no):
        return ((layer_no * batches + batch_no) * experts + me).astype(jnp.int32).reshape(1)

    if sections == 1:
        layers_out = []
        previous = [inputs[batch_no] for batch_no in range(batches)]
        routed = None
        for layer_no in range(routes.shape[0]):
            current_layer = []
            for batch_no in range(batches):
                current = previous[batch_no]
                normed = norm_rows(current, norm_gain[layer_no])
                if routed is None:
                    wide = gather_rows(jnp.concatenate([normed, columns], axis=1))
                    rows, routed = wide[:, :features], wide[:, features:]
                else:
                    rows = gather_rows(normed)
                current_layer.append(
                    moe_layer(
                        current,
                        rows,
                        routed,
                        column_of(layer_no, batch_no),
                        w_gate_up[layer_no, 0],
                        w_down[layer_no, 0],
                    )
                )
            layers_out.append(jnp.stack(current_layer))
            previous = current_layer
        return jnp.stack(layers_out)
    segment_no = lax.axis_index("section")
    routed = gather_rows(columns)
    handed = jnp.zeros((tokens, features), jnp.bfloat16)
    finished = []
    for turn_no in range(batches + 1):
        if turn_no < batches:
            fresh_rows = inputs[turn_no]
        else:
            fresh_rows = jnp.zeros((tokens, features), jnp.bfloat16)
        current = jnp.where(segment_no == 0, fresh_rows, handed)
        batch_pick = jnp.clip(turn_no - segment_no, 0, batches - 1)
        rows = gather_rows(norm_rows(current, norm_gain[0]))
        result = moe_layer(
            current, rows, routed, column_of(0, batch_pick), w_gate_up[0, 0], w_down[0, 0]
        )
        finished.append(result)
        if turn_no < batches:
            handed = from_behind(result, "section", 1)
    first_segment = jnp.stack(finished[:batches])
    second_segment = jnp.stack(finished[1:])
    return jnp.where(segment_no == 0, first_segment, second_segment)[None]


def solution(mesh):
    placed = (
        P(None, ("groups", "expert"), None),
        P("section", None, ("groups", "expert"), None),
        P("section", None),
        P("section", "expert", None, None),
        P("section", "expert", None, None),
    )
    return jax.shard_map(
        on_device,
        mesh=mesh,
        in_specs=placed,
        out_specs=P("section", None, ("groups", "expert"), None),
        check_vma=False,
    )
```

```python
import functools

import jax
import jax.numpy as jnp
from jax import lax
from jax.experimental import pallas as pl
from jax.experimental.pallas import tpu as pltpu
from jax.sharding import PartitionSpec as P

eps = 1e-06
LANES = 128
MIB = 2**20
VMEM = pl.BlockSpec(memory_space=pltpu.VMEM)
SMEM = pl.BlockSpec(memory_space=pltpu.SMEM)
ANY = pl.BlockSpec(memory_space=pl.ANY)
bf16, f32 = jnp.bfloat16, jnp.float32


def from_behind(value, axis, steps):
    count = lax.axis_size(axis)
    initial, last = (max(0, -steps), min(count, count - steps))
    return lax.ppermute(value, axis, [(source, source + steps) for source in range(initial, last)])


def call(kernel, outs, specs, *operands, scratch=(), limit=8, flops=0):
    shapes = tuple(jax.ShapeDtypeStruct(shape, dtype) for shape, dtype in outs)
    moved = sum(x.size * x.dtype.itemsize for x in operands + shapes)
    return pl.pallas_call(
        kernel,
        out_shape=shapes,
        in_specs=specs,
        out_specs=(VMEM,) * len(outs),
        scratch_shapes=scratch,
        compiler_params=pltpu.CompilerParams(vmem_limit_bytes=limit * MIB),
        cost_estimate=pl.CostEstimate(flops=flops, bytes_accessed=moved, transcendentals=0),
    )(*operands)


def swap(value, stride, step, radix, back=False):
    count = lax.axis_size("expert")

    def partner(index):
        digit = index // stride % radix
        if radix & (radix - 1) == 0:
            other = digit ^ step
        else:
            other = (digit + (step if back else radix - step)) % radix
        return index + (other - digit) * stride

    return lax.ppermute(value, "expert", [(i, partner(i)) for i in range(count)])


def join_kernel(*refs):
    *parts, whole = refs
    rows = parts[0].shape[0]
    for k, part in enumerate(parts):
        whole[k * rows : (k + 1) * rows] = part[...]


def gather_rows(rows):
    far = lax.axis_size("expert") // 4
    tokens, width = rows.shape
    parts = [rows] + [swap(rows, 4, k, far) for k in range(1, far)]
    (near,) = call(join_kernel, [((far * tokens, width), rows.dtype)], [VMEM] * far, *parts)
    beside = swap(near, 2, 1, 2)
    return [near, beside, swap(near, 1, 1, 2), swap(beside, 1, 1, 2)]


def sum_kernel(mine, arrived, total):
    total[...] = (mine[...] + arrived[...].astype(f32)).astype(total.dtype)


def split_kernel(mine, near, beside, kept, *sent):
    rows = kept.shape[0]
    total = mine[...] + near[...].astype(f32) + beside[...].astype(f32)
    kept[...] = total[:rows]
    for k, piece in enumerate(sent, 1):
        piece[...] = total[k * rows : (k + 1) * rows].astype(piece.dtype)


def return_rows(mine_near, mine_beside, other_near, other_beside):
    far = lax.axis_size("expert") // 4
    shape = mine_near.shape
    tokens, width = shape[0] // far, shape[1]
    arrived_beside = swap(other_beside, 1, 1, 2, True)
    arrived_near = swap(other_near, 1, 1, 2, True)
    (leaving,) = call(sum_kernel, [(shape, bf16)], [VMEM] * 2, mine_beside, arrived_beside)
    beside = swap(leaving, 2, 1, 2, True)
    kept, *sent = call(
        split_kernel,
        [((tokens, width), f32)] + [((tokens, width), bf16)] * (far - 1),
        [VMEM] * 3,
        mine_near,
        arrived_near,
        beside,
    )
    return [kept] + [swap(piece, 4, k, far, True) for k, piece in enumerate(sent, 1)]


def normed_rows(widened, gain_row):
    scale_inv = lax.rsqrt(jnp.mean(widened * widened, axis=-1, keepdims=True) + eps)
    return (widened * scale_inv * gain_row).astype(bf16)


def open_kernel(batch_no, experts, current_ref, routes_ref, gain_ref, wide_ref):
    features = current_ref.shape[-1]
    rows = current_ref[...] if batch_no is None else current_ref[batch_no]
    wide_ref[:, :features] = normed_rows(rows.astype(f32), gain_ref[0:1])
    layers, batches, tokens, top = routes_ref.shape
    places = lax.broadcasted_iota(jnp.int32, (tokens, wide_ref.shape[1] - features), 1)
    chosen = jnp.zeros(places.shape, f32)
    for layer_no in range(layers):
        for batch in range(batches):
            named = routes_ref[layer_no, batch] + (layer_no * batches + batch) * experts
            for k in range(top):
                chosen = jnp.where(places == named[:, k : k + 1], 1.0, chosen)
    wide_ref[:, features:] = chosen.astype(bf16)


def norm_kernel(batch_no, layer_no, current_ref, gain_ref, normed_ref):
    normed_ref[...] = normed_rows(
        current_ref[batch_no].astype(f32), gain_ref[layer_no : layer_no + 1]
    )


def total_rows(current, kept, sent):
    total = kept[...]
    for piece in sent:
        total = total + piece[...].astype(f32)
    return (current.astype(f32) + total * 0.125).astype(bf16)


def close_kernel(batch_no, layer_no, current_ref, gain_ref, kept, *refs):
    *sent, out_ref, normed_ref = refs
    current = current_ref[...] if batch_no is None else current_ref[batch_no]
    out = total_rows(current, kept, sent)
    out_ref[...] = out
    normed_ref[...] = normed_rows(out.astype(f32), gain_ref[layer_no : layer_no + 1])


def end_kernel(earlier, current_ref, kept, *refs):
    sent, before, outs_ref = refs[: -earlier - 1], refs[-earlier - 1 : -1], refs[-1]
    layers, batches = outs_ref.shape[:2]
    for place, done in enumerate(before):
        outs_ref[place // batches, place % batches] = done[...]
    outs_ref[earlier // batches, earlier % batches] = total_rows(current_ref[...], kept, sent)


def load_kernel(layer_no, cuts, gate_up_hbm, down_hbm, gate_up_ref, down_ref, sems):
    copies = []
    for source, target in ((gate_up_hbm, gate_up_ref), (down_hbm, down_ref)):
        rows = target.shape[0] // cuts
        for cut in range(cuts):
            span = pl.ds(cut * rows, rows)
            copies.append(
                pltpu.make_async_copy(
                    source.at[layer_no, 0, span], target.at[span], sems.at[len(copies)]
                )
            )
    for copy in copies:
        copy.start()
    for copy in copies:
        copy.wait()


def load_weights(layer_no, w_gate_up, w_down):
    cuts = 4
    return call(
        functools.partial(load_kernel, layer_no, cuts),
        [(w_gate_up.shape[2:], bf16), (w_down.shape[2:], bf16)],
        [ANY] * 2,
        w_gate_up,
        w_down,
        scratch=[pltpu.SemaphoreType.DMA((2 * cuts,))],
        limit=12,
    )


def tile_of(extent, most):
    size = most
    while extent % size:
        size //= 2
    return size


def expert_kernel(first_column, wide, me_ref, *refs):
    if wide:
        parts, refs = refs[:4], refs[4:]
        gate_up_ref, down_ref, *outs, routed_ref, rows_ref, hidden_ref = refs
    else:
        parts, refs = refs[:4], refs[4:]
        routed_ref, gate_up_ref, down_ref, *outs, rows_ref, hidden_ref = refs
    hidden_size, features = down_ref.shape
    quarter = parts[0].shape[0]
    for k, part in enumerate(parts):
        span = slice(k * quarter, (k + 1) * quarter)
        rows_ref[span] = part[:, :features]
        if wide:
            routed_ref[span] = part[:, features:]
    places = lax.broadcasted_iota(jnp.int32, routed_ref.shape, 1)
    chosen = jnp.where(places == me_ref[0] + first_column, routed_ref[...].astype(f32), 0.0)
    share = jnp.sum(chosen, axis=1, keepdims=True)
    rows = rows_ref[...]
    size = tile_of(hidden_size, 256)
    for low in range(0, hidden_size, size):
        span, beside = slice(low, low + size), slice(hidden_size + low, hidden_size + low + size)
        gate = jnp.dot(rows, gate_up_ref[:, span], preferred_element_type=f32)
        up = jnp.dot(rows, gate_up_ref[:, beside], preferred_element_type=f32)
        hidden_ref[:, span] = (gate / (1.0 + jnp.exp(-gate)) * up).astype(bf16)
    hidden = hidden_ref[...]
    size = tile_of(features, 512)
    for low in range(0, features, size):
        span = slice(low, low + size)
        done = jnp.dot(hidden, down_ref[:, span], preferred_element_type=f32) * share
        for k, out in enumerate(outs):
            out[:, span] = done[k * quarter : (k + 1) * quarter].astype(out.dtype)


def run_expert(parts, routed, me, first_column, weights):
    gate_up, down_proj = weights
    hidden_size, features = down_proj.shape
    quarter, width = parts[0].shape
    count = 4 * quarter
    wide = routed is None
    outs = [((quarter, features), f32)] * 2 + [((quarter, features), bf16)] * 2
    if wide:
        outs = outs + [((count, width - features), bf16)]
    found = call(
        functools.partial(expert_kernel, first_column, wide),
        outs,
        [SMEM] + [VMEM] * (6 if wide else 7),
        me,
        *parts,
        *([] if wide else [routed]),
        gate_up,
        down_proj,
        scratch=[pltpu.VMEM((count, features), bf16), pltpu.VMEM((count, hidden_size), bf16)],
        limit=24,
        flops=6 * count * features * hidden_size,
    )
    return found[:4], found[4] if wide else routed


def open_rows(batch_no, current, routes, gain, experts):
    tokens, features = current.shape[-2:]
    columns = routes.shape[0] * routes.shape[1] * experts
    width = features + columns + -columns % LANES
    (wide,) = call(
        functools.partial(open_kernel, batch_no, experts),
        [((tokens, width), bf16)],
        [VMEM] * 3,
        current,
        routes,
        gain,
    )
    return wide


def close_rows(batch_no, layer_no, current, gain, returned):
    shape = current.shape[-2:]
    return call(
        functools.partial(close_kernel, batch_no, layer_no),
        [(shape, bf16)] * 2,
        [VMEM] * (2 + len(returned)),
        current,
        gain,
        *returned,
    )


def on_device(inputs, routes, norm_gain, w_gate_up, w_down):
    experts = lax.axis_size("expert")
    sections = lax.axis_size("section")
    me = lax.axis_index("expert").astype(jnp.int32).reshape(1)
    batches, tokens, features = inputs.shape
    layers = routes.shape[0]
    weights = [load_weights(layer_no, w_gate_up, w_down) for layer_no in range(layers)]
    if sections == 1:
        outs, routed = [], None
        currents = [inputs] * batches
        normed = [open_rows(0, inputs, routes, norm_gain, experts)]
        for batch_no in range(1, batches):
            normed += call(
                functools.partial(norm_kernel, batch_no, 0),
                [((tokens, features), bf16)],
                [VMEM] * 2,
                inputs,
                norm_gain,
            )
        for layer_no in range(layers):
            for batch_no in range(batches):
                column = (layer_no * batches + batch_no) * experts
                parts = gather_rows(normed[batch_no])
                found, routed = run_expert(parts, routed, me, column, weights[layer_no])
                returned = return_rows(*found)
                current = currents[batch_no]
                if len(outs) == layers * batches - 1:
                    (whole,) = call(
                        functools.partial(end_kernel, len(outs)),
                        [((layers, batches, tokens, features), bf16)],
                        [VMEM] * (1 + len(returned) + len(outs)),
                        current,
                        *returned,
                        *outs,
                    )
                    return whole
                which = batch_no if layer_no == 0 else None
                following = min(layer_no + 1, layers - 1)
                done, after = close_rows(which, following, current, norm_gain, returned)
                outs.append(done)
                currents[batch_no], normed[batch_no] = done, after
    segment_no = lax.axis_index("section")
    handed = jnp.zeros((tokens, features), bf16)
    finished = []
    for turn_no in range(batches + 1):
        if turn_no < batches:
            fresh_rows = inputs[turn_no]
        else:
            fresh_rows = jnp.zeros((tokens, features), bf16)
        current = jnp.where(segment_no == 0, fresh_rows, handed)
        batch_pick = jnp.clip(turn_no - segment_no, 0, batches - 1)
        parts = gather_rows(open_rows(None, current, routes, norm_gain, experts))
        found, _ = run_expert(parts, None, me + batch_pick * experts, 0, weights[0])
        result, _ = close_rows(None, 0, current, norm_gain, return_rows(*found))
        finished.append(result)
        if turn_no < batches:
            handed = from_behind(result, "section", 1)
    first_segment = jnp.stack(finished[:batches])
    second_segment = jnp.stack(finished[1:])
    return jnp.where(segment_no == 0, first_segment, second_segment)[None]


def solution(mesh):
    placed = (
        P(None, ("groups", "expert"), None),
        P("section", None, ("groups", "expert"), None),
        P("section", None),
        P("section", "expert", None, None),
        P("section", "expert", None, None),
    )
    return jax.shard_map(
        on_device,
        mesh=mesh,
        in_specs=placed,
        out_specs=P("section", None, ("groups", "expert"), None),
        check_vma=False,
    )
```

```python
import functools

import jax
import jax.numpy as jnp
from jax import lax
from jax.experimental import pallas as pl
from jax.experimental.pallas import tpu as pltpu
from jax.sharding import PartitionSpec as P

eps = 1e-06
LANES = 128
MIB = 2**20
VMEM = pl.BlockSpec(memory_space=pltpu.VMEM)
SMEM = pl.BlockSpec(memory_space=pltpu.SMEM)
ANY = pl.BlockSpec(memory_space=pl.ANY)
bf16, f32 = jnp.bfloat16, jnp.float32


def from_behind(value, axis, steps):
    count = lax.axis_size(axis)
    initial, last = (max(0, -steps), min(count, count - steps))
    return lax.ppermute(value, axis, [(source, source + steps) for source in range(initial, last)])


def call(kernel, outs, specs, *operands, scratch=(), limit=8, flops=0, after=()):
    shapes = tuple(jax.ShapeDtypeStruct(shape, dtype) for shape, dtype in outs)
    moved = sum(x.size * x.dtype.itemsize for x in operands + shapes)
    operands = (*after, *operands)
    return pl.pallas_call(
        lambda *refs: kernel(*refs[len(after) :]),
        out_shape=shapes,
        in_specs=[ANY] * len(after) + specs,
        out_specs=(VMEM,) * len(outs),
        scratch_shapes=scratch,
        compiler_params=pltpu.CompilerParams(vmem_limit_bytes=limit * MIB),
        cost_estimate=pl.CostEstimate(flops=flops, bytes_accessed=moved, transcendentals=0),
    )(*operands)


def swap(value, stride, step, radix, back=False):
    count = lax.axis_size("expert")

    def partner(index):
        digit = index // stride % radix
        if radix & (radix - 1) == 0:
            other = digit ^ step
        else:
            other = (digit + (step if back else radix - step)) % radix
        return index + (other - digit) * stride

    return lax.ppermute(value, "expert", [(i, partner(i)) for i in range(count)])


def join_kernel(count, *refs):
    parts, wholes = refs[:count], refs[count:]
    rows, size = parts[0].shape[0], count // len(wholes)
    for k, part in enumerate(parts):
        wholes[k // size][k % size * rows : (k % size + 1) * rows] = part[...]


def gather_rows(rows):
    far = lax.axis_size("expert") // 4
    tokens, width = rows.shape
    parts = [rows] + [swap(rows, 4, k, far) for k in range(1, far)]
    shape = (far // 2 * tokens, width)
    batches = []
    for near in call(
        functools.partial(join_kernel, far),
        [(shape, rows.dtype)] * 2,
        [VMEM] * far,
        *parts[far // 2 :],
        *parts[: far // 2],
    ):
        beside = swap(near, 2, 1, 2)
        batches.append([near, beside, swap(near, 1, 1, 2), swap(beside, 1, 1, 2)])
    return batches


def sum_kernel(mine, arrived, total):
    total[...] = (mine[...] + arrived[...].astype(f32)).astype(total.dtype)


def split_kernel(mine, near, beside, *pieces):
    rows = pieces[0].shape[0]
    total = mine[...] + near[...].astype(f32) + beside[...].astype(f32)
    for k, piece in enumerate(pieces):
        piece[...] = total[k * rows : (k + 1) * rows].astype(piece.dtype)


def leave_pair(found):
    mine_near, mine_beside, other_near, other_beside = found
    arrived_beside = swap(other_beside, 1, 1, 2, True)
    arrived_near = swap(other_near, 1, 1, 2, True)
    (leaving,) = call(
        sum_kernel, [(mine_beside.shape, bf16)], [VMEM] * 2, mine_beside, arrived_beside
    )
    return mine_near, arrived_near, leaving


def return_rows(batches, tokens):
    far = lax.axis_size("expert") // 4
    returned, steps, earlier = {}, [range(far // 2, far), range(far // 2)], ()
    for (mine_near, arrived_near, leaving), distances in zip(batches, steps):
        shape = mine_near.shape
        beside = swap(leaving, 2, 1, 2, True)
        pieces = call(
            split_kernel,
            [((tokens, shape[1]), bf16 if k else f32) for k in distances],
            [VMEM] * 3,
            mine_near,
            arrived_near,
            beside,
            after=earlier,
        )
        earlier = (pieces[-1],)
        for k, piece in zip(distances, pieces):
            returned[k] = swap(piece, 4, k, far, True) if k else piece
    return [returned[k] for k in range(far)]


def normed_rows(widened, gain_row):
    scale_inv = lax.rsqrt(jnp.mean(widened * widened, axis=-1, keepdims=True) + eps)
    return (widened * scale_inv * gain_row).astype(bf16)


def open_kernel(experts, current_hbm, routes_hbm, gain_hbm, wide_ref, current, routes, gain, sems):
    pairs = ((current_hbm, current), (routes_hbm, routes), (gain_hbm, gain))
    copies = [pltpu.make_async_copy(a, b, sems.at[k]) for k, (a, b) in enumerate(pairs)]
    for copy in copies:
        copy.start()
    for copy in copies:
        copy.wait()
    features = current.shape[-1]
    layers, batches, top, tokens = routes.shape
    columns = wide_ref.shape[1] - features
    wide_ref[:, :features] = normed_rows(current[...].astype(f32), gain[0:1])
    places = lax.broadcasted_iota(jnp.int32, (columns, tokens), 0)
    same = lax.broadcasted_iota(jnp.int32, (tokens, tokens), 0) == lax.broadcasted_iota(
        jnp.int32, (tokens, tokens), 1
    )
    for batch in range(batches):
        chosen = jnp.zeros(places.shape, f32)
        for layer_no in range(layers):
            named = routes[layer_no, batch] + layer_no * experts
            for k in range(top):
                chosen = jnp.where(places == named[k : k + 1], 1.0, chosen)
        turned = lax.dot_general(
            same.astype(bf16),
            chosen.astype(bf16),
            (((1,), (1,)), ((), ())),
            preferred_element_type=f32,
        )
        wide_ref[batch * tokens : (batch + 1) * tokens, features:] = turned.astype(bf16)


def total_rows(current, kept, sent):
    total = kept[...]
    for piece in sent:
        total = total + piece[...].astype(f32)
    return (current.astype(f32) + total * 0.125).astype(bf16)


def close_kernel(layer_no, current_ref, gain_ref, kept, *refs):
    *sent, out_ref, normed_ref = refs
    out = total_rows(current_ref[...], kept, sent)
    out_ref[...] = out
    normed_ref[...] = normed_rows(out.astype(f32), gain_ref[layer_no : layer_no + 1])


def end_kernel(earlier, current_ref, kept, *refs):
    sent, before, outs_ref = refs[: len(refs) - earlier - 1], refs[-earlier - 1 : -1], refs[-1]
    layers, batches, tokens, _ = outs_ref.shape
    done = [ref[...] for ref in before] + [total_rows(current_ref[...], kept, sent)]
    for layer_no in range(layers):
        for batch in range(batches):
            outs_ref[layer_no, batch] = done[layer_no][batch * tokens : (batch + 1) * tokens]


def load_kernel(layer_no, cuts, gate_up_hbm, down_hbm, gate_up_ref, down_ref, sems):
    copies = []
    for source, target in ((gate_up_hbm, gate_up_ref), (down_hbm, down_ref)):
        rows = target.shape[0] // cuts
        for cut in range(cuts):
            span = pl.ds(cut * rows, rows)
            copies.append(
                pltpu.make_async_copy(
                    source.at[layer_no, 0, span], target.at[span], sems.at[len(copies)]
                )
            )
    for copy in copies:
        copy.start()
    for copy in copies:
        copy.wait()


def load_weights(layer_no, w_gate_up, w_down):
    cuts = 4
    return call(
        functools.partial(load_kernel, layer_no, cuts),
        [(w_gate_up.shape[2:], bf16), (w_down.shape[2:], bf16)],
        [ANY] * 2,
        in_hbm(w_gate_up),
        in_hbm(w_down),
        scratch=[pltpu.SemaphoreType.DMA((2 * cuts,))],
        limit=12,
    )


def tile_of(extent, most):
    size = most
    while extent % size:
        size //= 2
    return size


def expert_kernel(first_column, wide, me_ref, *refs):
    if wide:
        parts, refs = refs[:4], refs[4:]
        gate_up_ref, down_ref, *outs, routed_ref, rows_ref, hidden_ref = refs
    else:
        parts, refs = refs[:4], refs[4:]
        routed_ref, gate_up_ref, down_ref, *outs, rows_ref, hidden_ref = refs
    hidden_size, features = down_ref.shape
    quarter = parts[0].shape[0]
    for k, part in enumerate(parts):
        span = slice(k * quarter, (k + 1) * quarter)
        rows_ref[span] = part[:, :features]
        if wide:
            routed_ref[span] = part[:, features:]
    places = lax.broadcasted_iota(jnp.int32, routed_ref.shape, 1)
    chosen = jnp.where(places == me_ref[0] + first_column, routed_ref[...].astype(f32), 0.0)
    share = jnp.sum(chosen, axis=1, keepdims=True)
    rows = rows_ref[...]
    size = tile_of(hidden_size, 256)
    for low in range(0, hidden_size, size):
        span, beside = slice(low, low + size), slice(hidden_size + low, hidden_size + low + size)
        gate = jnp.dot(rows, gate_up_ref[:, span], preferred_element_type=f32)
        up = jnp.dot(rows, gate_up_ref[:, beside], preferred_element_type=f32)
        hidden_ref[:, span] = (gate / (1.0 + jnp.exp(-gate)) * up).astype(bf16)
    hidden = hidden_ref[...]
    size = tile_of(features, 512)
    for low in range(0, features, size):
        span = slice(low, low + size)
        done = jnp.dot(hidden, down_ref[:, span], preferred_element_type=f32) * share
        for k, out in enumerate(outs):
            out[:, span] = done[k * quarter : (k + 1) * quarter].astype(out.dtype)


def run_expert(parts, routed, me, first_column, weights, after):
    gate_up, down_proj = weights
    hidden_size, features = down_proj.shape
    quarter, width = parts[0].shape
    count = 4 * quarter
    wide = routed is None
    outs = [((quarter, features), f32)] * 2 + [((quarter, features), bf16)] * 2
    if wide:
        outs = outs + [((count, width - features), bf16)]
    found = call(
        functools.partial(expert_kernel, first_column, wide),
        outs,
        [SMEM] + [VMEM] * (6 if wide else 7),
        me,
        *parts,
        *([] if wide else [routed]),
        gate_up,
        down_proj,
        scratch=[pltpu.VMEM((count, features), bf16), pltpu.VMEM((count, hidden_size), bf16)],
        limit=24,
        after=after,
        flops=6 * count * features * hidden_size,
    )
    return found[:4], found[4] if wide else routed


def in_hbm(array):
    return pltpu.with_memory_space_constraint(array, pltpu.HBM)


def open_rows(current, routes, gain, experts):
    batches, tokens, features = current.shape
    rows = batches * tokens
    columns = routes.shape[0] * experts
    width = features + columns + -columns % LANES
    current, routes = current.reshape(rows, features), jnp.swapaxes(routes, 2, 3)
    (wide,) = call(
        functools.partial(open_kernel, experts),
        [((rows, width), bf16)],
        [ANY] * 3,
        in_hbm(current),
        in_hbm(routes),
        in_hbm(gain),
        scratch=[
            pltpu.VMEM(current.shape, bf16),
            pltpu.VMEM(routes.shape, jnp.int32),
            pltpu.VMEM(gain.shape, f32),
            pltpu.SemaphoreType.DMA((3,)),
        ],
    )
    return wide


def run_layer(rows, routed, me, first_column, weights):
    found, columns = [], []
    batches = gather_rows(rows)
    after = (batches[-1][0],)
    for place, parts in enumerate(batches):
        outs, kept = run_expert(
            parts, None if routed is None else routed[place], me, first_column, weights, after
        )
        found.append(leave_pair(outs))
        after = (found[-1][2],)
        columns.append(kept)
    return return_rows(found, rows.shape[0]), columns


def close_rows(layer_no, current, gain, returned):
    return call(
        functools.partial(close_kernel, layer_no),
        [(current.shape, bf16)] * 2,
        [VMEM] * (2 + len(returned)),
        current,
        gain,
        *returned,
    )


def on_device(inputs, routes, norm_gain, w_gate_up, w_down):
    experts = lax.axis_size("expert")
    sections = lax.axis_size("section")
    me = lax.axis_index("expert").astype(jnp.int32).reshape(1)
    batches, tokens, features = inputs.shape
    layers = routes.shape[0]
    weights = [load_weights(layer_no, w_gate_up, w_down) for layer_no in range(layers)]
    if sections == 1:
        outs, routed = [], None
        current = inputs.reshape(batches * tokens, features)
        rows = open_rows(inputs, routes, norm_gain, experts)
        for layer_no in range(layers):
            returned, routed = run_layer(rows, routed, me, layer_no * experts, weights[layer_no])
            if layer_no == layers - 1:
                (whole,) = call(
                    functools.partial(end_kernel, len(outs)),
                    [((layers, batches, tokens, features), bf16)],
                    [VMEM] * (1 + len(returned) + len(outs)),
                    current,
                    *returned,
                    *outs,
                )
                return whole
            current, rows = close_rows(layer_no + 1, current, norm_gain, returned)
            outs.append(current)
    segment_no = lax.axis_index("section")
    handed = jnp.zeros((tokens, features), bf16)
    finished = []
    for turn_no in range(batches + 1):
        if turn_no < batches:
            fresh_rows = inputs[turn_no]
        else:
            fresh_rows = jnp.zeros((tokens, features), bf16)
        current = jnp.where(segment_no == 0, fresh_rows, handed)
        batch_pick = jnp.clip(turn_no - segment_no, 0, batches - 1)
        turn_routes = lax.dynamic_slice_in_dim(routes, batch_pick, 1, 1)
        rows = open_rows(current[None], turn_routes, norm_gain, experts)
        returned, _ = run_layer(rows, None, me, 0, weights[0])
        result, _ = close_rows(0, current, norm_gain, returned)
        finished.append(result)
        if turn_no < batches:
            handed = from_behind(result, "section", 1)
    first_segment = jnp.stack(finished[:batches])
    second_segment = jnp.stack(finished[1:])
    return jnp.where(segment_no == 0, first_segment, second_segment)[None]


def solution(mesh):
    placed = (
        P(None, ("groups", "expert"), None),
        P("section", None, ("groups", "expert"), None),
        P("section", None),
        P("section", "expert", None, None),
        P("section", "expert", None, None),
    )
    return jax.shard_map(
        on_device,
        mesh=mesh,
        in_specs=placed,
        out_specs=P("section", None, ("groups", "expert"), None),
        check_vma=False,
    )
```

```python
import functools

import jax
import jax.numpy as jnp
from jax import lax
from jax.experimental import pallas as pl
from jax.experimental.pallas import tpu as pltpu
from jax.sharding import PartitionSpec as P

eps = 1e-06
LANES = 128
MIB = 2**20
VMEM = pl.BlockSpec(memory_space=pltpu.VMEM)
SMEM = pl.BlockSpec(memory_space=pltpu.SMEM)
ANY = pl.BlockSpec(memory_space=pl.ANY)
bf16, f32 = jnp.bfloat16, jnp.float32


def from_behind(value, axis, steps):
    count = lax.axis_size(axis)
    initial, last = (max(0, -steps), min(count, count - steps))
    return lax.ppermute(value, axis, [(source, source + steps) for source in range(initial, last)])


def call(kernel, outs, specs, *operands, scratch=(), limit=8, after=()):
    shapes = tuple(jax.ShapeDtypeStruct(shape, dtype) for shape, dtype in outs)
    operands = (*after, *operands)
    return pl.pallas_call(
        lambda *refs: kernel(*refs[len(after) :]),
        out_shape=shapes,
        in_specs=[ANY] * len(after) + specs,
        out_specs=(VMEM,) * len(outs),
        scratch_shapes=scratch,
        compiler_params=pltpu.CompilerParams(vmem_limit_bytes=limit * MIB),
        cost_estimate=pl.CostEstimate(flops=0, bytes_accessed=0, transcendentals=0),
    )(*operands)


def swap(value, stride, step, radix, back=False):
    count = lax.axis_size("expert")

    def partner(index):
        digit = index // stride % radix
        if radix & (radix - 1) == 0:
            other = digit ^ step
        else:
            other = (digit + (step if back else radix - step)) % radix
        return index + (other - digit) * stride

    return lax.ppermute(value, "expert", [(i, partner(i)) for i in range(count)])


def join_kernel(count, *refs):
    parts, wholes = refs[:count], refs[count:]
    rows, size = parts[0].shape[0], count // len(wholes)
    for k, part in enumerate(parts):
        wholes[k // size][k % size * rows : (k % size + 1) * rows] = part[...]


def gather_rows(rows, after):
    far = lax.axis_size("expert") // 4
    tokens, width = rows.shape
    parts = [rows] + [swap(rows, 4, k, far) for k in range(1, far)]
    shape = (far // 2 * tokens, width)
    batches = []
    for near in call(
        functools.partial(join_kernel, far),
        [(shape, rows.dtype)] * 2,
        [VMEM] * far,
        *parts[far // 2 :],
        *parts[: far // 2],
        after=after,
    ):
        beside = swap(near, 2, 1, 2)
        batches.append([near, beside, swap(near, 1, 1, 2), swap(beside, 1, 1, 2)])
    return batches


def sum_kernel(mine, arrived, total):
    total[...] = (mine[...] + arrived[...].astype(f32)).astype(total.dtype)


def split_kernel(mine, near, beside, *pieces):
    rows = pieces[0].shape[0]
    total = mine[...] + near[...].astype(f32) + beside[...].astype(f32)
    for k, piece in enumerate(pieces):
        piece[...] = total[k * rows : (k + 1) * rows].astype(piece.dtype)


def return_rows(batches, tokens):
    far = lax.axis_size("expert") // 4
    returned, steps, earlier = {}, [range(far // 2, far), range(far // 2)], ()
    for (mine_near, mine_beside, other_near, other_beside), distances in zip(batches, steps):
        shape = mine_near.shape
        arrived_beside = swap(other_beside, 1, 1, 2, True)
        arrived_near = swap(other_near, 1, 1, 2, True)
        (leaving,) = call(
            sum_kernel,
            [(shape, bf16)],
            [VMEM] * 2,
            mine_beside,
            arrived_beside,
            after=earlier,
        )
        beside = swap(leaving, 2, 1, 2, True)
        pieces = call(
            split_kernel,
            [((tokens, shape[1]), bf16 if k else f32) for k in distances],
            [VMEM] * 3,
            mine_near,
            arrived_near,
            beside,
        )
        earlier = (pieces[-1],)
        for k, piece in zip(distances, pieces):
            returned[k] = swap(piece, 4, k, far, True) if k else piece
    return [returned[k] for k in range(far)]


def normed_rows(widened, gain_row):
    scale_inv = lax.rsqrt(jnp.mean(widened * widened, axis=-1, keepdims=True) + eps)
    return (widened * scale_inv * gain_row).astype(bf16)


def open_kernel(experts, current_hbm, routes_hbm, gain_hbm, wide_ref, current, routes, gain, sems):
    pairs = ((current_hbm, current), (routes_hbm, routes), (gain_hbm, gain))
    copies = [pltpu.make_async_copy(a, b, sems.at[k]) for k, (a, b) in enumerate(pairs)]
    for copy in copies:
        copy.start()
    for copy in copies:
        copy.wait()
    features = current.shape[-1]
    layers, batches, top, tokens = routes.shape
    columns = wide_ref.shape[1] - features
    wide_ref[:, :features] = normed_rows(current[...].astype(f32), gain[0:1])
    places = lax.broadcasted_iota(jnp.int32, (columns, tokens), 0)
    same = lax.broadcasted_iota(jnp.int32, (tokens, tokens), 0) == lax.broadcasted_iota(
        jnp.int32, (tokens, tokens), 1
    )
    for batch in range(batches):
        chosen = jnp.zeros(places.shape, f32)
        for layer_no in range(layers):
            named = routes[layer_no, batch] + layer_no * experts
            for k in range(top):
                chosen = jnp.where(places == named[k : k + 1], 1.0, chosen)
        turned = lax.dot_general(
            same.astype(bf16),
            chosen.astype(bf16),
            (((1,), (1,)), ((), ())),
            preferred_element_type=f32,
        )
        wide_ref[batch * tokens : (batch + 1) * tokens, features:] = turned.astype(bf16)


def total_rows(current, kept, sent):
    total = kept[...]
    for piece in sent:
        total = total + piece[...].astype(f32)
    return (current.astype(f32) + total * 0.125).astype(bf16)


def close_kernel(layer_no, current_ref, gain_ref, kept, *refs):
    *sent, out_ref, normed_ref = refs
    out = total_rows(current_ref[...], kept, sent)
    out_ref[...] = out
    normed_ref[...] = normed_rows(out.astype(f32), gain_ref[layer_no : layer_no + 1])


def end_kernel(earlier, current_ref, kept, *refs):
    sent, before, outs_ref = refs[: len(refs) - earlier - 1], refs[-earlier - 1 : -1], refs[-1]
    layers, batches, tokens, _ = outs_ref.shape
    done = [ref[...] for ref in before] + [total_rows(current_ref[...], kept, sent)]
    for layer_no in range(layers):
        for batch in range(batches):
            outs_ref[layer_no, batch] = done[layer_no][batch * tokens : (batch + 1) * tokens]


def load_kernel(layer_no, cuts, gate_up_hbm, down_hbm, gate_up_ref, down_ref, token, sems):
    token[...] = jnp.zeros_like(token)
    copies = []
    for source, target in ((gate_up_hbm, gate_up_ref), (down_hbm, down_ref)):
        rows = target.shape[0] // cuts
        for cut in range(cuts):
            span = pl.ds(cut * rows, rows)
            copies.append(
                pltpu.make_async_copy(
                    source.at[layer_no, 0, span], target.at[span], sems.at[len(copies)]
                )
            )
    for copy in copies:
        copy.start()
    for copy in copies:
        copy.wait()


def load_weights(layer_no, w_gate_up, w_down, after=()):
    cuts = 4
    return call(
        functools.partial(load_kernel, layer_no, cuts),
        [(w_gate_up.shape[2:], bf16), (w_down.shape[2:], bf16), ((8, LANES), f32)],
        [ANY] * 2,
        in_hbm(w_gate_up),
        in_hbm(w_down),
        scratch=[pltpu.SemaphoreType.DMA((2 * cuts,))],
        limit=12,
        after=after,
    )


def tile_of(extent, most):
    size = most
    while extent % size:
        size //= 2
    return size


def expert_kernel(first_column, wide, me_ref, *refs):
    if wide:
        parts, refs = refs[:4], refs[4:]
        gate_up_ref, down_ref, *outs, routed_ref, rows_ref, hidden_ref = refs
    else:
        parts, refs = refs[:4], refs[4:]
        routed_ref, gate_up_ref, down_ref, *outs, rows_ref, hidden_ref = refs
    hidden_size, features = down_ref.shape
    quarter = parts[0].shape[0]
    for k, part in enumerate(parts):
        span = slice(k * quarter, (k + 1) * quarter)
        rows_ref[span] = part[:, :features]
        if wide:
            routed_ref[span] = part[:, features:]
    places = lax.broadcasted_iota(jnp.int32, routed_ref.shape, 1)
    chosen = jnp.where(places == me_ref[0] + first_column, routed_ref[...].astype(f32), 0.0)
    share = jnp.sum(chosen, axis=1, keepdims=True)
    rows = rows_ref[...]
    size = tile_of(hidden_size, 256)
    for low in range(0, hidden_size, size):
        span, beside = slice(low, low + size), slice(hidden_size + low, hidden_size + low + size)
        gate = jnp.dot(rows, gate_up_ref[:, span], preferred_element_type=f32)
        up = jnp.dot(rows, gate_up_ref[:, beside], preferred_element_type=f32)
        hidden_ref[:, span] = (gate / (1.0 + jnp.exp(-gate)) * up).astype(bf16)
    hidden = hidden_ref[...]
    size = tile_of(features, 512)
    for low in range(0, features, size):
        span = slice(low, low + size)
        done = jnp.dot(hidden, down_ref[:, span], preferred_element_type=f32) * share
        for k, out in enumerate(outs):
            out[:, span] = done[k * quarter : (k + 1) * quarter].astype(out.dtype)


def run_expert(parts, routed, me, first_column, weights, after):
    gate_up, down_proj, _ = weights
    hidden_size, features = down_proj.shape
    quarter, width = parts[0].shape
    count = 4 * quarter
    wide = routed is None
    outs = [((quarter, features), f32)] * 2 + [((quarter, features), bf16)] * 2
    if wide:
        outs = outs + [((count, width - features), bf16)]
    found = call(
        functools.partial(expert_kernel, first_column, wide),
        outs,
        [SMEM] + [VMEM] * (6 if wide else 7),
        me,
        *parts,
        *([] if wide else [routed]),
        gate_up,
        down_proj,
        scratch=[pltpu.VMEM((count, features), bf16), pltpu.VMEM((count, hidden_size), bf16)],
        limit=24,
        after=after,
    )
    return found[:4], found[4] if wide else routed


def in_hbm(array):
    return pltpu.with_memory_space_constraint(array, pltpu.HBM)


def open_rows(current, routes, gain, experts):
    batches, tokens, features = current.shape
    rows = batches * tokens
    columns = routes.shape[0] * experts
    width = features + columns + -columns % LANES
    current, routes = current.reshape(rows, features), jnp.swapaxes(routes, 2, 3)
    (wide,) = call(
        functools.partial(open_kernel, experts),
        [((rows, width), bf16)],
        [ANY] * 3,
        in_hbm(current),
        in_hbm(routes),
        in_hbm(gain),
        scratch=[
            pltpu.VMEM(current.shape, bf16),
            pltpu.VMEM(routes.shape, jnp.int32),
            pltpu.VMEM(gain.shape, f32),
            pltpu.SemaphoreType.DMA((3,)),
        ],
    )
    return wide


def run_layer(rows, routed, me, first_column, weights, loaded=()):
    found, columns = [], []
    batches = gather_rows(rows, loaded)
    after = ()
    for place, parts in enumerate(batches):
        outs, kept = run_expert(
            parts, None if routed is None else routed[place], me, first_column, weights, after
        )
        after = (outs[0],)
        found.append(outs)
        columns.append(kept)
    return return_rows(found, rows.shape[0]), columns, after


def close_rows(layer_no, current, gain, returned, after=()):
    return call(
        functools.partial(close_kernel, layer_no),
        [(current.shape, bf16)] * 2,
        [VMEM] * (2 + len(returned)),
        current,
        gain,
        *returned,
        after=after,
    )


def on_device(inputs, routes, norm_gain, w_gate_up, w_down):
    experts = lax.axis_size("expert")
    sections = lax.axis_size("section")
    me = lax.axis_index("expert").astype(jnp.int32).reshape(1)
    batches, tokens, features = inputs.shape
    layers = routes.shape[0]
    weights = load_weights(0, w_gate_up, w_down)
    if sections == 1:
        outs, routed = [], None
        current = inputs.reshape(batches * tokens, features)
        rows = open_rows(inputs, routes, norm_gain, experts)
        for layer_no in range(layers):
            returned, routed, worked = run_layer(
                rows, routed, me, layer_no * experts, weights, weights[2:]
            )
            if layer_no == layers - 1:
                (whole,) = call(
                    functools.partial(end_kernel, len(outs)),
                    [((layers, batches, tokens, features), bf16)],
                    [VMEM] * (1 + len(returned) + len(outs)),
                    current,
                    *returned,
                    *outs,
                )
                return whole
            weights = load_weights(layer_no + 1, w_gate_up, w_down, worked)
            current, rows = close_rows(layer_no + 1, current, norm_gain, returned, weights[2:])
            outs.append(current)
    segment_no = lax.axis_index("section")
    handed = jnp.zeros((tokens, features), bf16)
    finished = []
    for turn_no in range(batches + 1):
        if turn_no < batches:
            fresh_rows = inputs[turn_no]
        else:
            fresh_rows = jnp.zeros((tokens, features), bf16)
        current = jnp.where(segment_no == 0, fresh_rows, handed)
        batch_pick = jnp.clip(turn_no - segment_no, 0, batches - 1)
        turn_routes = lax.dynamic_slice_in_dim(routes, batch_pick, 1, 1)
        rows = open_rows(current[None], turn_routes, norm_gain, experts)
        returned, _, _ = run_layer(rows, None, me, 0, weights)
        result, _ = close_rows(0, current, norm_gain, returned)
        finished.append(result)
        if turn_no < batches:
            handed = from_behind(result, "section", 1)
    first_segment = jnp.stack(finished[:batches])
    second_segment = jnp.stack(finished[1:])
    return jnp.where(segment_no == 0, first_segment, second_segment)[None]


def solution(mesh):
    placed = (
        P(None, ("groups", "expert"), None),
        P("section", None, ("groups", "expert"), None),
        P("section", None),
        P("section", "expert", None, None),
        P("section", "expert", None, None),
    )
    return jax.shard_map(
        on_device,
        mesh=mesh,
        in_specs=placed,
        out_specs=P("section", None, ("groups", "expert"), None),
        check_vma=False,
    )
```

```python
import functools

import jax
import jax.numpy as jnp
from jax import lax
from jax.experimental import pallas as pl
from jax.experimental.pallas import tpu as pltpu
from jax.sharding import PartitionSpec as P

eps = 1e-06
LANES = 128
MIB = 2**20
VMEM = pl.BlockSpec(memory_space=pltpu.VMEM)
ANY = pl.BlockSpec(memory_space=pl.ANY)
bf16, f32 = jnp.bfloat16, jnp.float32


def from_behind(value, axis, steps):
    count = lax.axis_size(axis)
    initial, last = (max(0, -steps), min(count, count - steps))
    return lax.ppermute(value, axis, [(source, source + steps) for source in range(initial, last)])


def call(kernel, outs, specs, *operands, scratch=(), limit=8, after=()):
    shapes = tuple(jax.ShapeDtypeStruct(shape, dtype) for shape, dtype in outs)
    operands = (*after, *operands)
    return pl.pallas_call(
        lambda *refs: kernel(*refs[len(after) :]),
        out_shape=shapes,
        in_specs=[ANY] * len(after) + specs,
        out_specs=(VMEM,) * len(outs),
        scratch_shapes=scratch,
        compiler_params=pltpu.CompilerParams(vmem_limit_bytes=limit * MIB),
        cost_estimate=pl.CostEstimate(flops=0, bytes_accessed=0, transcendentals=0),
    )(*operands)


def swap(value, stride, step, radix, back=False):
    count = lax.axis_size("expert")

    def partner(index):
        digit = index // stride % radix
        if radix & (radix - 1) == 0:
            other = digit ^ step
        else:
            other = (digit + (step if back else radix - step)) % radix
        return index + (other - digit) * stride

    return lax.ppermute(value, "expert", [(i, partner(i)) for i in range(count)])


def join_kernel(count, *refs):
    parts, wholes = refs[:count], refs[count:]
    rows, size = parts[0].shape[0], count // len(wholes)
    for k, part in enumerate(parts):
        wholes[k // size][k % size * rows : (k % size + 1) * rows] = part[...]


def held(value, until):
    return lax.optimization_barrier((value, until))[0] if until is not None else value


def gather_rows(rows, after):
    far = lax.axis_size("expert") // 4
    tokens, width = rows.shape
    parts = [rows] + [swap(rows, 4, k, far) for k in range(1, far)]
    shape = (far // 2 * tokens, width)
    batches, beside = [], None
    for near in call(
        functools.partial(join_kernel, far),
        [(shape, rows.dtype)] * 2,
        [VMEM] * far,
        *parts[far // 2 :],
        *parts[: far // 2],
        after=after,
    ):
        near = held(near, beside)
        beside = swap(near, 2, 1, 2)
        batches.append([near, beside])
    return batches


def sum_kernel(mine, arrived, total):
    total[...] = (mine[...] + arrived[...].astype(f32)).astype(total.dtype)


def split_kernel(mine, near, beside, *pieces):
    rows = pieces[0].shape[0]
    total = mine[...] + near[...].astype(f32) + beside[...].astype(f32)
    for k, piece in enumerate(pieces):
        piece[...] = total[k * rows : (k + 1) * rows].astype(piece.dtype)


def leave_pair(found, after):
    mine_near, mine_beside, other_near, other_beside = found
    arrived_beside = swap(other_beside, 1, 1, 2, True)
    arrived_near = swap(other_near, 1, 1, 2, True)
    (leaving,) = call(
        sum_kernel,
        [(mine_beside.shape, bf16)],
        [VMEM] * 2,
        mine_beside,
        arrived_beside,
        after=after,
    )
    return mine_near, arrived_near, leaving


def split_rows(left, distances, tokens):
    far = lax.axis_size("expert") // 4
    mine_near, arrived_near, leaving = left
    beside = swap(leaving, 2, 1, 2, True)
    pieces = call(
        split_kernel,
        [((tokens, leaving.shape[1]), bf16 if k else f32) for k in distances],
        [VMEM] * 3,
        mine_near,
        arrived_near,
        beside,
    )
    arrived = [swap(piece, 4, k, far, True) if k else piece for k, piece in zip(distances, pieces)]
    return arrived, pieces[-1]


def normed_rows(widened, gain_row):
    scale_inv = lax.rsqrt(jnp.mean(widened * widened, axis=-1, keepdims=True) + eps)
    return (widened * scale_inv * gain_row).astype(bf16)


def open_kernel(experts, current_hbm, routes_hbm, gain_hbm, wide_ref, current, routes, gain, sems):
    pairs = ((current_hbm, current), (routes_hbm, routes), (gain_hbm, gain))
    copies = [pltpu.make_async_copy(a, b, sems.at[k]) for k, (a, b) in enumerate(pairs)]
    for copy in copies:
        copy.start()
    for copy in copies:
        copy.wait()
    features = current.shape[-1]
    layers, batches, top, tokens = routes.shape
    columns = wide_ref.shape[1] - features
    wide_ref[:, :features] = normed_rows(current[...].astype(f32), gain[0:1])
    places = lax.broadcasted_iota(jnp.int32, (columns, tokens), 0)
    same = lax.broadcasted_iota(jnp.int32, (tokens, tokens), 0) == lax.broadcasted_iota(
        jnp.int32, (tokens, tokens), 1
    )
    for batch in range(batches):
        chosen = jnp.zeros(places.shape, f32)
        for layer_no in range(layers):
            named = routes[layer_no, batch] + layer_no * experts
            for k in range(top):
                chosen = jnp.where(places == named[k : k + 1], 1.0, chosen)
        turned = lax.dot_general(
            same.astype(bf16),
            chosen.astype(bf16),
            (((1,), (1,)), ((), ())),
            preferred_element_type=f32,
        )
        wide_ref[batch * tokens : (batch + 1) * tokens, features:] = turned.astype(bf16)


def total_rows(current, kept, sent):
    total = kept[...]
    for piece in sent:
        total = total + piece[...].astype(f32)
    return (current.astype(f32) + total * 0.125).astype(bf16)


def close_kernel(layer_no, current_ref, gain_ref, kept, *refs):
    *sent, out_ref, normed_ref = refs
    out = total_rows(current_ref[...], kept, sent)
    out_ref[...] = out
    normed_ref[...] = normed_rows(out.astype(f32), gain_ref[layer_no : layer_no + 1])


def end_kernel(earlier, current_ref, kept, *refs):
    sent, before, outs_ref = refs[: len(refs) - earlier - 1], refs[-earlier - 1 : -1], refs[-1]
    layers, batches, tokens, _ = outs_ref.shape
    done = [ref[...] for ref in before] + [total_rows(current_ref[...], kept, sent)]
    for layer_no in range(layers):
        for batch in range(batches):
            outs_ref[layer_no, batch] = done[layer_no][batch * tokens : (batch + 1) * tokens]


def load_kernel(layer_no, cuts, gate_up_hbm, down_hbm, gate_up_ref, down_ref, token, sems):
    token[...] = jnp.zeros_like(token)
    copies = []
    for source, target in ((gate_up_hbm, gate_up_ref), (down_hbm, down_ref)):
        rows = target.shape[0] // cuts
        for cut in range(cuts):
            span = pl.ds(cut * rows, rows)
            copies.append(
                pltpu.make_async_copy(
                    source.at[layer_no, 0, span], target.at[span], sems.at[len(copies)]
                )
            )
    for copy in copies:
        copy.start()
    for copy in copies:
        copy.wait()


def load_weights(layer_no, w_gate_up, w_down, after=()):
    cuts = 4
    return call(
        functools.partial(load_kernel, layer_no, cuts),
        [(w_gate_up.shape[2:], bf16), (w_down.shape[2:], bf16), ((8, LANES), f32)],
        [ANY] * 2,
        in_hbm(w_gate_up),
        in_hbm(w_down),
        scratch=[pltpu.SemaphoreType.DMA((2 * cuts,))],
        limit=12,
        after=after,
    )


def tile_of(extent, most):
    size = most
    while extent % size:
        size //= 2
    return size


def expert_kernel(first_column, wide, *refs):
    if wide:
        parts, refs = refs[:4], refs[4:]
        gate_up_ref, down_ref, *outs, routed_ref, rows_ref, hidden_ref = refs
    else:
        parts, refs = refs[:4], refs[4:]
        routed_ref, gate_up_ref, down_ref, *outs, rows_ref, hidden_ref = refs
    hidden_size, features = down_ref.shape
    quarter = parts[0].shape[0]
    for k, part in enumerate(parts):
        span = slice(k * quarter, (k + 1) * quarter)
        rows_ref[span] = part[:, :features]
        if wide:
            routed_ref[span] = part[:, features:]
    places = lax.broadcasted_iota(jnp.int32, routed_ref.shape, 1)
    column = first_column + lax.axis_index("expert")
    chosen = jnp.where(places == column, routed_ref[...].astype(f32), 0.0)
    share = jnp.sum(chosen, axis=1, keepdims=True)
    rows = rows_ref[...]
    size = tile_of(hidden_size, 256)
    for low in range(0, hidden_size, size):
        span, beside = slice(low, low + size), slice(hidden_size + low, hidden_size + low + size)
        gate = jnp.dot(rows, gate_up_ref[:, span], preferred_element_type=f32)
        up = jnp.dot(rows, gate_up_ref[:, beside], preferred_element_type=f32)
        hidden_ref[:, span] = (gate / (1.0 + jnp.exp(-gate)) * up).astype(bf16)
    hidden = hidden_ref[...]
    size = tile_of(features, 512)
    for low in range(0, features, size):
        span = slice(low, low + size)
        done = jnp.dot(hidden, down_ref[:, span], preferred_element_type=f32) * share
        for k, out in enumerate(outs):
            out[:, span] = done[k * quarter : (k + 1) * quarter].astype(out.dtype)


def run_expert(parts, routed, first_column, weights, after):
    gate_up, down_proj, _ = weights
    hidden_size, features = down_proj.shape
    quarter, width = parts[0].shape
    count = 4 * quarter
    wide = routed is None
    outs = [((quarter, features), f32)] * 2 + [((quarter, features), bf16)] * 2
    if wide:
        outs = outs + [((count, width - features), bf16)]
    found = call(
        functools.partial(expert_kernel, first_column, wide),
        outs,
        [VMEM] * (6 if wide else 7),
        *parts,
        *([] if wide else [routed]),
        gate_up,
        down_proj,
        scratch=[pltpu.VMEM((count, features), bf16), pltpu.VMEM((count, hidden_size), bf16)],
        limit=24,
        after=after,
    )
    return found[:4], found[4] if wide else routed


def in_hbm(array):
    return pltpu.with_memory_space_constraint(array, pltpu.HBM)


def open_rows(current, routes, gain, experts):
    batches, tokens, features = current.shape
    rows = batches * tokens
    columns = routes.shape[0] * experts
    width = features + columns + -columns % LANES
    current, routes = current.reshape(rows, features), jnp.swapaxes(routes, 2, 3)
    (wide,) = call(
        functools.partial(open_kernel, experts),
        [((rows, width), bf16)],
        [ANY] * 3,
        in_hbm(current),
        in_hbm(routes),
        in_hbm(gain),
        scratch=[
            pltpu.VMEM(current.shape, bf16),
            pltpu.VMEM(routes.shape, jnp.int32),
            pltpu.VMEM(gain.shape, f32),
            pltpu.SemaphoreType.DMA((3,)),
        ],
    )
    return wide


def run_layer(rows, routed, first_column, weights, loaded=()):
    far, tokens = lax.axis_size("expert") // 4, rows.shape[0]
    columns, returned, after, worked = [], [], (), ()
    distances = [range(far // 2, far), range(far // 2)]
    for place, (near, beside) in enumerate(gather_rows(rows, loaded)):
        beside = held(beside, left[2] if place else None)
        parts = [near, beside, swap(near, 1, 1, 2), swap(beside, 1, 1, 2)]
        outs, kept = run_expert(
            parts, None if routed is None else routed[place], first_column, weights, worked
        )
        columns.append(kept)
        left = leave_pair(outs, after)
        arrived, last = split_rows(left, distances[place], tokens)
        returned = arrived + returned
        after, worked = (last,), (left[2],)
    return returned, columns, (outs[0],)


def close_rows(layer_no, current, gain, returned, after=()):
    return call(
        functools.partial(close_kernel, layer_no),
        [(current.shape, bf16)] * 2,
        [VMEM] * (2 + len(returned)),
        current,
        gain,
        *returned,
        after=after,
    )


def on_device(inputs, routes, norm_gain, w_gate_up, w_down):
    experts = lax.axis_size("expert")
    sections = lax.axis_size("section")
    batches, tokens, features = inputs.shape
    layers = routes.shape[0]
    weights = load_weights(0, w_gate_up, w_down)
    if sections == 1:
        outs, routed = [], None
        current = inputs.reshape(batches * tokens, features)
        rows = open_rows(inputs, routes, norm_gain, experts)
        for layer_no in range(layers):
            returned, routed, worked = run_layer(
                rows, routed, layer_no * experts, weights, weights[2:]
            )
            if layer_no == layers - 1:
                (whole,) = call(
                    functools.partial(end_kernel, len(outs)),
                    [((layers, batches, tokens, features), bf16)],
                    [VMEM] * (1 + len(returned) + len(outs)),
                    current,
                    *returned,
                    *outs,
                )
                return whole
            weights = load_weights(layer_no + 1, w_gate_up, w_down, worked)
            current, rows = close_rows(layer_no + 1, current, norm_gain, returned, weights[2:])
            outs.append(current)
    segment_no = lax.axis_index("section")
    handed = jnp.zeros((tokens, features), bf16)
    finished = []
    for turn_no in range(batches + 1):
        if turn_no < batches:
            fresh_rows = inputs[turn_no]
        else:
            fresh_rows = jnp.zeros((tokens, features), bf16)
        current = jnp.where(segment_no == 0, fresh_rows, handed)
        batch_pick = jnp.clip(turn_no - segment_no, 0, batches - 1)
        turn_routes = lax.dynamic_slice_in_dim(routes, batch_pick, 1, 1)
        rows = open_rows(current[None], turn_routes, norm_gain, experts)
        returned, _, _ = run_layer(rows, None, 0, weights)
        result, _ = close_rows(0, current, norm_gain, returned)
        finished.append(result)
        if turn_no < batches:
            handed = from_behind(result, "section", 1)
    first_segment = jnp.stack(finished[:batches])
    second_segment = jnp.stack(finished[1:])
    return jnp.where(segment_no == 0, first_segment, second_segment)[None]


def solution(mesh):
    placed = (
        P(None, ("groups", "expert"), None),
        P("section", None, ("groups", "expert"), None),
        P("section", None),
        P("section", "expert", None, None),
        P("section", "expert", None, None),
    )
    return jax.shard_map(
        on_device,
        mesh=mesh,
        in_specs=placed,
        out_specs=P("section", None, ("groups", "expert"), None),
        check_vma=False,
    )
```

```python
import functools

import jax
import jax.numpy as jnp
from jax import lax
from jax.experimental import pallas as pl
from jax.experimental.pallas import tpu as pltpu
from jax.sharding import PartitionSpec as P

eps = 1e-06
LANES = 128
MIB = 2**20
WAIT = 6 * 10**9
VMEM = pl.BlockSpec(memory_space=pltpu.VMEM)
ANY = pl.BlockSpec(memory_space=pl.ANY)
bf16, f32 = jnp.bfloat16, jnp.float32


def from_behind(value, axis, steps):
    count = lax.axis_size(axis)
    initial, last = (max(0, -steps), min(count, count - steps))
    return lax.ppermute(value, axis, [(source, source + steps) for source in range(initial, last)])


def call(kernel, outs, specs, *operands, scratch=(), limit=8, after=(), weight=0):
    shapes = tuple(jax.ShapeDtypeStruct(shape, dtype) for shape, dtype in outs)
    operands = (*after, *operands)
    return pl.pallas_call(
        lambda *refs: kernel(*refs[len(after) :]),
        out_shape=shapes,
        in_specs=[ANY] * len(after) + specs,
        out_specs=(VMEM,) * len(outs),
        scratch_shapes=scratch,
        compiler_params=pltpu.CompilerParams(vmem_limit_bytes=limit * MIB),
        cost_estimate=pl.CostEstimate(flops=weight, bytes_accessed=0, transcendentals=0),
    )(*operands)


def swap(value, stride, step, radix, back=False):
    count = lax.axis_size("expert")

    def partner(index):
        digit = index // stride % radix
        if radix & (radix - 1) == 0:
            other = digit ^ step
        else:
            other = (digit + (step if back else radix - step)) % radix
        return index + (other - digit) * stride

    return lax.ppermute(value, "expert", [(i, partner(i)) for i in range(count)])


def join_kernel(*refs):
    *parts, whole = refs
    rows = parts[0].shape[0]
    for k, part in enumerate(parts):
        whole[k * rows : (k + 1) * rows] = part[...]


def join_rows(parts, after, weight):
    tokens, width = parts[0].shape
    return call(
        join_kernel,
        [((len(parts) * tokens, width), parts[0].dtype)],
        [VMEM] * len(parts),
        *parts,
        after=after,
        weight=weight,
    )[0]


def held(value, until):
    return lax.optimization_barrier((value, until))[0]


def sum_kernel(mine, arrived, total):
    total[...] = (mine[...] + arrived[...].astype(f32)).astype(total.dtype)


def split_kernel(mine, near, beside, *pieces):
    rows = pieces[0].shape[0]
    total = mine[...] + near[...].astype(f32) + beside[...].astype(f32)
    for k, piece in enumerate(pieces):
        piece[...] = total[k * rows : (k + 1) * rows].astype(piece.dtype)


def leave_pair(found, after):
    mine_near, mine_beside, other_near, other_beside = found
    arrived_beside = swap(other_beside, 1, 1, 2, True)
    arrived_near = swap(other_near, 1, 1, 2, True)
    (leaving,) = call(
        sum_kernel,
        [(mine_beside.shape, bf16)],
        [VMEM] * 2,
        mine_beside,
        arrived_beside,
        after=after,
    )
    return mine_near, arrived_near, leaving


def split_rows(mine_near, arrived_near, beside, distances, tokens):
    far = lax.axis_size("expert") // 4
    pieces = call(
        split_kernel,
        [((tokens, beside.shape[1]), bf16 if k else f32) for k in distances],
        [VMEM] * 3,
        mine_near,
        arrived_near,
        beside,
    )
    arrived = [swap(piece, 4, k, far, True) if k else piece for k, piece in zip(distances, pieces)]
    return arrived, pieces[-1]


def normed_rows(widened, gain_row):
    scale_inv = lax.rsqrt(jnp.mean(widened * widened, axis=-1, keepdims=True) + eps)
    return (widened * scale_inv * gain_row).astype(bf16)


def open_kernel(experts, current_hbm, routes_hbm, gain_hbm, wide_ref, current, routes, gain, sems):
    pairs = ((current_hbm, current), (routes_hbm, routes), (gain_hbm, gain))
    copies = [pltpu.make_async_copy(a, b, sems.at[k]) for k, (a, b) in enumerate(pairs)]
    for copy in copies:
        copy.start()
    for copy in copies:
        copy.wait()
    features = current.shape[-1]
    layers, batches, top, tokens = routes.shape
    columns = wide_ref.shape[1] - features
    wide_ref[:, :features] = normed_rows(current[...].astype(f32), gain[0:1])
    places = lax.broadcasted_iota(jnp.int32, (columns, tokens), 0)
    same = lax.broadcasted_iota(jnp.int32, (tokens, tokens), 0) == lax.broadcasted_iota(
        jnp.int32, (tokens, tokens), 1
    )
    for batch in range(batches):
        chosen = jnp.zeros(places.shape, f32)
        for layer_no in range(layers):
            named = routes[layer_no, batch] + layer_no * experts
            for k in range(top):
                chosen = jnp.where(places == named[k : k + 1], 1.0, chosen)
        turned = lax.dot_general(
            same.astype(bf16),
            chosen.astype(bf16),
            (((1,), (1,)), ((), ())),
            preferred_element_type=f32,
        )
        wide_ref[batch * tokens : (batch + 1) * tokens, features:] = turned.astype(bf16)


def total_rows(current, kept, sent):
    total = kept[...]
    for piece in sent:
        total = total + piece[...].astype(f32)
    return (current.astype(f32) + total * 0.125).astype(bf16)


def close_kernel(layer_no, current_ref, gain_ref, kept, *refs):
    *sent, out_ref, normed_ref = refs
    out = total_rows(current_ref[...], kept, sent)
    out_ref[...] = out
    normed_ref[...] = normed_rows(out.astype(f32), gain_ref[layer_no : layer_no + 1])


def end_kernel(earlier, current_ref, kept, *refs):
    sent, before, outs_ref = refs[: len(refs) - earlier - 1], refs[-earlier - 1 : -1], refs[-1]
    layers, batches, tokens, _ = outs_ref.shape
    done = [ref[...] for ref in before] + [total_rows(current_ref[...], kept, sent)]
    for layer_no in range(layers):
        for batch in range(batches):
            outs_ref[layer_no, batch] = done[layer_no][batch * tokens : (batch + 1) * tokens]


def load_kernel(layer_no, cuts, gate_up_hbm, down_hbm, gate_up_ref, down_ref, token, sems):
    token[...] = jnp.zeros_like(token)
    copies = []
    for source, target in ((gate_up_hbm, gate_up_ref), (down_hbm, down_ref)):
        rows = target.shape[0] // cuts
        for cut in range(cuts):
            span = pl.ds(cut * rows, rows)
            copies.append(
                pltpu.make_async_copy(
                    source.at[layer_no, 0, span], target.at[span], sems.at[len(copies)]
                )
            )
    for copy in copies:
        copy.start()
    for copy in copies:
        copy.wait()


def load_weights(layer_no, w_gate_up, w_down, after=()):
    cuts = 4
    return call(
        functools.partial(load_kernel, layer_no, cuts),
        [(w_gate_up.shape[2:], bf16), (w_down.shape[2:], bf16), ((8, LANES), f32)],
        [ANY] * 2,
        in_hbm(w_gate_up),
        in_hbm(w_down),
        scratch=[pltpu.SemaphoreType.DMA((2 * cuts,))],
        limit=12,
        after=after,
    )


def tile_of(extent, most):
    size = most
    while extent % size:
        size //= 2
    return size


def expert_kernel(first_column, wide, *refs):
    if wide:
        parts, refs = refs[:4], refs[4:]
        gate_up_ref, down_ref, *outs, routed_ref, rows_ref, hidden_ref = refs
    else:
        parts, refs = refs[:4], refs[4:]
        routed_ref, gate_up_ref, down_ref, *outs, rows_ref, hidden_ref = refs
    hidden_size, features = down_ref.shape
    quarter = parts[0].shape[0]
    for k, part in enumerate(parts):
        span = slice(k * quarter, (k + 1) * quarter)
        rows_ref[span] = part[:, :features]
        if wide:
            routed_ref[span] = part[:, features:]
    places = lax.broadcasted_iota(jnp.int32, routed_ref.shape, 1)
    column = first_column + lax.axis_index("expert")
    chosen = jnp.where(places == column, routed_ref[...].astype(f32), 0.0)
    share = jnp.sum(chosen, axis=1, keepdims=True)
    rows = rows_ref[...]
    size = tile_of(hidden_size, 256)
    for low in range(0, hidden_size, size):
        span, beside = slice(low, low + size), slice(hidden_size + low, hidden_size + low + size)
        gate = jnp.dot(rows, gate_up_ref[:, span], preferred_element_type=f32)
        up = jnp.dot(rows, gate_up_ref[:, beside], preferred_element_type=f32)
        hidden_ref[:, span] = (gate / (1.0 + jnp.exp(-gate)) * up).astype(bf16)
    hidden = hidden_ref[...]
    size = tile_of(features, 512)
    for low in range(0, features, size):
        span = slice(low, low + size)
        done = jnp.dot(hidden, down_ref[:, span], preferred_element_type=f32) * share
        for k, out in enumerate(outs):
            out[:, span] = done[k * quarter : (k + 1) * quarter].astype(out.dtype)


def run_expert(parts, routed, first_column, weights, after):
    gate_up, down_proj, _ = weights
    hidden_size, features = down_proj.shape
    quarter, width = parts[0].shape
    count = 4 * quarter
    wide = routed is None
    outs = [((quarter, features), f32)] * 2 + [((quarter, features), bf16)] * 2
    if wide:
        outs = outs + [((count, width - features), bf16)]
    found = call(
        functools.partial(expert_kernel, first_column, wide),
        outs,
        [VMEM] * (6 if wide else 7),
        *parts,
        *([] if wide else [routed]),
        gate_up,
        down_proj,
        scratch=[pltpu.VMEM((count, features), bf16), pltpu.VMEM((count, hidden_size), bf16)],
        limit=24,
        after=after,
    )
    return found[:4], found[4] if wide else routed


def in_hbm(array):
    return pltpu.with_memory_space_constraint(array, pltpu.HBM)


def open_rows(current, routes, gain, experts):
    batches, tokens, features = current.shape
    rows = batches * tokens
    columns = routes.shape[0] * experts
    width = features + columns + -columns % LANES
    current, routes = current.reshape(rows, features), jnp.swapaxes(routes, 2, 3)
    (wide,) = call(
        functools.partial(open_kernel, experts),
        [((rows, width), bf16)],
        [ANY] * 3,
        in_hbm(current),
        in_hbm(routes),
        in_hbm(gain),
        scratch=[
            pltpu.VMEM(current.shape, bf16),
            pltpu.VMEM(routes.shape, jnp.int32),
            pltpu.VMEM(gain.shape, f32),
            pltpu.SemaphoreType.DMA((3,)),
        ],
    )
    return wide


def run_layer(rows, routed, first_column, weights, loaded=()):
    far, tokens = lax.axis_size("expert") // 4, rows.shape[0]
    routed = routed or [None, None]
    half = far // 2
    sent = [rows] + [swap(rows, 4, k, far) for k in range(1, far)]
    first = join_rows(sent[:half], loaded, 0)
    first_beside = swap(first, 2, 1, 2)
    second = join_rows(sent[half:], (first,), WAIT)
    second_beside = swap(second, 2, 1, 2)

    def worked(near, beside, routed, until):
        beside = held(beside, until)
        parts = [near, beside, swap(near, 1, 1, 2), swap(beside, 1, 1, 2)]
        outs, columns = run_expert(parts, routed, first_column, weights, (until,))
        return outs, columns

    outs, first_columns = worked(first, first_beside, routed[0], second)
    mine, near, leaving = leave_pair(outs, ())
    outs2, second_columns = worked(second, second_beside, routed[1], outs[0])
    first_back = swap(held(leaving, second_beside), 2, 1, 2, True)
    arrived, last = split_rows(mine, near, first_back, range(half), tokens)
    mine2, near2, leaving2 = leave_pair(outs2, (last,))
    second_back = swap(leaving2, 2, 1, 2, True)
    arrived += split_rows(mine2, near2, second_back, range(half, far), tokens)[0]
    return arrived, [first_columns, second_columns], (outs2[0],)


def close_rows(layer_no, current, gain, returned, after=()):
    return call(
        functools.partial(close_kernel, layer_no),
        [(current.shape, bf16)] * 2,
        [VMEM] * (2 + len(returned)),
        current,
        gain,
        *returned,
        after=after,
    )


def on_device(inputs, routes, norm_gain, w_gate_up, w_down):
    experts = lax.axis_size("expert")
    sections = lax.axis_size("section")
    batches, tokens, features = inputs.shape
    layers = routes.shape[0]
    weights = load_weights(0, w_gate_up, w_down)
    if sections == 1:
        outs, routed = [], None
        current = inputs.reshape(batches * tokens, features)
        rows = open_rows(inputs, routes, norm_gain, experts)
        for layer_no in range(layers):
            returned, routed, worked = run_layer(
                rows, routed, layer_no * experts, weights, weights[2:]
            )
            if layer_no == layers - 1:
                (whole,) = call(
                    functools.partial(end_kernel, len(outs)),
                    [((layers, batches, tokens, features), bf16)],
                    [VMEM] * (1 + len(returned) + len(outs)),
                    current,
                    *returned,
                    *outs,
                )
                return whole
            weights = load_weights(layer_no + 1, w_gate_up, w_down, worked)
            current, rows = close_rows(layer_no + 1, current, norm_gain, returned, weights[2:])
            outs.append(current)
    segment_no = lax.axis_index("section")
    handed = jnp.zeros((tokens, features), bf16)
    finished = []
    for turn_no in range(batches + 1):
        if turn_no < batches:
            fresh_rows = inputs[turn_no]
        else:
            fresh_rows = jnp.zeros((tokens, features), bf16)
        current = jnp.where(segment_no == 0, fresh_rows, handed)
        batch_pick = jnp.clip(turn_no - segment_no, 0, batches - 1)
        turn_routes = lax.dynamic_slice_in_dim(routes, batch_pick, 1, 1)
        rows = open_rows(current[None], turn_routes, norm_gain, experts)
        returned, _, _ = run_layer(rows, None, 0, weights)
        result, _ = close_rows(0, current, norm_gain, returned)
        finished.append(result)
        if turn_no < batches:
            handed = from_behind(result, "section", 1)
    first_segment = jnp.stack(finished[:batches])
    second_segment = jnp.stack(finished[1:])
    return jnp.where(segment_no == 0, first_segment, second_segment)[None]


def solution(mesh):
    placed = (
        P(None, ("groups", "expert"), None),
        P("section", None, ("groups", "expert"), None),
        P("section", None),
        P("section", "expert", None, None),
        P("section", "expert", None, None),
    )
    return jax.shard_map(
        on_device,
        mesh=mesh,
        in_specs=placed,
        out_specs=P("section", None, ("groups", "expert"), None),
        check_vma=False,
    )
```

```python
import functools

import jax
import jax.numpy as jnp
from jax import lax
from jax.experimental import pallas as pl
from jax.experimental.pallas import tpu as pltpu
from jax.sharding import PartitionSpec as P

eps = 1e-06
LANES = 128
MIB = 2**20
WAIT = 6 * 10**9
VMEM = pl.BlockSpec(memory_space=pltpu.VMEM)
ANY = pl.BlockSpec(memory_space=pl.ANY)
bf16, f32 = jnp.bfloat16, jnp.float32


def from_behind(value, axis, steps):
    count = lax.axis_size(axis)
    initial, last = (max(0, -steps), min(count, count - steps))
    return lax.ppermute(value, axis, [(source, source + steps) for source in range(initial, last)])


def call(kernel, outs, specs, *operands, scratch=(), limit=8, after=(), weight=0):
    shapes = tuple(jax.ShapeDtypeStruct(shape, dtype) for shape, dtype in outs)
    operands = (*after, *operands)
    return pl.pallas_call(
        lambda *refs: kernel(*refs[len(after) :]),
        out_shape=shapes,
        in_specs=[ANY] * len(after) + specs,
        out_specs=(VMEM,) * len(outs),
        scratch_shapes=scratch,
        compiler_params=pltpu.CompilerParams(vmem_limit_bytes=limit * MIB),
        cost_estimate=pl.CostEstimate(flops=weight, bytes_accessed=0, transcendentals=0),
    )(*operands)


def swap(value, stride, step, radix, back=False):
    count = lax.axis_size("expert")

    def partner(index):
        digit = index // stride % radix
        if radix & (radix - 1) == 0:
            other = digit ^ step
        else:
            other = (digit + (step if back else radix - step)) % radix
        return index + (other - digit) * stride

    return lax.ppermute(value, "expert", [(i, partner(i)) for i in range(count)])


def join_kernel(*refs):
    *parts, whole = refs
    rows = parts[0].shape[0]
    for k, part in enumerate(parts):
        whole[k * rows : (k + 1) * rows] = part[...]


def join_rows(parts, after, weight):
    tokens, width = parts[0].shape
    return call(
        join_kernel,
        [((len(parts) * tokens, width), parts[0].dtype)],
        [VMEM] * len(parts),
        *parts,
        after=after,
        weight=weight,
    )[0]


def held(value, until):
    return lax.optimization_barrier((value, until))[0]


def sum_kernel(mine, upper, lower, total):
    half = upper.shape[0]
    total[:half] = (mine[:half] + upper[...].astype(f32)).astype(total.dtype)
    total[half:] = (mine[half:] + lower[...].astype(f32)).astype(total.dtype)


def split_kernel(mine, near, beside, *pieces):
    rows = pieces[0].shape[0]
    total = mine[...] + near[...].astype(f32) + beside[...].astype(f32)
    for k, piece in enumerate(pieces):
        piece[...] = total[k * rows : (k + 1) * rows].astype(piece.dtype)


def leave_pair(found, after):
    mine_near, mine_beside, other_near, *other_beside = found
    arrived_beside = [swap(half, 1, 1, 2, True) for half in other_beside]
    arrived_near = swap(other_near, 1, 1, 2, True)
    (leaving,) = call(
        sum_kernel,
        [(mine_beside.shape, bf16)],
        [VMEM] * 3,
        mine_beside,
        *arrived_beside,
        after=after,
    )
    return mine_near, arrived_near, leaving


def split_rows(mine_near, arrived_near, beside, distances, tokens):
    far = lax.axis_size("expert") // 4
    pieces = call(
        split_kernel,
        [((tokens, beside.shape[1]), bf16 if k else f32) for k in distances],
        [VMEM] * 3,
        mine_near,
        arrived_near,
        beside,
    )
    arrived = [swap(piece, 4, k, far, True) if k else piece for k, piece in zip(distances, pieces)]
    return arrived, pieces[-1]


def normed_rows(widened, gain_row):
    scale_inv = lax.rsqrt(jnp.mean(widened * widened, axis=-1, keepdims=True) + eps)
    return (widened * scale_inv * gain_row).astype(bf16)


def open_kernel(experts, current_hbm, routes_hbm, gain_hbm, wide_ref, current, routes, gain, sems):
    pairs = ((current_hbm, current), (routes_hbm, routes), (gain_hbm, gain))
    copies = [pltpu.make_async_copy(a, b, sems.at[k]) for k, (a, b) in enumerate(pairs)]
    for copy in copies:
        copy.start()
    for copy in copies:
        copy.wait()
    features = current.shape[-1]
    layers, batches, top, tokens = routes.shape
    columns = wide_ref.shape[1] - features
    wide_ref[:, :features] = normed_rows(current[...].astype(f32), gain[0:1])
    places = lax.broadcasted_iota(jnp.int32, (columns, tokens), 0)
    same = lax.broadcasted_iota(jnp.int32, (tokens, tokens), 0) == lax.broadcasted_iota(
        jnp.int32, (tokens, tokens), 1
    )
    for batch in range(batches):
        chosen = jnp.zeros(places.shape, f32)
        for layer_no in range(layers):
            named = routes[layer_no, batch] + layer_no * experts
            for k in range(top):
                chosen = jnp.where(places == named[k : k + 1], 1.0, chosen)
        turned = lax.dot_general(
            same.astype(bf16),
            chosen.astype(bf16),
            (((1,), (1,)), ((), ())),
            preferred_element_type=f32,
        )
        wide_ref[batch * tokens : (batch + 1) * tokens, features:] = turned.astype(bf16)


def total_rows(current, kept, sent):
    total = kept[...]
    for piece in sent:
        total = total + piece[...].astype(f32)
    return (current.astype(f32) + total * 0.125).astype(bf16)


def close_kernel(layer_no, current_ref, gain_ref, kept, *refs):
    *sent, out_ref, normed_ref = refs
    out = total_rows(current_ref[...], kept, sent)
    out_ref[...] = out
    normed_ref[...] = normed_rows(out.astype(f32), gain_ref[layer_no : layer_no + 1])


def end_kernel(earlier, current_ref, kept, *refs):
    sent, before, outs_ref = refs[: len(refs) - earlier - 1], refs[-earlier - 1 : -1], refs[-1]
    layers, batches, tokens, _ = outs_ref.shape
    done = [ref[...] for ref in before] + [total_rows(current_ref[...], kept, sent)]
    for layer_no in range(layers):
        for batch in range(batches):
            outs_ref[layer_no, batch] = done[layer_no][batch * tokens : (batch + 1) * tokens]


def load_kernel(layer_no, cuts, gate_up_hbm, down_hbm, gate_up_ref, down_ref, token, sems):
    token[...] = jnp.zeros_like(token)
    copies = []
    for source, target in ((gate_up_hbm, gate_up_ref), (down_hbm, down_ref)):
        rows = target.shape[0] // cuts
        for cut in range(cuts):
            span = pl.ds(cut * rows, rows)
            copies.append(
                pltpu.make_async_copy(
                    source.at[layer_no, 0, span], target.at[span], sems.at[len(copies)]
                )
            )
    for copy in copies:
        copy.start()
    for copy in copies:
        copy.wait()


def load_weights(layer_no, w_gate_up, w_down, after=()):
    cuts = 4
    return call(
        functools.partial(load_kernel, layer_no, cuts),
        [(w_gate_up.shape[2:], bf16), (w_down.shape[2:], bf16), ((8, LANES), f32)],
        [ANY] * 2,
        in_hbm(w_gate_up),
        in_hbm(w_down),
        scratch=[pltpu.SemaphoreType.DMA((2 * cuts,))],
        limit=12,
        after=after,
    )


def tile_of(extent, most):
    size = most
    while extent % size:
        size //= 2
    return size


def expert_kernel(first_column, wide, *refs):
    if wide:
        parts, refs = refs[:4], refs[4:]
        gate_up_ref, down_ref, *outs, routed_ref, rows_ref, hidden_ref = refs
    else:
        parts, refs = refs[:4], refs[4:]
        routed_ref, gate_up_ref, down_ref, *outs, rows_ref, hidden_ref = refs
    hidden_size, features = down_ref.shape
    quarter = parts[0].shape[0]
    for k, part in enumerate(parts):
        span = slice(k * quarter, (k + 1) * quarter)
        rows_ref[span] = part[:, :features]
        if wide:
            routed_ref[span] = part[:, features:]
    places = lax.broadcasted_iota(jnp.int32, routed_ref.shape, 1)
    column = first_column + lax.axis_index("expert")
    chosen = jnp.where(places == column, routed_ref[...].astype(f32), 0.0)
    share = jnp.sum(chosen, axis=1, keepdims=True)
    rows = rows_ref[...]
    size = tile_of(hidden_size, 256)
    for low in range(0, hidden_size, size):
        span, beside = slice(low, low + size), slice(hidden_size + low, hidden_size + low + size)
        gate = jnp.dot(rows, gate_up_ref[:, span], preferred_element_type=f32)
        up = jnp.dot(rows, gate_up_ref[:, beside], preferred_element_type=f32)
        hidden_ref[:, span] = (gate / (1.0 + jnp.exp(-gate)) * up).astype(bf16)
    hidden = hidden_ref[...]
    size = tile_of(features, 512)
    for low in range(0, features, size):
        span = slice(low, low + size)
        done = jnp.dot(hidden, down_ref[:, span], preferred_element_type=f32) * share
        first = 0
        for out in outs:
            out[:, span] = done[first : first + out.shape[0]].astype(out.dtype)
            first += out.shape[0]


def run_expert(parts, routed, first_column, weights, after):
    gate_up, down_proj, _ = weights
    hidden_size, features = down_proj.shape
    quarter, width = parts[0].shape
    count = 4 * quarter
    wide = routed is None
    outs = [((quarter, features), f32)] * 2 + [((quarter, features), bf16)]
    outs += [((quarter // 2, features), bf16)] * 2
    if wide:
        outs = outs + [((count, width - features), bf16)]
    found = call(
        functools.partial(expert_kernel, first_column, wide),
        outs,
        [VMEM] * (6 if wide else 7),
        *parts,
        *([] if wide else [routed]),
        gate_up,
        down_proj,
        scratch=[pltpu.VMEM((count, features), bf16), pltpu.VMEM((count, hidden_size), bf16)],
        limit=24,
        after=after,
    )
    return found[:5], found[5] if wide else routed


def in_hbm(array):
    return pltpu.with_memory_space_constraint(array, pltpu.HBM)


def open_rows(current, routes, gain, experts):
    batches, tokens, features = current.shape
    rows = batches * tokens
    columns = routes.shape[0] * experts
    width = features + columns + -columns % LANES
    current, routes = current.reshape(rows, features), jnp.swapaxes(routes, 2, 3)
    (wide,) = call(
        functools.partial(open_kernel, experts),
        [((rows, width), bf16)],
        [ANY] * 3,
        in_hbm(current),
        in_hbm(routes),
        in_hbm(gain),
        scratch=[
            pltpu.VMEM(current.shape, bf16),
            pltpu.VMEM(routes.shape, jnp.int32),
            pltpu.VMEM(gain.shape, f32),
            pltpu.SemaphoreType.DMA((3,)),
        ],
    )
    return wide


def run_layer(rows, routed, first_column, weights, loaded=()):
    far, tokens = lax.axis_size("expert") // 4, rows.shape[0]
    routed = routed or [None, None]
    half = far // 2
    sent = [rows] + [swap(rows, 4, k, far) for k in range(1, far)]
    first = join_rows(sent[:half], loaded, 0)
    first_beside = swap(first, 2, 1, 2)
    second = join_rows(sent[half:], (first,), WAIT)
    second_beside = swap(second, 2, 1, 2)

    def worked(near, beside, routed, until):
        beside = held(beside, until)
        parts = [near, beside, swap(near, 1, 1, 2), swap(beside, 1, 1, 2)]
        return run_expert(parts, routed, first_column, weights, (until,))

    outs, first_columns = worked(first, first_beside, routed[0], second)
    mine, near, leaving = leave_pair(outs, ())
    first_back = swap(leaving, 2, 1, 2, True)
    outs2, second_columns = worked(second, second_beside, routed[1], leaving)
    arrived, last = split_rows(mine, near, first_back, range(half), tokens)
    mine2, near2, leaving2 = leave_pair(outs2, (last,))
    second_back = swap(leaving2, 2, 1, 2, True)
    arrived += split_rows(mine2, near2, second_back, range(half, far), tokens)[0]
    return arrived, [first_columns, second_columns], (outs2[0],)


def close_rows(layer_no, current, gain, returned, after=()):
    return call(
        functools.partial(close_kernel, layer_no),
        [(current.shape, bf16)] * 2,
        [VMEM] * (2 + len(returned)),
        current,
        gain,
        *returned,
        after=after,
    )


def on_device(inputs, routes, norm_gain, w_gate_up, w_down):
    experts = lax.axis_size("expert")
    sections = lax.axis_size("section")
    batches, tokens, features = inputs.shape
    layers = routes.shape[0]
    weights = load_weights(0, w_gate_up, w_down)
    if sections == 1:
        outs, routed = [], None
        current = inputs.reshape(batches * tokens, features)
        rows = open_rows(inputs, routes, norm_gain, experts)
        for layer_no in range(layers):
            returned, routed, worked = run_layer(
                rows, routed, layer_no * experts, weights, weights[2:]
            )
            if layer_no == layers - 1:
                (whole,) = call(
                    functools.partial(end_kernel, len(outs)),
                    [((layers, batches, tokens, features), bf16)],
                    [VMEM] * (1 + len(returned) + len(outs)),
                    current,
                    *returned,
                    *outs,
                )
                return whole
            weights = load_weights(layer_no + 1, w_gate_up, w_down, worked)
            current, rows = close_rows(layer_no + 1, current, norm_gain, returned, weights[2:])
            outs.append(current)
    segment_no = lax.axis_index("section")
    handed = jnp.zeros((tokens, features), bf16)
    finished = []
    for turn_no in range(batches + 1):
        if turn_no < batches:
            fresh_rows = inputs[turn_no]
        else:
            fresh_rows = jnp.zeros((tokens, features), bf16)
        current = jnp.where(segment_no == 0, fresh_rows, handed)
        batch_pick = jnp.clip(turn_no - segment_no, 0, batches - 1)
        turn_routes = lax.dynamic_slice_in_dim(routes, batch_pick, 1, 1)
        rows = open_rows(current[None], turn_routes, norm_gain, experts)
        returned, _, _ = run_layer(rows, None, 0, weights)
        result, _ = close_rows(0, current, norm_gain, returned)
        finished.append(result)
        if turn_no < batches:
            handed = from_behind(result, "section", 1)
    first_segment = jnp.stack(finished[:batches])
    second_segment = jnp.stack(finished[1:])
    return jnp.where(segment_no == 0, first_segment, second_segment)[None]


def solution(mesh):
    placed = (
        P(None, ("groups", "expert"), None),
        P("section", None, ("groups", "expert"), None),
        P("section", None),
        P("section", "expert", None, None),
        P("section", "expert", None, None),
    )
    return jax.shard_map(
        on_device,
        mesh=mesh,
        in_specs=placed,
        out_specs=P("section", None, ("groups", "expert"), None),
        check_vma=False,
    )
```

```python
import functools

import jax
import jax.numpy as jnp
from jax import lax
from jax.experimental import pallas as pl
from jax.experimental.pallas import tpu as pltpu
from jax.sharding import PartitionSpec as P

eps = 1e-06
LANES = 128
MIB = 2**20
CUTS = 2
VMEM = pl.BlockSpec(memory_space=pltpu.VMEM)
ANY = pl.BlockSpec(memory_space=pl.ANY)
bf16, f32 = jnp.bfloat16, jnp.float32


def from_behind(value, axis, steps):
    count = lax.axis_size(axis)
    initial, last = (max(0, -steps), min(count, count - steps))
    return lax.ppermute(value, axis, [(source, source + steps) for source in range(initial, last)])


def call(kernel, outs, specs, *operands, scratch=(), limit=8, after=()):
    shapes = tuple(jax.ShapeDtypeStruct(shape, dtype) for shape, dtype in outs)
    operands = (*after, *operands)
    return pl.pallas_call(
        lambda *refs: kernel(*refs[len(after) :]),
        out_shape=shapes,
        in_specs=[ANY] * len(after) + specs,
        out_specs=(VMEM,) * len(outs),
        scratch_shapes=scratch,
        compiler_params=pltpu.CompilerParams(vmem_limit_bytes=limit * MIB),
        cost_estimate=pl.CostEstimate(flops=0, bytes_accessed=0, transcendentals=0),
    )(*operands)


def swap(value, stride, step, radix, back=False):
    count = lax.axis_size("expert")

    def partner(index):
        digit = index // stride % radix
        if radix & (radix - 1) == 0:
            other = digit ^ step
        else:
            other = (digit + (step if back else radix - step)) % radix
        return index + (other - digit) * stride

    return lax.ppermute(value, "expert", [(i, partner(i)) for i in range(count)])


def join_kernel(count, *refs):
    parts, wholes = refs[:count], refs[count:]
    rows, size = parts[0].shape[0], count // len(wholes)
    for k, part in enumerate(parts):
        wholes[k // size][k % size * rows : (k % size + 1) * rows] = part[...]


def cut_kernel(whole, *parts):
    rows = parts[0].shape[0]
    for k, part in enumerate(parts):
        part[...] = whole[k * rows : (k + 1) * rows]


def cut_rows(whole, count, after):
    shape = (whole.shape[0] // count, whole.shape[1])
    return call(cut_kernel, [(shape, whole.dtype)] * count, [VMEM], whole, after=after)


def held(value, until):
    return lax.optimization_barrier((value, until))[0] if until is not None else value


def gather_rows(rows, after):
    far = lax.axis_size("expert") // 4
    tokens, width = rows.shape
    parts = [rows] + [swap(rows, 4, k, far) for k in range(1, far)]
    shape = (far // 2 * tokens, width)
    batches, beside = [], None
    for near in call(
        functools.partial(join_kernel, far),
        [(shape, rows.dtype)] * 2,
        [VMEM] * far,
        *parts[far // 2 :],
        *parts[: far // 2],
        after=after,
    ):
        near = held(near, beside)
        beside = swap(near, 2, 1, 2)
        batches.append([near, beside])
    return batches


def sum_kernel(mine, upper, lower, total):
    half = upper.shape[0]
    total[:half] = (mine[:half] + upper[...].astype(f32)).astype(total.dtype)
    total[half:] = (mine[half:] + lower[...].astype(f32)).astype(total.dtype)


def split_kernel(mine, near, beside, *pieces):
    rows = pieces[0].shape[0]
    total = mine[...] + near[...].astype(f32) + beside[...].astype(f32)
    for k, piece in enumerate(pieces):
        piece[...] = total[k * rows : (k + 1) * rows].astype(piece.dtype)


def leave_pair(found, after):
    mine_near, mine_beside, other_near, *other_beside = found
    arrived_beside = [swap(half, 1, 1, 2, True) for half in other_beside]
    arrived_near = swap(other_near, 1, 1, 2, True)
    (leaving,) = call(
        sum_kernel,
        [(mine_beside.shape, bf16)],
        [VMEM] * 3,
        mine_beside,
        *arrived_beside,
        after=after,
    )
    return mine_near, arrived_near, leaving


def split_rows(left, distances, tokens):
    far = lax.axis_size("expert") // 4
    mine_near, arrived_near, leaving = left
    beside = swap(leaving, 2, 1, 2, True)
    pieces = call(
        split_kernel,
        [((tokens, leaving.shape[1]), bf16 if k else f32) for k in distances],
        [VMEM] * 3,
        mine_near,
        arrived_near,
        beside,
    )
    arrived = [swap(piece, 4, k, far, True) if k else piece for k, piece in zip(distances, pieces)]
    return arrived, pieces[-1]


def normed_rows(widened, gain_row):
    scale_inv = lax.rsqrt(jnp.mean(widened * widened, axis=-1, keepdims=True) + eps)
    return (widened * scale_inv * gain_row).astype(bf16)


def open_kernel(experts, current_hbm, routes_hbm, gain_hbm, wide_ref, current, routes, gain, sems):
    pairs = ((current_hbm, current), (routes_hbm, routes), (gain_hbm, gain))
    copies = [pltpu.make_async_copy(a, b, sems.at[k]) for k, (a, b) in enumerate(pairs)]
    for copy in copies:
        copy.start()
    for copy in copies:
        copy.wait()
    features = current.shape[-1]
    layers, batches, top, tokens = routes.shape
    columns = wide_ref.shape[1] - features
    wide_ref[:, :features] = normed_rows(current[...].astype(f32), gain[0:1])
    places = lax.broadcasted_iota(jnp.int32, (columns, tokens), 0)
    same = lax.broadcasted_iota(jnp.int32, (tokens, tokens), 0) == lax.broadcasted_iota(
        jnp.int32, (tokens, tokens), 1
    )
    for batch in range(batches):
        chosen = jnp.zeros(places.shape, f32)
        for layer_no in range(layers):
            named = routes[layer_no, batch] + layer_no * experts
            for k in range(top):
                chosen = jnp.where(places == named[k : k + 1], 1.0, chosen)
        turned = lax.dot_general(
            same.astype(bf16),
            chosen.astype(bf16),
            (((1,), (1,)), ((), ())),
            preferred_element_type=f32,
        )
        wide_ref[batch * tokens : (batch + 1) * tokens, features:] = turned.astype(bf16)


def total_rows(current, kept, sent):
    total = kept[...]
    for piece in sent:
        total = total + piece[...].astype(f32)
    return (current.astype(f32) + total * 0.125).astype(bf16)


def close_kernel(layer_no, current_ref, gain_ref, kept, *refs):
    *sent, out_ref, normed_ref = refs
    out = total_rows(current_ref[...], kept, sent)
    out_ref[...] = out
    normed_ref[...] = normed_rows(out.astype(f32), gain_ref[layer_no : layer_no + 1])


def end_kernel(earlier, current_ref, kept, *refs):
    sent, before, outs_ref = refs[: len(refs) - earlier - 1], refs[-earlier - 1 : -1], refs[-1]
    layers, batches, tokens, _ = outs_ref.shape
    done = [ref[...] for ref in before] + [total_rows(current_ref[...], kept, sent)]
    for layer_no in range(layers):
        for batch in range(batches):
            outs_ref[layer_no, batch] = done[layer_no][batch * tokens : (batch + 1) * tokens]


def load_kernel(layer_no, cuts, gate_up_hbm, down_hbm, gate_up_ref, down_ref, token, sems):
    token[...] = jnp.zeros_like(token)
    copies = []
    for source, target in ((gate_up_hbm, gate_up_ref), (down_hbm, down_ref)):
        rows = target.shape[0] // cuts
        for cut in range(cuts):
            span = pl.ds(cut * rows, rows)
            copies.append(
                pltpu.make_async_copy(
                    source.at[layer_no, 0, span], target.at[span], sems.at[len(copies)]
                )
            )
    for copy in copies:
        copy.start()
    for copy in copies:
        copy.wait()


def load_weights(layer_no, w_gate_up, w_down, after=()):
    cuts = 4
    return call(
        functools.partial(load_kernel, layer_no, cuts),
        [(w_gate_up.shape[2:], bf16), (w_down.shape[2:], bf16), ((8, LANES), f32)],
        [ANY] * 2,
        in_hbm(w_gate_up),
        in_hbm(w_down),
        scratch=[pltpu.SemaphoreType.DMA((2 * cuts,))],
        limit=12,
        after=after,
    )


def tile_of(extent, most):
    size = most
    while extent % size:
        size //= 2
    return size


def expert_kernel(count, first_column, wide, *refs):
    parts, refs = refs[:count], refs[count:]
    if wide:
        gate_up_ref, down_ref, *outs, routed_ref, rows_ref, hidden_ref = refs
    else:
        routed_ref, gate_up_ref, down_ref, *outs, rows_ref, hidden_ref = refs
    hidden_size, features = down_ref.shape
    first = 0
    for part in parts:
        span = slice(first, first + part.shape[0])
        first += part.shape[0]
        rows_ref[span] = part[:, :features]
        if wide:
            routed_ref[span] = part[:, features:]
    places = lax.broadcasted_iota(jnp.int32, routed_ref.shape, 1)
    column = first_column + lax.axis_index("expert")
    chosen = jnp.where(places == column, routed_ref[...].astype(f32), 0.0)
    share = jnp.sum(chosen, axis=1, keepdims=True)
    rows = rows_ref[...]
    size = tile_of(hidden_size, 256)
    for low in range(0, hidden_size, size):
        span, beside = slice(low, low + size), slice(hidden_size + low, hidden_size + low + size)
        gate = jnp.dot(rows, gate_up_ref[:, span], preferred_element_type=f32)
        up = jnp.dot(rows, gate_up_ref[:, beside], preferred_element_type=f32)
        hidden_ref[:, span] = (gate / (1.0 + jnp.exp(-gate)) * up).astype(bf16)
    hidden = hidden_ref[...]
    size = tile_of(features, 512)
    for low in range(0, features, size):
        span = slice(low, low + size)
        done = jnp.dot(hidden, down_ref[:, span], preferred_element_type=f32) * share
        first = 0
        for out in outs:
            out[:, span] = done[first : first + out.shape[0]].astype(out.dtype)
            first += out.shape[0]


def run_expert(parts, routed, first_column, weights, after):
    gate_up, down_proj, _ = weights
    hidden_size, features = down_proj.shape
    width = parts[0].shape[1]
    count = sum(part.shape[0] for part in parts)
    quarter = count // 4
    wide = routed is None
    outs = [((quarter, features), f32)] * 2 + [((quarter, features), bf16)]
    outs += [((quarter // 2, features), bf16)] * 2
    if wide:
        outs = outs + [((count, width - features), bf16)]
    found = call(
        functools.partial(expert_kernel, len(parts), first_column, wide),
        outs,
        [VMEM] * (len(parts) + (2 if wide else 3)),
        *parts,
        *([] if wide else [routed]),
        gate_up,
        down_proj,
        scratch=[pltpu.VMEM((count, features), bf16), pltpu.VMEM((count, hidden_size), bf16)],
        limit=24,
        after=after,
    )
    return found[:5], found[5] if wide else routed


def in_hbm(array):
    return pltpu.with_memory_space_constraint(array, pltpu.HBM)


def open_rows(current, routes, gain, experts):
    batches, tokens, features = current.shape
    rows = batches * tokens
    columns = routes.shape[0] * experts
    width = features + columns + -columns % LANES
    current, routes = current.reshape(rows, features), jnp.swapaxes(routes, 2, 3)
    (wide,) = call(
        functools.partial(open_kernel, experts),
        [((rows, width), bf16)],
        [ANY] * 3,
        in_hbm(current),
        in_hbm(routes),
        in_hbm(gain),
        scratch=[
            pltpu.VMEM(current.shape, bf16),
            pltpu.VMEM(routes.shape, jnp.int32),
            pltpu.VMEM(gain.shape, f32),
            pltpu.SemaphoreType.DMA((3,)),
        ],
    )
    return wide


def run_layer(rows, routed, first_column, weights, loaded=()):
    far, tokens = lax.axis_size("expert") // 4, rows.shape[0]
    columns, returned, after, worked = [], [], (), ()
    distances = [range(far // 2, far), range(far // 2)]
    for place, (near, beside) in enumerate(gather_rows(rows, loaded)):
        parts = [near, *cut_rows(beside, CUTS, (left[2],))] if place else [near, beside]
        parts += [swap(part, 1, 1, 2) for part in parts]
        outs, kept = run_expert(
            parts, None if routed is None else routed[place], first_column, weights, worked
        )
        columns.append(kept)
        left = leave_pair(outs, after)
        arrived, last = split_rows(left, distances[place], tokens)
        returned = arrived + returned
        after, worked = (last,), (left[2],)
    return returned, columns, (outs[0],)


def close_rows(layer_no, current, gain, returned, after=()):
    return call(
        functools.partial(close_kernel, layer_no),
        [(current.shape, bf16)] * 2,
        [VMEM] * (2 + len(returned)),
        current,
        gain,
        *returned,
        after=after,
    )


def on_device(inputs, routes, norm_gain, w_gate_up, w_down):
    experts = lax.axis_size("expert")
    sections = lax.axis_size("section")
    batches, tokens, features = inputs.shape
    layers = routes.shape[0]
    weights = load_weights(0, w_gate_up, w_down)
    if sections == 1:
        outs, routed = [], None
        current = inputs.reshape(batches * tokens, features)
        rows = open_rows(inputs, routes, norm_gain, experts)
        for layer_no in range(layers):
            returned, routed, worked = run_layer(
                rows, routed, layer_no * experts, weights, weights[2:]
            )
            if layer_no == layers - 1:
                (whole,) = call(
                    functools.partial(end_kernel, len(outs)),
                    [((layers, batches, tokens, features), bf16)],
                    [VMEM] * (1 + len(returned) + len(outs)),
                    current,
                    *returned,
                    *outs,
                )
                return whole
            weights = load_weights(layer_no + 1, w_gate_up, w_down, worked)
            current, rows = close_rows(layer_no + 1, current, norm_gain, returned, weights[2:])
            outs.append(current)
    segment_no = lax.axis_index("section")
    handed = jnp.zeros((tokens, features), bf16)
    finished = []
    for turn_no in range(batches + 1):
        if turn_no < batches:
            fresh_rows = inputs[turn_no]
        else:
            fresh_rows = jnp.zeros((tokens, features), bf16)
        current = jnp.where(segment_no == 0, fresh_rows, handed)
        batch_pick = jnp.clip(turn_no - segment_no, 0, batches - 1)
        turn_routes = lax.dynamic_slice_in_dim(routes, batch_pick, 1, 1)
        rows = open_rows(current[None], turn_routes, norm_gain, experts)
        returned, _, _ = run_layer(rows, None, 0, weights)
        result, _ = close_rows(0, current, norm_gain, returned)
        finished.append(result)
        if turn_no < batches:
            handed = from_behind(result, "section", 1)
    first_segment = jnp.stack(finished[:batches])
    second_segment = jnp.stack(finished[1:])
    return jnp.where(segment_no == 0, first_segment, second_segment)[None]


def solution(mesh):
    placed = (
        P(None, ("groups", "expert"), None),
        P("section", None, ("groups", "expert"), None),
        P("section", None),
        P("section", "expert", None, None),
        P("section", "expert", None, None),
    )
    return jax.shard_map(
        on_device,
        mesh=mesh,
        in_specs=placed,
        out_specs=P("section", None, ("groups", "expert"), None),
        check_vma=False,
    )
```

```python
import functools

import jax
import jax.numpy as jnp
from jax import lax
from jax.experimental import pallas as pl
from jax.experimental.pallas import tpu as pltpu
from jax.sharding import PartitionSpec as P

eps = 1e-06
LANES = 128
MIB = 2**20
CUTS = 2
WAIT = 6 * 10**9
VMEM = pl.BlockSpec(memory_space=pltpu.VMEM)
ANY = pl.BlockSpec(memory_space=pl.ANY)
bf16, f32 = jnp.bfloat16, jnp.float32


def from_behind(value, axis, steps):
    count = lax.axis_size(axis)
    initial, last = (max(0, -steps), min(count, count - steps))
    return lax.ppermute(value, axis, [(source, source + steps) for source in range(initial, last)])


def call(kernel, outs, specs, *operands, scratch=(), limit=8, after=(), weight=0):
    shapes = tuple(jax.ShapeDtypeStruct(shape, dtype) for shape, dtype in outs)
    operands = (*after, *operands)
    return pl.pallas_call(
        lambda *refs: kernel(*refs[len(after) :]),
        out_shape=shapes,
        in_specs=[ANY] * len(after) + specs,
        out_specs=(VMEM,) * len(outs),
        scratch_shapes=scratch,
        compiler_params=pltpu.CompilerParams(vmem_limit_bytes=limit * MIB),
        cost_estimate=pl.CostEstimate(flops=weight, bytes_accessed=0, transcendentals=0),
    )(*operands)


def swap(value, stride, step, radix, back=False):
    count = lax.axis_size("expert")

    def partner(index):
        digit = index // stride % radix
        if radix & (radix - 1) == 0:
            other = digit ^ step
        else:
            other = (digit + (step if back else radix - step)) % radix
        return index + (other - digit) * stride

    return lax.ppermute(value, "expert", [(i, partner(i)) for i in range(count)])


def join_kernel(*refs):
    *parts, whole = refs
    rows = parts[0].shape[0]
    for k, part in enumerate(parts):
        whole[k * rows : (k + 1) * rows] = part[...]


def join_rows(parts, after, weight):
    tokens, width = parts[0].shape
    return call(
        join_kernel,
        [((len(parts) * tokens, width), parts[0].dtype)],
        [VMEM] * len(parts),
        *parts,
        after=after,
        weight=weight,
    )[0]


def held(value, until):
    return lax.optimization_barrier((value, until))[0]


def sum_kernel(mine, *refs):
    *parts, total = refs
    rows = parts[0].shape[0]
    for k, part in enumerate(parts):
        span = slice(k * rows, (k + 1) * rows)
        total[span] = (mine[span] + part[...].astype(f32)).astype(total.dtype)


def split_kernel(mine, near, beside, *pieces):
    rows = pieces[0].shape[0]
    total = mine[...] + near[...].astype(f32) + beside[...].astype(f32)
    for k, piece in enumerate(pieces):
        piece[...] = total[k * rows : (k + 1) * rows].astype(piece.dtype)


def leave_pair(found, after):
    mine_near, mine_beside, other_near, *other_beside = found
    arrived_beside = [swap(half, 1, 1, 2, True) for half in other_beside]
    arrived_near = swap(other_near, 1, 1, 2, True)
    (leaving,) = call(
        sum_kernel,
        [(mine_beside.shape, bf16)],
        [VMEM] * (1 + CUTS),
        mine_beside,
        *arrived_beside,
        after=after,
    )
    return mine_near, arrived_near, leaving


def split_rows(mine_near, arrived_near, beside, distances, tokens):
    far = lax.axis_size("expert") // 4
    pieces = call(
        split_kernel,
        [((tokens, beside.shape[1]), bf16 if k else f32) for k in distances],
        [VMEM] * 3,
        mine_near,
        arrived_near,
        beside,
    )
    arrived = [swap(piece, 4, k, far, True) if k else piece for k, piece in zip(distances, pieces)]
    return arrived, pieces[-1]


def normed_rows(widened, gain_row):
    scale_inv = lax.rsqrt(jnp.mean(widened * widened, axis=-1, keepdims=True) + eps)
    return (widened * scale_inv * gain_row).astype(bf16)


def open_kernel(experts, current_hbm, routes_hbm, gain_hbm, wide_ref, current, routes, gain, sems):
    pairs = ((current_hbm, current), (routes_hbm, routes), (gain_hbm, gain))
    copies = [pltpu.make_async_copy(a, b, sems.at[k]) for k, (a, b) in enumerate(pairs)]
    for copy in copies:
        copy.start()
    for copy in copies:
        copy.wait()
    features = current.shape[-1]
    layers, batches, top, tokens = routes.shape
    columns = wide_ref.shape[1] - features
    wide_ref[:, :features] = normed_rows(current[...].astype(f32), gain[0:1])
    places = lax.broadcasted_iota(jnp.int32, (columns, tokens), 0)
    same = lax.broadcasted_iota(jnp.int32, (tokens, tokens), 0) == lax.broadcasted_iota(
        jnp.int32, (tokens, tokens), 1
    )
    for batch in range(batches):
        chosen = jnp.zeros(places.shape, f32)
        for layer_no in range(layers):
            named = routes[layer_no, batch] + layer_no * experts
            for k in range(top):
                chosen = jnp.where(places == named[k : k + 1], 1.0, chosen)
        turned = lax.dot_general(
            same.astype(bf16),
            chosen.astype(bf16),
            (((1,), (1,)), ((), ())),
            preferred_element_type=f32,
        )
        wide_ref[batch * tokens : (batch + 1) * tokens, features:] = turned.astype(bf16)


def total_rows(current, kept, sent):
    total = kept[...]
    for piece in sent:
        total = total + piece[...].astype(f32)
    return (current.astype(f32) + total * 0.125).astype(bf16)


def close_kernel(layer_no, current_ref, gain_ref, kept, *refs):
    *sent, out_ref, normed_ref = refs
    out = total_rows(current_ref[...], kept, sent)
    out_ref[...] = out
    normed_ref[...] = normed_rows(out.astype(f32), gain_ref[layer_no : layer_no + 1])


def end_kernel(earlier, current_ref, kept, *refs):
    sent, before, outs_ref = refs[: len(refs) - earlier - 1], refs[-earlier - 1 : -1], refs[-1]
    layers, batches, tokens, _ = outs_ref.shape
    done = [ref[...] for ref in before] + [total_rows(current_ref[...], kept, sent)]
    for layer_no in range(layers):
        for batch in range(batches):
            outs_ref[layer_no, batch] = done[layer_no][batch * tokens : (batch + 1) * tokens]


def load_kernel(layer_no, cuts, gate_up_hbm, down_hbm, gate_up_ref, down_ref, token, sems):
    token[...] = jnp.zeros_like(token)
    copies = []
    for source, target in ((gate_up_hbm, gate_up_ref), (down_hbm, down_ref)):
        rows = target.shape[0] // cuts
        for cut in range(cuts):
            span = pl.ds(cut * rows, rows)
            copies.append(
                pltpu.make_async_copy(
                    source.at[layer_no, 0, span], target.at[span], sems.at[len(copies)]
                )
            )
    for copy in copies:
        copy.start()
    for copy in copies:
        copy.wait()


def load_weights(layer_no, w_gate_up, w_down, after=()):
    cuts = 4
    return call(
        functools.partial(load_kernel, layer_no, cuts),
        [(w_gate_up.shape[2:], bf16), (w_down.shape[2:], bf16), ((8, LANES), f32)],
        [ANY] * 2,
        in_hbm(w_gate_up),
        in_hbm(w_down),
        scratch=[pltpu.SemaphoreType.DMA((2 * cuts,))],
        limit=12,
        after=after,
    )


def tile_of(extent, most):
    size = most
    while extent % size:
        size //= 2
    return size


def expert_kernel(count, first_column, wide, *refs):
    parts, refs = refs[:count], refs[count:]
    if wide:
        gate_up_ref, down_ref, *outs, routed_ref, rows_ref, hidden_ref = refs
    else:
        routed_ref, gate_up_ref, down_ref, *outs, rows_ref, hidden_ref = refs
    hidden_size, features = down_ref.shape
    first = 0
    for part in parts:
        span = slice(first, first + part.shape[0])
        first += part.shape[0]
        rows_ref[span] = part[:, :features]
        if wide:
            routed_ref[span] = part[:, features:]
    places = lax.broadcasted_iota(jnp.int32, routed_ref.shape, 1)
    column = first_column + lax.axis_index("expert")
    chosen = jnp.where(places == column, routed_ref[...].astype(f32), 0.0)
    share = jnp.sum(chosen, axis=1, keepdims=True)
    rows = rows_ref[...]
    size = tile_of(hidden_size, 256)
    for low in range(0, hidden_size, size):
        span, beside = slice(low, low + size), slice(hidden_size + low, hidden_size + low + size)
        gate = jnp.dot(rows, gate_up_ref[:, span], preferred_element_type=f32)
        up = jnp.dot(rows, gate_up_ref[:, beside], preferred_element_type=f32)
        hidden_ref[:, span] = (gate / (1.0 + jnp.exp(-gate)) * up).astype(bf16)
    hidden = hidden_ref[...]
    size = tile_of(features, 512)
    for low in range(0, features, size):
        span = slice(low, low + size)
        done = jnp.dot(hidden, down_ref[:, span], preferred_element_type=f32) * share
        first = 0
        for out in outs:
            out[:, span] = done[first : first + out.shape[0]].astype(out.dtype)
            first += out.shape[0]


def run_expert(parts, routed, first_column, weights, after):
    gate_up, down_proj, _ = weights
    hidden_size, features = down_proj.shape
    width = parts[0].shape[1]
    count = sum(part.shape[0] for part in parts)
    quarter = count // 4
    wide = routed is None
    outs = [((quarter, features), f32)] * 2 + [((quarter, features), bf16)]
    outs += [((quarter // CUTS, features), bf16)] * CUTS
    if wide:
        outs = outs + [((count, width - features), bf16)]
    found = call(
        functools.partial(expert_kernel, len(parts), first_column, wide),
        outs,
        [VMEM] * (len(parts) + (2 if wide else 3)),
        *parts,
        *([] if wide else [routed]),
        gate_up,
        down_proj,
        scratch=[pltpu.VMEM((count, features), bf16), pltpu.VMEM((count, hidden_size), bf16)],
        limit=24,
        after=after,
    )
    return found[: 3 + CUTS], found[3 + CUTS] if wide else routed


def in_hbm(array):
    return pltpu.with_memory_space_constraint(array, pltpu.HBM)


def open_rows(current, routes, gain, experts):
    batches, tokens, features = current.shape
    rows = batches * tokens
    columns = routes.shape[0] * experts
    width = features + columns + -columns % LANES
    current, routes = current.reshape(rows, features), jnp.swapaxes(routes, 2, 3)
    (wide,) = call(
        functools.partial(open_kernel, experts),
        [((rows, width), bf16)],
        [ANY] * 3,
        in_hbm(current),
        in_hbm(routes),
        in_hbm(gain),
        scratch=[
            pltpu.VMEM(current.shape, bf16),
            pltpu.VMEM(routes.shape, jnp.int32),
            pltpu.VMEM(gain.shape, f32),
            pltpu.SemaphoreType.DMA((3,)),
        ],
    )
    return wide


def run_layer(rows, routed, first_column, weights, loaded=()):
    far, tokens = lax.axis_size("expert") // 4, rows.shape[0]
    routed = routed or [None, None]
    half = far // 2
    sent = [rows] + [swap(rows, 4, k, far) for k in range(1, half)]
    first = join_rows(sent, loaded, 0)
    first_beside = swap(first, 2, 1, 2)
    crossed = join_rows([swap(rows, 4, half, far)], (first,), WAIT)
    second = [crossed] + [swap(crossed, 4, k, far) for k in range(1, half)]
    second_beside = [swap(crossed, 2, 1, 2)]
    for piece in second[1:]:
        second_beside.append(swap(held(piece, (second_beside[0], first_beside)), 2, 1, 2))

    def worked(near, beside, routed, after):
        parts = near + beside
        parts += [swap(piece, 1, 1, 2) for piece in parts]
        return run_expert(parts, routed, first_column, weights, after)

    outs, second_columns = worked(second, second_beside, routed[1], ())
    mine, near, leaving = leave_pair(outs, ())
    back = swap(leaving, 2, 1, 2, True)
    far_arrived, last = split_rows(mine, near, back, range(half, far), tokens)
    outs, first_columns = worked([first], [first_beside], routed[0], (leaving,))
    mine, near, leaving = leave_pair(outs, (last,))
    back = swap(leaving, 2, 1, 2, True)
    arrived, _ = split_rows(mine, near, back, range(half), tokens)
    return arrived + far_arrived, [first_columns, second_columns], (outs[0],)


def close_rows(layer_no, current, gain, returned, after=()):
    return call(
        functools.partial(close_kernel, layer_no),
        [(current.shape, bf16)] * 2,
        [VMEM] * (2 + len(returned)),
        current,
        gain,
        *returned,
        after=after,
    )


def on_device(inputs, routes, norm_gain, w_gate_up, w_down):
    experts = lax.axis_size("expert")
    sections = lax.axis_size("section")
    batches, tokens, features = inputs.shape
    layers = routes.shape[0]
    weights = load_weights(0, w_gate_up, w_down)
    if sections == 1:
        outs, routed = [], None
        current = inputs.reshape(batches * tokens, features)
        rows = open_rows(inputs, routes, norm_gain, experts)
        for layer_no in range(layers):
            returned, routed, worked = run_layer(
                rows, routed, layer_no * experts, weights, weights[2:]
            )
            if layer_no == layers - 1:
                (whole,) = call(
                    functools.partial(end_kernel, len(outs)),
                    [((layers, batches, tokens, features), bf16)],
                    [VMEM] * (1 + len(returned) + len(outs)),
                    current,
                    *returned,
                    *outs,
                )
                return whole
            weights = load_weights(layer_no + 1, w_gate_up, w_down, worked)
            current, rows = close_rows(layer_no + 1, current, norm_gain, returned, weights[2:])
            outs.append(current)
    segment_no = lax.axis_index("section")
    handed = jnp.zeros((tokens, features), bf16)
    finished = []
    for turn_no in range(batches + 1):
        if turn_no < batches:
            fresh_rows = inputs[turn_no]
        else:
            fresh_rows = jnp.zeros((tokens, features), bf16)
        current = jnp.where(segment_no == 0, fresh_rows, handed)
        batch_pick = jnp.clip(turn_no - segment_no, 0, batches - 1)
        turn_routes = lax.dynamic_slice_in_dim(routes, batch_pick, 1, 1)
        rows = open_rows(current[None], turn_routes, norm_gain, experts)
        returned, _, _ = run_layer(rows, None, 0, weights)
        result, _ = close_rows(0, current, norm_gain, returned)
        finished.append(result)
        if turn_no < batches:
            handed = from_behind(result, "section", 1)
    first_segment = jnp.stack(finished[:batches])
    second_segment = jnp.stack(finished[1:])
    return jnp.where(segment_no == 0, first_segment, second_segment)[None]


def solution(mesh):
    placed = (
        P(None, ("groups", "expert"), None),
        P("section", None, ("groups", "expert"), None),
        P("section", None),
        P("section", "expert", None, None),
        P("section", "expert", None, None),
    )
    return jax.shard_map(
        on_device,
        mesh=mesh,
        in_specs=placed,
        out_specs=P("section", None, ("groups", "expert"), None),
        check_vma=False,
    )
```

```python
import functools

import jax
import jax.numpy as jnp
from jax import lax
from jax.experimental import pallas as pl
from jax.experimental.pallas import tpu as pltpu
from jax.sharding import PartitionSpec as P

eps = 1e-06
LANES = 128
MIB = 2**20
WAIT = 6 * 10**9
VMEM = pl.BlockSpec(memory_space=pltpu.VMEM)
ANY = pl.BlockSpec(memory_space=pl.ANY)
bf16, f32 = jnp.bfloat16, jnp.float32


def from_behind(value, axis, steps):
    count = lax.axis_size(axis)
    initial, last = (max(0, -steps), min(count, count - steps))
    return lax.ppermute(value, axis, [(source, source + steps) for source in range(initial, last)])


def call(kernel, outs, specs, *operands, scratch=(), limit=8, after=(), weight=0):
    shapes = tuple(jax.ShapeDtypeStruct(shape, dtype) for shape, dtype in outs)
    operands = (*after, *operands)
    return pl.pallas_call(
        lambda *refs: kernel(*refs[len(after) :]),
        out_shape=shapes,
        in_specs=[ANY] * len(after) + specs,
        out_specs=(VMEM,) * len(outs),
        scratch_shapes=scratch,
        compiler_params=pltpu.CompilerParams(vmem_limit_bytes=limit * MIB),
        cost_estimate=pl.CostEstimate(flops=weight, bytes_accessed=0, transcendentals=0),
    )(*operands)


def swap(value, stride, step, radix, back=False):
    count = lax.axis_size("expert")

    def partner(index):
        digit = index // stride % radix
        if radix & (radix - 1) == 0:
            other = digit ^ step
        else:
            other = (digit + (step if back else radix - step)) % radix
        return index + (other - digit) * stride

    return lax.ppermute(value, "expert", [(i, partner(i)) for i in range(count)])


def join_kernel(*refs):
    *parts, whole = refs
    rows = parts[0].shape[0]
    for k, part in enumerate(parts):
        whole[k * rows : (k + 1) * rows] = part[...]


def join_rows(parts, after, weight):
    tokens, width = parts[0].shape
    return call(
        join_kernel,
        [((len(parts) * tokens, width), parts[0].dtype)],
        [VMEM] * len(parts),
        *parts,
        after=after,
        weight=weight,
    )[0]


def held(value, until):
    return lax.optimization_barrier((value, until))[0]


def sum_kernel(count, mine, *refs):
    parts, totals = refs[:count], refs[count:]
    size, rows = parts[0].shape[0], totals[0].shape[0]
    grain = min(size, rows)
    for low in range(0, mine.shape[0], grain):
        part, total = parts[low // size], totals[low // rows]
        inside = slice(low % size, low % size + grain)
        total[low % rows : low % rows + grain] = (
            mine[low : low + grain] + part[inside].astype(f32)
        ).astype(total.dtype)


def apart_kernel(first, count, mine, near, *refs):
    beside, pieces = refs[:count], refs[count:]
    rows = pieces[0].shape[0]
    for k in range(count):
        span = slice((first + k) * rows, (first + k + 1) * rows)
        total = mine[span] + near[span].astype(f32) + beside[k][...].astype(f32)
        pieces[k][...] = total.astype(pieces[k].dtype)


def cross_kernel(mine, near, beside, *refs):
    *arrived, out = refs
    rows = out.shape[0]
    total = mine[:rows] + near[:rows].astype(f32) + beside[...].astype(f32)
    for piece in arrived:
        total = total + piece[...].astype(f32)
    out[...] = total.astype(out.dtype)


def leave_pair(found, count, after):
    mine_near, mine_beside, other_near, *other_beside = found
    arrived_beside = [swap(half, 1, 1, 2, True) for half in other_beside]
    arrived_near = swap(other_near, 1, 1, 2, True)
    rows, width = mine_beside.shape
    leaving = call(
        functools.partial(sum_kernel, len(other_beside)),
        [((rows // count, width), bf16)] * count,
        [VMEM] * (1 + len(other_beside)),
        mine_beside,
        *arrived_beside,
        after=after,
    )
    return mine_near, arrived_near, leaving


def cross_rows(mine, near, beside):
    far, count = lax.axis_size("expert") // 4, len(beside)
    shape = beside[0].shape
    hops, arrived = [], []
    if count > 1:
        hops = call(
            functools.partial(apart_kernel, 1, count - 1),
            [(shape, bf16)] * (count - 1),
            [VMEM] * (count + 1),
            mine,
            near,
            *beside[1:],
        )
        arrived = [swap(piece, 4, k, far, True) for k, piece in enumerate(hops, 1)]
    (crossing,) = call(
        cross_kernel, [(shape, bf16)], [VMEM] * (3 + len(arrived)), mine, near, beside[0], *arrived
    )
    return swap(crossing, 4, count, far, True), tuple(hops[-1:])


def normed_rows(widened, gain_row):
    scale_inv = lax.rsqrt(jnp.mean(widened * widened, axis=-1, keepdims=True) + eps)
    return (widened * scale_inv * gain_row).astype(bf16)


def open_kernel(experts, current_hbm, routes_hbm, gain_hbm, wide_ref, current, routes, gain, sems):
    pairs = ((current_hbm, current), (routes_hbm, routes), (gain_hbm, gain))
    copies = [pltpu.make_async_copy(a, b, sems.at[k]) for k, (a, b) in enumerate(pairs)]
    for copy in copies:
        copy.start()
    for copy in copies:
        copy.wait()
    features = current.shape[-1]
    layers, batches, top, tokens = routes.shape
    columns = wide_ref.shape[1] - features
    wide_ref[:, :features] = normed_rows(current[...].astype(f32), gain[0:1])
    places = lax.broadcasted_iota(jnp.int32, (columns, tokens), 0)
    same = lax.broadcasted_iota(jnp.int32, (tokens, tokens), 0) == lax.broadcasted_iota(
        jnp.int32, (tokens, tokens), 1
    )
    for batch in range(batches):
        chosen = jnp.zeros(places.shape, f32)
        for layer_no in range(layers):
            named = routes[layer_no, batch] + layer_no * experts
            for k in range(top):
                chosen = jnp.where(places == named[k : k + 1], 1.0, chosen)
        turned = lax.dot_general(
            same.astype(bf16),
            chosen.astype(bf16),
            (((1,), (1,)), ((), ())),
            preferred_element_type=f32,
        )
        wide_ref[batch * tokens : (batch + 1) * tokens, features:] = turned.astype(bf16)


def total_rows(current, kept, sent):
    total = kept[...]
    for piece in sent:
        total = total + piece[...].astype(f32)
    return (current.astype(f32) + total * 0.125).astype(bf16)


def close_kernel(layer_no, current_ref, gain_ref, kept, *refs):
    *sent, out_ref, normed_ref = refs
    out = total_rows(current_ref[...], kept, sent)
    out_ref[...] = out
    normed_ref[...] = normed_rows(out.astype(f32), gain_ref[layer_no : layer_no + 1])


def end_kernel(earlier, current_ref, kept, *refs):
    sent, before, outs_ref = refs[: len(refs) - earlier - 1], refs[-earlier - 1 : -1], refs[-1]
    layers, batches, tokens, _ = outs_ref.shape
    done = [ref[...] for ref in before] + [total_rows(current_ref[...], kept, sent)]
    for layer_no in range(layers):
        for batch in range(batches):
            outs_ref[layer_no, batch] = done[layer_no][batch * tokens : (batch + 1) * tokens]


def load_kernel(layer_no, cuts, gate_up_hbm, down_hbm, gate_up_ref, down_ref, token, sems):
    token[...] = jnp.zeros_like(token)
    copies = []
    for source, target in ((gate_up_hbm, gate_up_ref), (down_hbm, down_ref)):
        rows = target.shape[0] // cuts
        for cut in range(cuts):
            span = pl.ds(cut * rows, rows)
            copies.append(
                pltpu.make_async_copy(
                    source.at[layer_no, 0, span], target.at[span], sems.at[len(copies)]
                )
            )
    for copy in copies:
        copy.start()
    for copy in copies:
        copy.wait()


def load_weights(layer_no, w_gate_up, w_down, after=()):
    cuts = 4
    return call(
        functools.partial(load_kernel, layer_no, cuts),
        [(w_gate_up.shape[2:], bf16), (w_down.shape[2:], bf16), ((8, LANES), f32)],
        [ANY] * 2,
        in_hbm(w_gate_up),
        in_hbm(w_down),
        scratch=[pltpu.SemaphoreType.DMA((2 * cuts,))],
        limit=12,
        after=after,
    )


def tile_of(extent, most):
    size = most
    while extent % size:
        size //= 2
    return size


def expert_kernel(count, first_column, wide, *refs):
    parts, refs = refs[:count], refs[count:]
    if wide:
        gate_up_ref, down_ref, *outs, routed_ref, rows_ref, hidden_ref = refs
    else:
        routed_ref, gate_up_ref, down_ref, *outs, rows_ref, hidden_ref = refs
    hidden_size, features = down_ref.shape
    first = 0
    for part in parts:
        span = slice(first, first + part.shape[0])
        first += part.shape[0]
        rows_ref[span] = part[:, :features]
        if wide:
            routed_ref[span] = part[:, features:]
    places = lax.broadcasted_iota(jnp.int32, routed_ref.shape, 1)
    column = first_column + lax.axis_index("expert")
    chosen = jnp.where(places == column, routed_ref[...].astype(f32), 0.0)
    share = jnp.sum(chosen, axis=1, keepdims=True)
    rows = rows_ref[...]
    size = tile_of(hidden_size, 256)
    for low in range(0, hidden_size, size):
        span, beside = slice(low, low + size), slice(hidden_size + low, hidden_size + low + size)
        gate = jnp.dot(rows, gate_up_ref[:, span], preferred_element_type=f32)
        up = jnp.dot(rows, gate_up_ref[:, beside], preferred_element_type=f32)
        hidden_ref[:, span] = (gate / (1.0 + jnp.exp(-gate)) * up).astype(bf16)
    hidden = hidden_ref[...]
    size = tile_of(features, 512)
    for low in range(0, features, size):
        span = slice(low, low + size)
        done = jnp.dot(hidden, down_ref[:, span], preferred_element_type=f32) * share
        first = 0
        for out in outs:
            out[:, span] = done[first : first + out.shape[0]].astype(out.dtype)
            first += out.shape[0]


def run_expert(parts, routed, first_column, weights, cuts, after):
    gate_up, down_proj, _ = weights
    hidden_size, features = down_proj.shape
    width = parts[0].shape[1]
    count = sum(part.shape[0] for part in parts)
    quarter = count // 4
    wide = routed is None
    outs = [((quarter, features), f32)] * 2 + [((quarter, features), bf16)]
    outs += [((quarter // cuts, features), bf16)] * cuts
    if wide:
        outs = outs + [((count, width - features), bf16)]
    found = call(
        functools.partial(expert_kernel, len(parts), first_column, wide),
        outs,
        [VMEM] * (len(parts) + (2 if wide else 3)),
        *parts,
        *([] if wide else [routed]),
        gate_up,
        down_proj,
        scratch=[pltpu.VMEM((count, features), bf16), pltpu.VMEM((count, hidden_size), bf16)],
        limit=24,
        after=after,
    )
    return found[: 3 + cuts], found[3 + cuts] if wide else routed


def in_hbm(array):
    return pltpu.with_memory_space_constraint(array, pltpu.HBM)


def open_rows(current, routes, gain, experts):
    batches, tokens, features = current.shape
    rows = batches * tokens
    columns = routes.shape[0] * experts
    width = features + columns + -columns % LANES
    current, routes = current.reshape(rows, features), jnp.swapaxes(routes, 2, 3)
    (wide,) = call(
        functools.partial(open_kernel, experts),
        [((rows, width), bf16)],
        [ANY] * 3,
        in_hbm(current),
        in_hbm(routes),
        in_hbm(gain),
        scratch=[
            pltpu.VMEM(current.shape, bf16),
            pltpu.VMEM(routes.shape, jnp.int32),
            pltpu.VMEM(gain.shape, f32),
            pltpu.SemaphoreType.DMA((3,)),
        ],
    )
    return wide


def run_layer(rows, routed, first_column, weights, loaded=()):
    far = lax.axis_size("expert") // 4
    routed = routed or [None, None]
    half = far // 2
    sent = [rows] + [swap(rows, 4, k, far) for k in range(1, half)]
    first = join_rows(sent, loaded, 0)
    first_beside = swap(first, 2, 1, 2)
    crossed = join_rows([swap(rows, 4, half, far)], (first,), WAIT)
    second = [crossed] + [swap(crossed, 4, k, far) for k in range(1, half)]
    second_beside = [swap(crossed, 2, 1, 2)]
    for piece in second[1:]:
        second_beside.append(swap(held(piece, (second_beside[0], first_beside)), 2, 1, 2))

    def worked(near, beside, routed, cuts, after):
        parts = near + beside
        parts += [swap(piece, 1, 1, 2) for piece in parts]
        return run_expert(parts, routed, first_column, weights, cuts, after)

    outs, second_columns = worked(second, second_beside, routed[1], 2, ())
    mine, near, leaving = leave_pair(outs, half, ())
    back = [swap(piece, 2, 1, 2, True) for piece in leaving]
    crossed_back, hopped = cross_rows(mine, near, back)
    outs, first_columns = worked([first], [first_beside], routed[0], 4, tuple(leaving[-1:]))
    mine, near, leaving = leave_pair(outs, half, (*hopped, back[0]))
    back = [swap(piece, 2, 1, 2, True) for piece in leaving]
    pieces = call(
        functools.partial(apart_kernel, 0, half),
        [(rows.shape[:1] + mine.shape[1:], bf16 if k else f32) for k in range(half)],
        [VMEM] * (2 + half),
        mine,
        near,
        *back,
    )
    arrived = [swap(piece, 4, k, far, True) if k else piece for k, piece in enumerate(pieces)]
    return [*arrived, crossed_back], [first_columns, second_columns], (outs[0],)


def close_rows(layer_no, current, gain, returned, after=()):
    return call(
        functools.partial(close_kernel, layer_no),
        [(current.shape, bf16)] * 2,
        [VMEM] * (2 + len(returned)),
        current,
        gain,
        *returned,
        after=after,
    )


def on_device(inputs, routes, norm_gain, w_gate_up, w_down):
    experts = lax.axis_size("expert")
    sections = lax.axis_size("section")
    batches, tokens, features = inputs.shape
    layers = routes.shape[0]
    weights = load_weights(0, w_gate_up, w_down)
    if sections == 1:
        outs, routed = [], None
        current = inputs.reshape(batches * tokens, features)
        rows = open_rows(inputs, routes, norm_gain, experts)
        for layer_no in range(layers):
            returned, routed, worked = run_layer(
                rows, routed, layer_no * experts, weights, weights[2:]
            )
            if layer_no == layers - 1:
                (whole,) = call(
                    functools.partial(end_kernel, len(outs)),
                    [((layers, batches, tokens, features), bf16)],
                    [VMEM] * (1 + len(returned) + len(outs)),
                    current,
                    *returned,
                    *outs,
                )
                return whole
            weights = load_weights(layer_no + 1, w_gate_up, w_down, worked)
            current, rows = close_rows(layer_no + 1, current, norm_gain, returned, weights[2:])
            outs.append(current)
    segment_no = lax.axis_index("section")
    handed = jnp.zeros((tokens, features), bf16)
    finished = []
    for turn_no in range(batches + 1):
        if turn_no < batches:
            fresh_rows = inputs[turn_no]
        else:
            fresh_rows = jnp.zeros((tokens, features), bf16)
        current = jnp.where(segment_no == 0, fresh_rows, handed)
        batch_pick = jnp.clip(turn_no - segment_no, 0, batches - 1)
        turn_routes = lax.dynamic_slice_in_dim(routes, batch_pick, 1, 1)
        rows = open_rows(current[None], turn_routes, norm_gain, experts)
        returned, _, _ = run_layer(rows, None, 0, weights)
        result, _ = close_rows(0, current, norm_gain, returned)
        finished.append(result)
        if turn_no < batches:
            handed = from_behind(result, "section", 1)
    first_segment = jnp.stack(finished[:batches])
    second_segment = jnp.stack(finished[1:])
    return jnp.where(segment_no == 0, first_segment, second_segment)[None]


def solution(mesh):
    placed = (
        P(None, ("groups", "expert"), None),
        P("section", None, ("groups", "expert"), None),
        P("section", None),
        P("section", "expert", None, None),
        P("section", "expert", None, None),
    )
    return jax.shard_map(
        on_device,
        mesh=mesh,
        in_specs=placed,
        out_specs=P("section", None, ("groups", "expert"), None),
        check_vma=False,
    )
```

```python
import functools

import jax
import jax.numpy as jnp
from jax import lax
from jax.experimental import pallas as pl
from jax.experimental.pallas import tpu as pltpu
from jax.sharding import PartitionSpec as P

eps = 1e-06
LANES = 128
MIB = 2**20
WAIT = 6 * 10**9
VMEM = pl.BlockSpec(memory_space=pltpu.VMEM)
ANY = pl.BlockSpec(memory_space=pl.ANY)
bf16, f32 = jnp.bfloat16, jnp.float32


def from_behind(value, axis, steps):
    count = lax.axis_size(axis)
    initial, last = (max(0, -steps), min(count, count - steps))
    return lax.ppermute(value, axis, [(source, source + steps) for source in range(initial, last)])


def call(kernel, outs, specs, *operands, scratch=(), limit=8, after=(), weight=0):
    shapes = tuple(jax.ShapeDtypeStruct(shape, dtype) for shape, dtype in outs)
    operands = (*after, *operands)
    return pl.pallas_call(
        lambda *refs: kernel(*refs[len(after) :]),
        out_shape=shapes,
        in_specs=[ANY] * len(after) + specs,
        out_specs=(VMEM,) * len(outs),
        scratch_shapes=scratch,
        compiler_params=pltpu.CompilerParams(vmem_limit_bytes=limit * MIB),
        cost_estimate=pl.CostEstimate(flops=weight, bytes_accessed=0, transcendentals=0),
    )(*operands)


def swap(value, stride, step, radix, back=False):
    count = lax.axis_size("expert")

    def partner(index):
        digit = index // stride % radix
        if radix & (radix - 1) == 0:
            other = digit ^ step
        else:
            other = (digit + (step if back else radix - step)) % radix
        return index + (other - digit) * stride

    return lax.ppermute(value, "expert", [(i, partner(i)) for i in range(count)])


def join_kernel(*refs):
    *parts, whole = refs
    rows = parts[0].shape[0]
    for k, part in enumerate(parts):
        whole[k * rows : (k + 1) * rows] = part[...]


def join_rows(parts, after, weight):
    tokens, width = parts[0].shape
    return call(
        join_kernel,
        [((len(parts) * tokens, width), parts[0].dtype)],
        [VMEM] * len(parts),
        *parts,
        after=after,
        weight=weight,
    )[0]


def held(value, until):
    return lax.optimization_barrier((value, until))[0]


def sum_kernel(count, mine, *refs):
    parts, totals = refs[:count], refs[count:]
    size, rows = parts[0].shape[0], totals[0].shape[0]
    grain = min(size, rows)
    for low in range(0, mine.shape[0], grain):
        part, total = parts[low // size], totals[low // rows]
        inside = slice(low % size, low % size + grain)
        total[low % rows : low % rows + grain] = (
            mine[low : low + grain] + part[inside].astype(f32)
        ).astype(total.dtype)


def apart_kernel(first, count, mine, near, *refs):
    beside, pieces = refs[:-count], refs[-count:]
    rows = pieces[0].shape[0]
    for k, piece in enumerate(pieces):
        span = slice((first + k) * rows, (first + k + 1) * rows)
        part = beside[k][...] if len(beside) == count else beside[0][span]
        total = mine[span] + near[span].astype(f32) + part.astype(f32)
        piece[...] = total.astype(piece.dtype)


def cross_kernel(mine, near, beside, *refs):
    *arrived, out = refs
    rows = out.shape[0]
    total = mine[:rows] + near[:rows].astype(f32) + beside[...].astype(f32)
    for piece in arrived:
        total = total + piece[...].astype(f32)
    out[...] = total.astype(out.dtype)


def leave_pair(found, count, after):
    mine_near, mine_beside, other_near, *other_beside = found
    arrived_beside = [swap(half, 1, 1, 2, True) for half in other_beside]
    arrived_near = swap(other_near, 1, 1, 2, True)
    rows, width = mine_beside.shape
    leaving = call(
        functools.partial(sum_kernel, len(other_beside)),
        [((rows // count, width), bf16)] * count,
        [VMEM] * (1 + len(other_beside)),
        mine_beside,
        *arrived_beside,
        after=after,
    )
    return mine_near, arrived_near, leaving


def cross_rows(mine, near, beside):
    far, count = lax.axis_size("expert") // 4, len(beside)
    shape = beside[0].shape
    arrived = []
    if count > 1:
        hops = call(
            functools.partial(apart_kernel, 1, count - 1),
            [(shape, bf16)] * (count - 1),
            [VMEM] * (count + 1),
            mine,
            near,
            *beside[1:],
        )
        arrived = [swap(piece, 4, k, far, True) for k, piece in enumerate(hops, 1)]
    (crossing,) = call(
        cross_kernel, [(shape, bf16)], [VMEM] * (3 + len(arrived)), mine, near, beside[0], *arrived
    )
    return swap(crossing, 4, count, far, True)


def normed_rows(widened, gain_row):
    scale_inv = lax.rsqrt(jnp.mean(widened * widened, axis=-1, keepdims=True) + eps)
    return (widened * scale_inv * gain_row).astype(bf16)


def open_kernel(experts, current_hbm, routes_hbm, gain_hbm, wide_ref, current, routes, gain, sems):
    pairs = ((current_hbm, current), (routes_hbm, routes), (gain_hbm, gain))
    copies = [pltpu.make_async_copy(a, b, sems.at[k]) for k, (a, b) in enumerate(pairs)]
    for copy in copies:
        copy.start()
    for copy in copies:
        copy.wait()
    features = current.shape[-1]
    layers, batches, top, tokens = routes.shape
    columns = wide_ref.shape[1] - features
    wide_ref[:, :features] = normed_rows(current[...].astype(f32), gain[0:1])
    places = lax.broadcasted_iota(jnp.int32, (columns, tokens), 0)
    same = lax.broadcasted_iota(jnp.int32, (tokens, tokens), 0) == lax.broadcasted_iota(
        jnp.int32, (tokens, tokens), 1
    )
    for batch in range(batches):
        chosen = jnp.zeros(places.shape, f32)
        for layer_no in range(layers):
            named = routes[layer_no, batch] + layer_no * experts
            for k in range(top):
                chosen = jnp.where(places == named[k : k + 1], 1.0, chosen)
        turned = lax.dot_general(
            same.astype(bf16),
            chosen.astype(bf16),
            (((1,), (1,)), ((), ())),
            preferred_element_type=f32,
        )
        wide_ref[batch * tokens : (batch + 1) * tokens, features:] = turned.astype(bf16)


def total_rows(current, kept, sent):
    total = kept[...]
    for piece in sent:
        total = total + piece[...].astype(f32)
    return (current.astype(f32) + total * 0.125).astype(bf16)


def close_kernel(layer_no, current_ref, gain_ref, kept, *refs):
    *sent, out_ref, normed_ref = refs
    out = total_rows(current_ref[...], kept, sent)
    out_ref[...] = out
    normed_ref[...] = normed_rows(out.astype(f32), gain_ref[layer_no : layer_no + 1])


def end_kernel(earlier, current_ref, kept, *refs):
    sent, before, outs_ref = refs[: len(refs) - earlier - 1], refs[-earlier - 1 : -1], refs[-1]
    layers, batches, tokens, _ = outs_ref.shape
    done = [ref[...] for ref in before] + [total_rows(current_ref[...], kept, sent)]
    for layer_no in range(layers):
        for batch in range(batches):
            outs_ref[layer_no, batch] = done[layer_no][batch * tokens : (batch + 1) * tokens]


def load_kernel(layer_no, cuts, gate_up_hbm, down_hbm, gate_up_ref, down_ref, token, sems):
    token[...] = jnp.zeros_like(token)
    copies = []
    for source, target in ((gate_up_hbm, gate_up_ref), (down_hbm, down_ref)):
        rows = target.shape[0] // cuts
        for cut in range(cuts):
            span = pl.ds(cut * rows, rows)
            copies.append(
                pltpu.make_async_copy(
                    source.at[layer_no, 0, span], target.at[span], sems.at[len(copies)]
                )
            )
    for copy in copies:
        copy.start()
    for copy in copies:
        copy.wait()


def load_weights(layer_no, w_gate_up, w_down, after=()):
    cuts = 4
    return call(
        functools.partial(load_kernel, layer_no, cuts),
        [(w_gate_up.shape[2:], bf16), (w_down.shape[2:], bf16), ((8, LANES), f32)],
        [ANY] * 2,
        in_hbm(w_gate_up),
        in_hbm(w_down),
        scratch=[pltpu.SemaphoreType.DMA((2 * cuts,))],
        limit=12,
        after=after,
    )


def tile_of(extent, most):
    size = most
    while extent % size:
        size //= 2
    return size


def expert_kernel(count, first_column, wide, *refs):
    parts, refs = refs[:count], refs[count:]
    if wide:
        gate_up_ref, down_ref, *outs, routed_ref, rows_ref, hidden_ref = refs
    else:
        routed_ref, gate_up_ref, down_ref, *outs, rows_ref, hidden_ref = refs
    hidden_size, features = down_ref.shape
    first = 0
    for part in parts:
        span = slice(first, first + part.shape[0])
        first += part.shape[0]
        rows_ref[span] = part[:, :features]
        if wide:
            routed_ref[span] = part[:, features:]
    places = lax.broadcasted_iota(jnp.int32, routed_ref.shape, 1)
    column = first_column + lax.axis_index("expert")
    chosen = jnp.where(places == column, routed_ref[...].astype(f32), 0.0)
    share = jnp.sum(chosen, axis=1, keepdims=True)
    rows = rows_ref[...]
    size = tile_of(hidden_size, 256)
    for low in range(0, hidden_size, size):
        span, beside = slice(low, low + size), slice(hidden_size + low, hidden_size + low + size)
        gate = jnp.dot(rows, gate_up_ref[:, span], preferred_element_type=f32)
        up = jnp.dot(rows, gate_up_ref[:, beside], preferred_element_type=f32)
        hidden_ref[:, span] = (gate / (1.0 + jnp.exp(-gate)) * up).astype(bf16)
    hidden = hidden_ref[...]
    size = tile_of(features, 512)
    for low in range(0, features, size):
        span = slice(low, low + size)
        done = jnp.dot(hidden, down_ref[:, span], preferred_element_type=f32) * share
        first = 0
        for out in outs:
            out[:, span] = done[first : first + out.shape[0]].astype(out.dtype)
            first += out.shape[0]


def run_expert(parts, routed, first_column, weights, after):
    gate_up, down_proj, _ = weights
    hidden_size, features = down_proj.shape
    width = parts[0].shape[1]
    count = sum(part.shape[0] for part in parts)
    quarter = count // 4
    wide = routed is None
    outs = [((quarter, features), f32)] * 2 + [((quarter, features), bf16)]
    outs += [((quarter // 2, features), bf16)] * 2
    if wide:
        outs = outs + [((count, width - features), bf16)]
    found = call(
        functools.partial(expert_kernel, len(parts), first_column, wide),
        outs,
        [VMEM] * (len(parts) + (2 if wide else 3)),
        *parts,
        *([] if wide else [routed]),
        gate_up,
        down_proj,
        scratch=[pltpu.VMEM((count, features), bf16), pltpu.VMEM((count, hidden_size), bf16)],
        limit=24,
        after=after,
    )
    return found[:5], found[5] if wide else routed


def in_hbm(array):
    return pltpu.with_memory_space_constraint(array, pltpu.HBM)


def open_rows(current, routes, gain, experts):
    batches, tokens, features = current.shape
    rows = batches * tokens
    columns = routes.shape[0] * experts
    width = features + columns + -columns % LANES
    current, routes = current.reshape(rows, features), jnp.swapaxes(routes, 2, 3)
    (wide,) = call(
        functools.partial(open_kernel, experts),
        [((rows, width), bf16)],
        [ANY] * 3,
        in_hbm(current),
        in_hbm(routes),
        in_hbm(gain),
        scratch=[
            pltpu.VMEM(current.shape, bf16),
            pltpu.VMEM(routes.shape, jnp.int32),
            pltpu.VMEM(gain.shape, f32),
            pltpu.SemaphoreType.DMA((3,)),
        ],
    )
    return wide


def run_layer(rows, routed, first_column, weights, loaded=()):
    far = lax.axis_size("expert") // 4
    routed = routed or [None, None]
    half = far // 2
    sent = [rows] + [swap(rows, 4, k, far) for k in range(1, half)]
    first = join_rows(sent, loaded, 0)
    first_beside = swap(first, 2, 1, 2)
    crossed = join_rows([swap(rows, 4, half, far)], (first,), WAIT)
    second = [crossed] + [swap(crossed, 4, k, far) for k in range(1, half)]
    second_beside = [swap(crossed, 2, 1, 2)]
    for piece in second[1:]:
        second_beside.append(swap(held(piece, (second_beside[0], first_beside)), 2, 1, 2))

    def worked(near, beside, routed, after):
        parts = near + beside
        parts += [swap(piece, 1, 1, 2) for piece in parts]
        return run_expert(parts, routed, first_column, weights, after)

    first_beside = held(first_beside, (second[-1], second_beside[0]))
    outs, first_columns = worked([first], [first_beside], routed[0], (second[-1],))
    mine1, near1, leaving1 = leave_pair(outs, 1, ())
    second_beside[-1] = held(second_beside[-1], outs[0])
    outs, second_columns = worked(second, second_beside, routed[1], tuple(leaving1))
    mine2, near2, leaving2 = leave_pair(outs, half, ())
    back2 = [swap(piece, 2, 1, 2, True) for piece in leaving2]
    back1 = [swap(held(piece, back2[0]), 2, 1, 2, True) for piece in leaving1]
    crossed_back = cross_rows(mine2, near2, back2)
    pieces = call(
        functools.partial(apart_kernel, 0, half),
        [(rows.shape[:1] + mine1.shape[1:], bf16 if k else f32) for k in range(half)],
        [VMEM] * (2 + len(back1)),
        mine1,
        near1,
        *back1,
        after=tuple(leaving2),
    )
    arrived = [swap(piece, 4, k, far, True) if k else piece for k, piece in enumerate(pieces)]
    return [*arrived, crossed_back], [first_columns, second_columns], (outs[0],)


def close_rows(layer_no, current, gain, returned, after=()):
    return call(
        functools.partial(close_kernel, layer_no),
        [(current.shape, bf16)] * 2,
        [VMEM] * (2 + len(returned)),
        current,
        gain,
        *returned,
        after=after,
    )


def on_device(inputs, routes, norm_gain, w_gate_up, w_down):
    experts = lax.axis_size("expert")
    sections = lax.axis_size("section")
    batches, tokens, features = inputs.shape
    layers = routes.shape[0]
    weights = load_weights(0, w_gate_up, w_down)
    if sections == 1:
        outs, routed = [], None
        current = inputs.reshape(batches * tokens, features)
        rows = open_rows(inputs, routes, norm_gain, experts)
        for layer_no in range(layers):
            returned, routed, worked = run_layer(
                rows, routed, layer_no * experts, weights, weights[2:]
            )
            if layer_no == layers - 1:
                (whole,) = call(
                    functools.partial(end_kernel, len(outs)),
                    [((layers, batches, tokens, features), bf16)],
                    [VMEM] * (1 + len(returned) + len(outs)),
                    current,
                    *returned,
                    *outs,
                )
                return whole
            weights = load_weights(layer_no + 1, w_gate_up, w_down, worked)
            current, rows = close_rows(layer_no + 1, current, norm_gain, returned, weights[2:])
            outs.append(current)
    segment_no = lax.axis_index("section")
    handed = jnp.zeros((tokens, features), bf16)
    finished = []
    for turn_no in range(batches + 1):
        if turn_no < batches:
            fresh_rows = inputs[turn_no]
        else:
            fresh_rows = jnp.zeros((tokens, features), bf16)
        current = jnp.where(segment_no == 0, fresh_rows, handed)
        batch_pick = jnp.clip(turn_no - segment_no, 0, batches - 1)
        turn_routes = lax.dynamic_slice_in_dim(routes, batch_pick, 1, 1)
        rows = open_rows(current[None], turn_routes, norm_gain, experts)
        returned, _, _ = run_layer(rows, None, 0, weights)
        result, _ = close_rows(0, current, norm_gain, returned)
        finished.append(result)
        if turn_no < batches:
            handed = from_behind(result, "section", 1)
    first_segment = jnp.stack(finished[:batches])
    second_segment = jnp.stack(finished[1:])
    return jnp.where(segment_no == 0, first_segment, second_segment)[None]


def solution(mesh):
    placed = (
        P(None, ("groups", "expert"), None),
        P("section", None, ("groups", "expert"), None),
        P("section", None),
        P("section", "expert", None, None),
        P("section", "expert", None, None),
    )
    return jax.shard_map(
        on_device,
        mesh=mesh,
        in_specs=placed,
        out_specs=P("section", None, ("groups", "expert"), None),
        check_vma=False,
    )
```

```python
import functools

import jax
import jax.numpy as jnp
from jax import lax
from jax.experimental import pallas as pl
from jax.experimental.pallas import tpu as pltpu
from jax.sharding import PartitionSpec as P

eps = 1e-06
LANES = 128
MIB = 2**20
WAIT = 6 * 10**9
VMEM = pl.BlockSpec(memory_space=pltpu.VMEM)
ANY = pl.BlockSpec(memory_space=pl.ANY)
bf16, f32 = jnp.bfloat16, jnp.float32


def from_behind(value, axis, steps):
    count = lax.axis_size(axis)
    initial, last = (max(0, -steps), min(count, count - steps))
    return lax.ppermute(value, axis, [(source, source + steps) for source in range(initial, last)])


def call(kernel, outs, specs, *operands, scratch=(), limit=8, after=(), weight=0):
    shapes = tuple(jax.ShapeDtypeStruct(shape, dtype) for shape, dtype in outs)
    operands = (*after, *operands)
    return pl.pallas_call(
        lambda *refs: kernel(*refs[len(after) :]),
        out_shape=shapes,
        in_specs=[ANY] * len(after) + specs,
        out_specs=(VMEM,) * len(outs),
        scratch_shapes=scratch,
        compiler_params=pltpu.CompilerParams(vmem_limit_bytes=limit * MIB),
        cost_estimate=pl.CostEstimate(flops=weight, bytes_accessed=0, transcendentals=0),
    )(*operands)


def swap(value, stride, step, radix, back=False):
    count = lax.axis_size("expert")

    def partner(index):
        digit = index // stride % radix
        if radix & (radix - 1) == 0:
            other = digit ^ step
        else:
            other = (digit + (step if back else radix - step)) % radix
        return index + (other - digit) * stride

    return lax.ppermute(value, "expert", [(i, partner(i)) for i in range(count)])


def join_kernel(*refs):
    *parts, whole = refs
    rows = parts[0].shape[0]
    for k, part in enumerate(parts):
        whole[k * rows : (k + 1) * rows] = part[...]


def join_rows(parts, after, weight):
    tokens, width = parts[0].shape
    return call(
        join_kernel,
        [((len(parts) * tokens, width), parts[0].dtype)],
        [VMEM] * len(parts),
        *parts,
        after=after,
        weight=weight,
    )[0]


def held(value, until):
    return lax.optimization_barrier((value, until))[0]


def sum_kernel(count, mine, *refs):
    parts, totals = refs[:count], refs[count:]
    size, rows = parts[0].shape[0], totals[0].shape[0]
    grain = min(size, rows)
    for low in range(0, mine.shape[0], grain):
        part, total = parts[low // size], totals[low // rows]
        inside = slice(low % size, low % size + grain)
        total[low % rows : low % rows + grain] = (
            mine[low : low + grain] + part[inside].astype(f32)
        ).astype(total.dtype)


def apart_kernel(first, count, mine, near, *refs):
    beside, pieces = refs[:-count], refs[-count:]
    rows = pieces[0].shape[0]
    for k, piece in enumerate(pieces):
        span = slice((first + k) * rows, (first + k + 1) * rows)
        part = beside[k][...] if beside[0].shape[0] == rows else beside[0][span]
        total = mine[span] + near[span].astype(f32) + part.astype(f32)
        piece[...] = total.astype(piece.dtype)


def cross_kernel(mine, near, beside, *refs):
    *arrived, out = refs
    rows = out.shape[0]
    total = mine[:rows] + near[:rows].astype(f32) + beside[:rows].astype(f32)
    for piece in arrived:
        total = total + piece[...].astype(f32)
    out[...] = total.astype(out.dtype)


def leave_pair(found, count, after):
    mine_near, mine_beside, other_near, *other_beside = found
    arrived_beside = [swap(half, 1, 1, 2, True) for half in other_beside]
    arrived_near = swap(other_near, 1, 1, 2, True)
    rows, width = mine_beside.shape
    leaving = call(
        functools.partial(sum_kernel, len(other_beside)),
        [((rows // count, width), bf16)] * count,
        [VMEM] * (1 + len(other_beside)),
        mine_beside,
        *arrived_beside,
        after=after,
    )
    return mine_near, arrived_near, leaving


def cross_rows(mine, near, beside, count):
    far = lax.axis_size("expert") // 4
    shape = (mine.shape[0] // count, mine.shape[1])
    arrived = []
    if count > 1:
        hops = call(
            functools.partial(apart_kernel, 1, count - 1),
            [(shape, bf16)] * (count - 1),
            [VMEM] * 3,
            mine,
            near,
            beside,
        )
        arrived = [swap(piece, 4, k, far, True) for k, piece in enumerate(hops, 1)]
    (crossing,) = call(
        cross_kernel, [(shape, bf16)], [VMEM] * (3 + len(arrived)), mine, near, beside, *arrived
    )
    return swap(crossing, 4, count, far, True)


def normed_rows(widened, gain_row):
    scale_inv = lax.rsqrt(jnp.mean(widened * widened, axis=-1, keepdims=True) + eps)
    return (widened * scale_inv * gain_row).astype(bf16)


def open_kernel(experts, current_hbm, routes_hbm, gain_hbm, wide_ref, current, routes, gain, sems):
    pairs = ((current_hbm, current), (routes_hbm, routes), (gain_hbm, gain))
    copies = [pltpu.make_async_copy(a, b, sems.at[k]) for k, (a, b) in enumerate(pairs)]
    for copy in copies:
        copy.start()
    for copy in copies:
        copy.wait()
    features = current.shape[-1]
    layers, batches, top, tokens = routes.shape
    columns = wide_ref.shape[1] - features
    wide_ref[:, :features] = normed_rows(current[...].astype(f32), gain[0:1])
    places = lax.broadcasted_iota(jnp.int32, (columns, tokens), 0)
    same = lax.broadcasted_iota(jnp.int32, (tokens, tokens), 0) == lax.broadcasted_iota(
        jnp.int32, (tokens, tokens), 1
    )
    for batch in range(batches):
        chosen = jnp.zeros(places.shape, f32)
        for layer_no in range(layers):
            named = routes[layer_no, batch] + layer_no * experts
            for k in range(top):
                chosen = jnp.where(places == named[k : k + 1], 1.0, chosen)
        turned = lax.dot_general(
            same.astype(bf16),
            chosen.astype(bf16),
            (((1,), (1,)), ((), ())),
            preferred_element_type=f32,
        )
        wide_ref[batch * tokens : (batch + 1) * tokens, features:] = turned.astype(bf16)


def total_rows(current, kept, sent):
    total = kept[...]
    for piece in sent:
        total = total + piece[...].astype(f32)
    return (current.astype(f32) + total * 0.125).astype(bf16)


def close_kernel(layer_no, current_ref, gain_ref, kept, *refs):
    *sent, out_ref, normed_ref = refs
    out = total_rows(current_ref[...], kept, sent)
    out_ref[...] = out
    normed_ref[...] = normed_rows(out.astype(f32), gain_ref[layer_no : layer_no + 1])


def end_kernel(earlier, current_ref, kept, *refs):
    sent, before, outs_ref = refs[: len(refs) - earlier - 1], refs[-earlier - 1 : -1], refs[-1]
    layers, batches, tokens, _ = outs_ref.shape
    done = [ref[...] for ref in before] + [total_rows(current_ref[...], kept, sent)]
    for layer_no in range(layers):
        for batch in range(batches):
            outs_ref[layer_no, batch] = done[layer_no][batch * tokens : (batch + 1) * tokens]


def load_kernel(layer_no, cuts, gate_up_hbm, down_hbm, gate_up_ref, down_ref, token, sems):
    token[...] = jnp.zeros_like(token)
    copies = []
    for source, target in ((gate_up_hbm, gate_up_ref), (down_hbm, down_ref)):
        rows = target.shape[0] // cuts
        for cut in range(cuts):
            span = pl.ds(cut * rows, rows)
            copies.append(
                pltpu.make_async_copy(
                    source.at[layer_no, 0, span], target.at[span], sems.at[len(copies)]
                )
            )
    for copy in copies:
        copy.start()
    for copy in copies:
        copy.wait()


def load_weights(layer_no, w_gate_up, w_down, after=()):
    cuts = 4
    return call(
        functools.partial(load_kernel, layer_no, cuts),
        [(w_gate_up.shape[2:], bf16), (w_down.shape[2:], bf16), ((8, LANES), f32)],
        [ANY] * 2,
        in_hbm(w_gate_up),
        in_hbm(w_down),
        scratch=[pltpu.SemaphoreType.DMA((2 * cuts,))],
        limit=12,
        after=after,
    )


def tile_of(extent, most):
    size = most
    while extent % size:
        size //= 2
    return size


def expert_kernel(count, first_column, wide, *refs):
    parts, refs = refs[:count], refs[count:]
    if wide:
        gate_up_ref, down_ref, *outs, routed_ref, rows_ref, hidden_ref = refs
    else:
        routed_ref, gate_up_ref, down_ref, *outs, rows_ref, hidden_ref = refs
    hidden_size, features = down_ref.shape
    first = 0
    for part in parts:
        span = slice(first, first + part.shape[0])
        first += part.shape[0]
        rows_ref[span] = part[:, :features]
        if wide:
            routed_ref[span] = part[:, features:]
    places = lax.broadcasted_iota(jnp.int32, routed_ref.shape, 1)
    column = first_column + lax.axis_index("expert")
    chosen = jnp.where(places == column, routed_ref[...].astype(f32), 0.0)
    share = jnp.sum(chosen, axis=1, keepdims=True)
    rows = rows_ref[...]
    size = tile_of(hidden_size, 256)
    for low in range(0, hidden_size, size):
        span, beside = slice(low, low + size), slice(hidden_size + low, hidden_size + low + size)
        gate = jnp.dot(rows, gate_up_ref[:, span], preferred_element_type=f32)
        up = jnp.dot(rows, gate_up_ref[:, beside], preferred_element_type=f32)
        hidden_ref[:, span] = (gate / (1.0 + jnp.exp(-gate)) * up).astype(bf16)
    hidden = hidden_ref[...]
    size = tile_of(features, 512)
    for low in range(0, features, size):
        span = slice(low, low + size)
        done = jnp.dot(hidden, down_ref[:, span], preferred_element_type=f32) * share
        first = 0
        for out in outs:
            out[:, span] = done[first : first + out.shape[0]].astype(out.dtype)
            first += out.shape[0]


def run_expert(parts, routed, first_column, weights, after):
    gate_up, down_proj, _ = weights
    hidden_size, features = down_proj.shape
    width = parts[0].shape[1]
    count = sum(part.shape[0] for part in parts)
    quarter = count // 4
    wide = routed is None
    outs = [((quarter, features), f32)] * 2 + [((quarter, features), bf16)]
    outs += [((quarter // 2, features), bf16)] * 2
    if wide:
        outs = outs + [((count, width - features), bf16)]
    found = call(
        functools.partial(expert_kernel, len(parts), first_column, wide),
        outs,
        [VMEM] * (len(parts) + (2 if wide else 3)),
        *parts,
        *([] if wide else [routed]),
        gate_up,
        down_proj,
        scratch=[pltpu.VMEM((count, features), bf16), pltpu.VMEM((count, hidden_size), bf16)],
        limit=24,
        after=after,
    )
    return found[:5], found[5] if wide else routed


def in_hbm(array):
    return pltpu.with_memory_space_constraint(array, pltpu.HBM)


def open_rows(current, routes, gain, experts):
    batches, tokens, features = current.shape
    rows = batches * tokens
    columns = routes.shape[0] * experts
    width = features + columns + -columns % LANES
    current, routes = current.reshape(rows, features), jnp.swapaxes(routes, 2, 3)
    (wide,) = call(
        functools.partial(open_kernel, experts),
        [((rows, width), bf16)],
        [ANY] * 3,
        in_hbm(current),
        in_hbm(routes),
        in_hbm(gain),
        scratch=[
            pltpu.VMEM(current.shape, bf16),
            pltpu.VMEM(routes.shape, jnp.int32),
            pltpu.VMEM(gain.shape, f32),
            pltpu.SemaphoreType.DMA((3,)),
        ],
    )
    return wide


def run_layer(rows, routed, first_column, weights, loaded=()):
    far = lax.axis_size("expert") // 4
    routed = routed or [None, None]
    half = far // 2
    sent = [rows] + [swap(rows, 4, k, far) for k in range(1, half)]
    first = join_rows(sent, loaded, 0)
    first_beside = swap(first, 2, 1, 2)
    crossed = join_rows([swap(rows, 4, half, far)], (first,), WAIT)
    second = [crossed] + [swap(crossed, 4, k, far) for k in range(1, half)]
    second_beside = [swap(crossed, 2, 1, 2)]
    for piece in second[1:]:
        second_beside.append(swap(held(piece, (second_beside[0], first_beside)), 2, 1, 2))

    def worked(near, beside, routed, after):
        parts = near + beside
        parts += [swap(piece, 1, 1, 2) for piece in parts]
        return run_expert(parts, routed, first_column, weights, after)

    first_beside = held(first_beside, (second[-1], second_beside[0]))
    outs, first_columns = worked([first], [first_beside], routed[0], (second[-1],))
    mine1, near1, leaving1 = leave_pair(outs, 1, ())
    second_beside[-1] = held(second_beside[-1], outs[0])
    outs, second_columns = worked(second, second_beside, routed[1], tuple(leaving1))
    mine2, near2, leaving2 = leave_pair(outs, 1, ())
    back2 = [swap(piece, 2, 1, 2, True) for piece in leaving2]
    back1 = [swap(held(piece, back2[0]), 2, 1, 2, True) for piece in leaving1]
    crossed_back = cross_rows(mine2, near2, back2[0], half)
    pieces = call(
        functools.partial(apart_kernel, 0, half),
        [(rows.shape[:1] + mine1.shape[1:], bf16 if k else f32) for k in range(half)],
        [VMEM] * (2 + len(back1)),
        mine1,
        near1,
        *back1,
        after=tuple(leaving2),
    )
    arrived = [swap(piece, 4, k, far, True) if k else piece for k, piece in enumerate(pieces)]
    return [*arrived, crossed_back], [first_columns, second_columns], (outs[0],)


def close_rows(layer_no, current, gain, returned, after=()):
    return call(
        functools.partial(close_kernel, layer_no),
        [(current.shape, bf16)] * 2,
        [VMEM] * (2 + len(returned)),
        current,
        gain,
        *returned,
        after=after,
    )


def on_device(inputs, routes, norm_gain, w_gate_up, w_down):
    experts = lax.axis_size("expert")
    sections = lax.axis_size("section")
    batches, tokens, features = inputs.shape
    layers = routes.shape[0]
    weights = load_weights(0, w_gate_up, w_down)
    if sections == 1:
        outs, routed = [], None
        current = inputs.reshape(batches * tokens, features)
        rows = open_rows(inputs, routes, norm_gain, experts)
        for layer_no in range(layers):
            returned, routed, worked = run_layer(
                rows, routed, layer_no * experts, weights, weights[2:]
            )
            if layer_no == layers - 1:
                (whole,) = call(
                    functools.partial(end_kernel, len(outs)),
                    [((layers, batches, tokens, features), bf16)],
                    [VMEM] * (1 + len(returned) + len(outs)),
                    current,
                    *returned,
                    *outs,
                )
                return whole
            weights = load_weights(layer_no + 1, w_gate_up, w_down, worked)
            current, rows = close_rows(layer_no + 1, current, norm_gain, returned, weights[2:])
            outs.append(current)
    segment_no = lax.axis_index("section")
    handed = jnp.zeros((tokens, features), bf16)
    finished = []
    for turn_no in range(batches + 1):
        if turn_no < batches:
            fresh_rows = inputs[turn_no]
        else:
            fresh_rows = jnp.zeros((tokens, features), bf16)
        current = jnp.where(segment_no == 0, fresh_rows, handed)
        batch_pick = jnp.clip(turn_no - segment_no, 0, batches - 1)
        turn_routes = lax.dynamic_slice_in_dim(routes, batch_pick, 1, 1)
        rows = open_rows(current[None], turn_routes, norm_gain, experts)
        returned, _, _ = run_layer(rows, None, 0, weights)
        result, _ = close_rows(0, current, norm_gain, returned)
        finished.append(result)
        if turn_no < batches:
            handed = from_behind(result, "section", 1)
    first_segment = jnp.stack(finished[:batches])
    second_segment = jnp.stack(finished[1:])
    return jnp.where(segment_no == 0, first_segment, second_segment)[None]


def solution(mesh):
    placed = (
        P(None, ("groups", "expert"), None),
        P("section", None, ("groups", "expert"), None),
        P("section", None),
        P("section", "expert", None, None),
        P("section", "expert", None, None),
    )
    return jax.shard_map(
        on_device,
        mesh=mesh,
        in_specs=placed,
        out_specs=P("section", None, ("groups", "expert"), None),
        check_vma=False,
    )
```

```python
import functools

import jax
import jax.numpy as jnp
from jax import lax
from jax.experimental import pallas as pl
from jax.experimental.pallas import tpu as pltpu
from jax.sharding import PartitionSpec as P

eps = 1e-06
LANES = 128
MIB = 2**20
WAIT = 6 * 10**9
VMEM = pl.BlockSpec(memory_space=pltpu.VMEM)
ANY = pl.BlockSpec(memory_space=pl.ANY)
bf16, f32 = jnp.bfloat16, jnp.float32


def from_behind(value, axis, steps):
    count = lax.axis_size(axis)
    initial, last = (max(0, -steps), min(count, count - steps))
    return lax.ppermute(value, axis, [(source, source + steps) for source in range(initial, last)])


def call(kernel, outs, specs, *operands, scratch=(), limit=8, after=(), weight=0):
    shapes = tuple(jax.ShapeDtypeStruct(shape, dtype) for shape, dtype in outs)
    operands = (*after, *operands)
    return pl.pallas_call(
        lambda *refs: kernel(*refs[len(after) :]),
        out_shape=shapes,
        in_specs=[ANY] * len(after) + specs,
        out_specs=(VMEM,) * len(outs),
        scratch_shapes=scratch,
        compiler_params=pltpu.CompilerParams(vmem_limit_bytes=limit * MIB),
        cost_estimate=pl.CostEstimate(flops=weight, bytes_accessed=0, transcendentals=0),
    )(*operands)


def swap(value, stride, step, radix, back=False):
    count = lax.axis_size("expert")

    def partner(index):
        digit = index // stride % radix
        if radix & (radix - 1) == 0:
            other = digit ^ step
        else:
            other = (digit + (step if back else radix - step)) % radix
        return index + (other - digit) * stride

    return lax.ppermute(value, "expert", [(i, partner(i)) for i in range(count)])


def join_kernel(*refs):
    *parts, whole = refs
    rows = parts[0].shape[0]
    for k, part in enumerate(parts):
        whole[k * rows : (k + 1) * rows] = part[...]


def join_rows(parts, after, weight):
    tokens, width = parts[0].shape
    return call(
        join_kernel,
        [((len(parts) * tokens, width), parts[0].dtype)],
        [VMEM] * len(parts),
        *parts,
        after=after,
        weight=weight,
    )[0]


def held(value, until):
    return lax.optimization_barrier((value, until))[0]


def sum_kernel(count, mine, *refs):
    parts, totals = refs[:count], refs[count:]
    size, rows = parts[0].shape[0], totals[0].shape[0]
    grain = min(size, rows)
    for low in range(0, mine.shape[0], grain):
        part, total = parts[low // size], totals[low // rows]
        inside = slice(low % size, low % size + grain)
        total[low % rows : low % rows + grain] = (
            mine[low : low + grain] + part[inside].astype(f32)
        ).astype(total.dtype)


def apart_kernel(first, count, mine, near, *refs):
    beside, pieces = refs[:-count], refs[-count:]
    rows = pieces[0].shape[0]
    for k, piece in enumerate(pieces):
        span = slice((first + k) * rows, (first + k + 1) * rows)
        part = beside[k][...] if len(beside) == count else beside[0][span]
        total = mine[span] + near[span].astype(f32) + part.astype(f32)
        piece[...] = total.astype(piece.dtype)


def cross_kernel(mine, near, beside, *refs):
    *arrived, out = refs
    rows = out.shape[0]
    total = mine[:rows] + near[:rows].astype(f32) + beside[...].astype(f32)
    for piece in arrived:
        total = total + piece[...].astype(f32)
    out[...] = total.astype(out.dtype)


def leave_pair(found, count, after):
    mine_near, mine_beside, other_near, *other_beside = found
    arrived_beside = [swap(half, 1, 1, 2, True) for half in other_beside]
    arrived_near = swap(other_near, 1, 1, 2, True)
    rows, width = mine_beside.shape
    leaving = call(
        functools.partial(sum_kernel, len(other_beside)),
        [((rows // count, width), bf16)] * count,
        [VMEM] * (1 + len(other_beside)),
        mine_beside,
        *arrived_beside,
        after=after,
    )
    return mine_near, arrived_near, leaving


def cross_rows(mine, near, beside):
    far, count = lax.axis_size("expert") // 4, len(beside)
    shape = beside[0].shape
    hops, arrived = [], []
    if count > 1:
        hops = call(
            functools.partial(apart_kernel, 1, count - 1),
            [(shape, bf16)] * (count - 1),
            [VMEM] * (count + 1),
            mine,
            near,
            *beside[1:],
        )
        arrived = [swap(piece, 4, k, far, True) for k, piece in enumerate(hops, 1)]
    (crossing,) = call(
        cross_kernel, [(shape, bf16)], [VMEM] * (3 + len(arrived)), mine, near, beside[0], *arrived
    )
    return swap(crossing, 4, count, far, True), tuple(hops)


def normed_rows(widened, gain_row):
    scale_inv = lax.rsqrt(jnp.mean(widened * widened, axis=-1, keepdims=True) + eps)
    return (widened * scale_inv * gain_row).astype(bf16)


def open_kernel(experts, current_hbm, routes_hbm, gain_hbm, wide_ref, current, routes, gain, sems):
    pairs = ((current_hbm, current), (routes_hbm, routes), (gain_hbm, gain))
    copies = [pltpu.make_async_copy(a, b, sems.at[k]) for k, (a, b) in enumerate(pairs)]
    for copy in copies:
        copy.start()
    for copy in copies:
        copy.wait()
    features = current.shape[-1]
    layers, batches, top, tokens = routes.shape
    columns = wide_ref.shape[1] - features
    wide_ref[:, :features] = normed_rows(current[...].astype(f32), gain[0:1])
    places = lax.broadcasted_iota(jnp.int32, (columns, tokens), 0)
    same = lax.broadcasted_iota(jnp.int32, (tokens, tokens), 0) == lax.broadcasted_iota(
        jnp.int32, (tokens, tokens), 1
    )
    for batch in range(batches):
        chosen = jnp.zeros(places.shape, f32)
        for layer_no in range(layers):
            named = routes[layer_no, batch] + layer_no * experts
            for k in range(top):
                chosen = jnp.where(places == named[k : k + 1], 1.0, chosen)
        turned = lax.dot_general(
            same.astype(bf16),
            chosen.astype(bf16),
            (((1,), (1,)), ((), ())),
            preferred_element_type=f32,
        )
        wide_ref[batch * tokens : (batch + 1) * tokens, features:] = turned.astype(bf16)


def total_rows(current, kept, sent):
    total = kept[...]
    for piece in sent:
        total = total + piece[...].astype(f32)
    return (current.astype(f32) + total * 0.125).astype(bf16)


def close_kernel(layer_no, current_ref, gain_ref, kept, *refs):
    *sent, out_ref, normed_ref = refs
    out = total_rows(current_ref[...], kept, sent)
    out_ref[...] = out
    normed_ref[...] = normed_rows(out.astype(f32), gain_ref[layer_no : layer_no + 1])


def end_kernel(earlier, current_ref, kept, *refs):
    sent, before, outs_ref = refs[: len(refs) - earlier - 1], refs[-earlier - 1 : -1], refs[-1]
    layers, batches, tokens, _ = outs_ref.shape
    done = [ref[...] for ref in before] + [total_rows(current_ref[...], kept, sent)]
    for layer_no in range(layers):
        for batch in range(batches):
            outs_ref[layer_no, batch] = done[layer_no][batch * tokens : (batch + 1) * tokens]


def load_kernel(layer_no, cuts, gate_up_hbm, down_hbm, gate_up_ref, down_ref, token, sems):
    token[...] = jnp.zeros_like(token)
    copies = []
    for source, target in ((gate_up_hbm, gate_up_ref), (down_hbm, down_ref)):
        rows = target.shape[0] // cuts
        for cut in range(cuts):
            span = pl.ds(cut * rows, rows)
            copies.append(
                pltpu.make_async_copy(
                    source.at[layer_no, 0, span], target.at[span], sems.at[len(copies)]
                )
            )
    for copy in copies:
        copy.start()
    for copy in copies:
        copy.wait()


def load_weights(layer_no, w_gate_up, w_down, after=()):
    cuts = 4
    return call(
        functools.partial(load_kernel, layer_no, cuts),
        [(w_gate_up.shape[2:], bf16), (w_down.shape[2:], bf16), ((8, LANES), f32)],
        [ANY] * 2,
        in_hbm(w_gate_up),
        in_hbm(w_down),
        scratch=[pltpu.SemaphoreType.DMA((2 * cuts,))],
        limit=12,
        after=after,
    )


def tile_of(extent, most):
    size = most
    while extent % size:
        size //= 2
    return size


def expert_kernel(count, first_column, wide, *refs):
    parts, refs = refs[:count], refs[count:]
    if wide:
        gate_up_ref, down_ref, *outs, routed_ref, rows_ref, hidden_ref = refs
    else:
        routed_ref, gate_up_ref, down_ref, *outs, rows_ref, hidden_ref = refs
    hidden_size, features = down_ref.shape
    first = 0
    for part in parts:
        span = slice(first, first + part.shape[0])
        first += part.shape[0]
        rows_ref[span] = part[:, :features]
        if wide:
            routed_ref[span] = part[:, features:]
    places = lax.broadcasted_iota(jnp.int32, routed_ref.shape, 1)
    column = first_column + lax.axis_index("expert")
    chosen = jnp.where(places == column, routed_ref[...].astype(f32), 0.0)
    share = jnp.sum(chosen, axis=1, keepdims=True)
    rows = rows_ref[...]
    size = tile_of(hidden_size, 256)
    for low in range(0, hidden_size, size):
        span, beside = slice(low, low + size), slice(hidden_size + low, hidden_size + low + size)
        gate = jnp.dot(rows, gate_up_ref[:, span], preferred_element_type=f32)
        up = jnp.dot(rows, gate_up_ref[:, beside], preferred_element_type=f32)
        hidden_ref[:, span] = (gate / (1.0 + jnp.exp(-gate)) * up).astype(bf16)
    hidden = hidden_ref[...]
    size = tile_of(features, 512)
    for low in range(0, features, size):
        span = slice(low, low + size)
        done = jnp.dot(hidden, down_ref[:, span], preferred_element_type=f32) * share
        first = 0
        for out in outs:
            out[:, span] = done[first : first + out.shape[0]].astype(out.dtype)
            first += out.shape[0]


def run_expert(parts, routed, first_column, weights, after):
    gate_up, down_proj, _ = weights
    hidden_size, features = down_proj.shape
    width = parts[0].shape[1]
    count = sum(part.shape[0] for part in parts)
    quarter = count // 4
    wide = routed is None
    outs = [((quarter, features), f32)] * 2 + [((quarter, features), bf16)]
    outs += [((quarter // 2, features), bf16)] * 2
    if wide:
        outs = outs + [((count, width - features), bf16)]
    found = call(
        functools.partial(expert_kernel, len(parts), first_column, wide),
        outs,
        [VMEM] * (len(parts) + (2 if wide else 3)),
        *parts,
        *([] if wide else [routed]),
        gate_up,
        down_proj,
        scratch=[pltpu.VMEM((count, features), bf16), pltpu.VMEM((count, hidden_size), bf16)],
        limit=24,
        after=after,
    )
    return found[:5], found[5] if wide else routed


def in_hbm(array):
    return pltpu.with_memory_space_constraint(array, pltpu.HBM)


def open_rows(current, routes, gain, experts):
    batches, tokens, features = current.shape
    rows = batches * tokens
    columns = routes.shape[0] * experts
    width = features + columns + -columns % LANES
    current, routes = current.reshape(rows, features), jnp.swapaxes(routes, 2, 3)
    (wide,) = call(
        functools.partial(open_kernel, experts),
        [((rows, width), bf16)],
        [ANY] * 3,
        in_hbm(current),
        in_hbm(routes),
        in_hbm(gain),
        scratch=[
            pltpu.VMEM(current.shape, bf16),
            pltpu.VMEM(routes.shape, jnp.int32),
            pltpu.VMEM(gain.shape, f32),
            pltpu.SemaphoreType.DMA((3,)),
        ],
    )
    return wide


def run_layer(rows, routed, first_column, weights, loaded=()):
    far = lax.axis_size("expert") // 4
    routed = routed or [None, None]
    half = far // 2
    sent = [rows] + [swap(rows, 4, k, far) for k in range(1, half)]
    first = join_rows(sent, loaded, 0)
    first_beside = swap(first, 2, 1, 2)
    crossed = join_rows([swap(rows, 4, half, far)], (first,), WAIT)
    second = [crossed] + [swap(crossed, 4, k, far) for k in range(1, half)]
    second_beside = [swap(crossed, 2, 1, 2)]
    for piece in second[1:]:
        second_beside.append(swap(held(piece, (second_beside[0], first_beside)), 2, 1, 2))

    def worked(near, beside, routed, after):
        parts = near + beside
        parts += [swap(piece, 1, 1, 2) for piece in parts]
        return run_expert(parts, routed, first_column, weights, after)

    first_beside = held(first_beside, (second[-1], second_beside[0]))
    outs, first_columns = worked([first], [first_beside], routed[0], (second[-1],))
    mine1, near1, leaving1 = leave_pair(outs, half, ())
    second_beside[-1] = held(second_beside[-1], outs[0])
    outs, second_columns = worked(second, second_beside, routed[1], tuple(leaving1))
    mine2, near2, leaving2 = leave_pair(outs, half, ())
    back2 = [swap(piece, 2, 1, 2, True) for piece in leaving2]
    crossed_back, hops = cross_rows(mine2, near2, back2)
    back1 = [swap(held(piece, (back2[0], *hops)), 2, 1, 2, True) for piece in leaving1]
    pieces = call(
        functools.partial(apart_kernel, 0, half),
        [(rows.shape[:1] + mine1.shape[1:], bf16 if k else f32) for k in range(half)],
        [VMEM] * (2 + len(back1)),
        mine1,
        near1,
        *back1,
        after=tuple(leaving2),
    )
    arrived = [swap(piece, 4, k, far, True) if k else piece for k, piece in enumerate(pieces)]
    return [*arrived, crossed_back], [first_columns, second_columns], (outs[0],)


def close_rows(layer_no, current, gain, returned, after=()):
    return call(
        functools.partial(close_kernel, layer_no),
        [(current.shape, bf16)] * 2,
        [VMEM] * (2 + len(returned)),
        current,
        gain,
        *returned,
        after=after,
    )


def on_device(inputs, routes, norm_gain, w_gate_up, w_down):
    experts = lax.axis_size("expert")
    sections = lax.axis_size("section")
    batches, tokens, features = inputs.shape
    layers = routes.shape[0]
    weights = load_weights(0, w_gate_up, w_down)
    if sections == 1:
        outs, routed = [], None
        current = inputs.reshape(batches * tokens, features)
        rows = open_rows(inputs, routes, norm_gain, experts)
        for layer_no in range(layers):
            returned, routed, worked = run_layer(
                rows, routed, layer_no * experts, weights, weights[2:]
            )
            if layer_no == layers - 1:
                (whole,) = call(
                    functools.partial(end_kernel, len(outs)),
                    [((layers, batches, tokens, features), bf16)],
                    [VMEM] * (1 + len(returned) + len(outs)),
                    current,
                    *returned,
                    *outs,
                )
                return whole
            weights = load_weights(layer_no + 1, w_gate_up, w_down, worked)
            current, rows = close_rows(layer_no + 1, current, norm_gain, returned, weights[2:])
            outs.append(current)
    segment_no = lax.axis_index("section")
    handed = jnp.zeros((tokens, features), bf16)
    finished = []
    for turn_no in range(batches + 1):
        if turn_no < batches:
            fresh_rows = inputs[turn_no]
        else:
            fresh_rows = jnp.zeros((tokens, features), bf16)
        current = jnp.where(segment_no == 0, fresh_rows, handed)
        batch_pick = jnp.clip(turn_no - segment_no, 0, batches - 1)
        turn_routes = lax.dynamic_slice_in_dim(routes, batch_pick, 1, 1)
        rows = open_rows(current[None], turn_routes, norm_gain, experts)
        returned, _, _ = run_layer(rows, None, 0, weights)
        result, _ = close_rows(0, current, norm_gain, returned)
        finished.append(result)
        if turn_no < batches:
            handed = from_behind(result, "section", 1)
    first_segment = jnp.stack(finished[:batches])
    second_segment = jnp.stack(finished[1:])
    return jnp.where(segment_no == 0, first_segment, second_segment)[None]


def solution(mesh):
    placed = (
        P(None, ("groups", "expert"), None),
        P("section", None, ("groups", "expert"), None),
        P("section", None),
        P("section", "expert", None, None),
        P("section", "expert", None, None),
    )
    return jax.shard_map(
        on_device,
        mesh=mesh,
        in_specs=placed,
        out_specs=P("section", None, ("groups", "expert"), None),
        check_vma=False,
    )
```

```python
import functools

import jax
import jax.numpy as jnp
from jax import lax
from jax.experimental import pallas as pl
from jax.experimental.pallas import tpu as pltpu
from jax.sharding import PartitionSpec as P

eps = 1e-06
LANES = 128
MIB = 2**20
WAIT = 6 * 10**9
VMEM = pl.BlockSpec(memory_space=pltpu.VMEM)
ANY = pl.BlockSpec(memory_space=pl.ANY)
bf16, f32 = jnp.bfloat16, jnp.float32


def from_behind(value, axis, steps):
    count = lax.axis_size(axis)
    initial, last = (max(0, -steps), min(count, count - steps))
    return lax.ppermute(value, axis, [(source, source + steps) for source in range(initial, last)])


def call(kernel, outs, specs, *operands, scratch=(), limit=8, after=(), weight=0):
    shapes = tuple(jax.ShapeDtypeStruct(shape, dtype) for shape, dtype in outs)
    operands = (*after, *operands)
    return pl.pallas_call(
        lambda *refs: kernel(*refs[len(after) :]),
        out_shape=shapes,
        in_specs=[ANY] * len(after) + specs,
        out_specs=(VMEM,) * len(outs),
        scratch_shapes=scratch,
        compiler_params=pltpu.CompilerParams(vmem_limit_bytes=limit * MIB),
        cost_estimate=pl.CostEstimate(flops=weight, bytes_accessed=0, transcendentals=0),
    )(*operands)


def swap(value, stride, step, radix, back=False):
    count = lax.axis_size("expert")

    def partner(index):
        digit = index // stride % radix
        if radix & (radix - 1) == 0:
            other = digit ^ step
        else:
            other = (digit + (step if back else radix - step)) % radix
        return index + (other - digit) * stride

    return lax.ppermute(value, "expert", [(i, partner(i)) for i in range(count)])


def join_kernel(*refs):
    *parts, whole = refs
    rows = parts[0].shape[0]
    for k, part in enumerate(parts):
        whole[k * rows : (k + 1) * rows] = part[...]


def join_rows(parts, after, weight):
    tokens, width = parts[0].shape
    return call(
        join_kernel,
        [((len(parts) * tokens, width), parts[0].dtype)],
        [VMEM] * len(parts),
        *parts,
        after=after,
        weight=weight,
    )[0]


def held(value, until):
    return lax.optimization_barrier((value, until))[0]


def sum_kernel(count, mine, *refs):
    parts, totals = refs[:count], refs[count:]
    size, rows = parts[0].shape[0], totals[0].shape[0]
    grain = min(size, rows)
    for low in range(0, mine.shape[0], grain):
        part, total = parts[low // size], totals[low // rows]
        inside = slice(low % size, low % size + grain)
        total[low % rows : low % rows + grain] = (
            mine[low : low + grain] + part[inside].astype(f32)
        ).astype(total.dtype)


def apart_kernel(first, count, mine, near, *refs):
    beside, pieces = refs[:-count], refs[-count:]
    rows = pieces[0].shape[0]
    for k, piece in enumerate(pieces):
        span = slice((first + k) * rows, (first + k + 1) * rows)
        part = beside[k][...] if len(beside) == count else beside[0][span]
        total = mine[span] + near[span].astype(f32) + part.astype(f32)
        piece[...] = total.astype(piece.dtype)


def cross_kernel(mine, near, beside, *refs):
    *arrived, out = refs
    rows = out.shape[0]
    total = mine[:rows] + near[:rows].astype(f32) + beside[...].astype(f32)
    for piece in arrived:
        total = total + piece[...].astype(f32)
    out[...] = total.astype(out.dtype)


def leave_pair(found, count, after):
    mine_near, mine_beside, other_near, *other_beside = found
    arrived_beside = [swap(half, 1, 1, 2, True) for half in other_beside]
    arrived_near = swap(other_near, 1, 1, 2, True)
    rows, width = mine_beside.shape
    leaving = call(
        functools.partial(sum_kernel, len(other_beside)),
        [((rows // count, width), bf16)] * count,
        [VMEM] * (1 + len(other_beside)),
        mine_beside,
        *arrived_beside,
        after=after,
    )
    return mine_near, arrived_near, leaving


def cross_rows(mine, near, beside):
    far, count = lax.axis_size("expert") // 4, len(beside)
    shape = beside[0].shape
    hops, arrived = [], []
    if count > 1:
        hops = call(
            functools.partial(apart_kernel, 1, count - 1),
            [(shape, bf16)] * (count - 1),
            [VMEM] * (count + 1),
            mine,
            near,
            *beside[1:],
        )
        arrived = [swap(piece, 4, k, far, True) for k, piece in enumerate(hops, 1)]
    (crossing,) = call(
        cross_kernel, [(shape, bf16)], [VMEM] * (3 + len(arrived)), mine, near, beside[0], *arrived
    )
    return swap(crossing, 4, count, far, True), tuple(hops)


def normed_rows(widened, gain_row):
    scale_inv = lax.rsqrt(jnp.mean(widened * widened, axis=-1, keepdims=True) + eps)
    return (widened * scale_inv * gain_row).astype(bf16)


def open_kernel(experts, current_hbm, routes_hbm, gain_hbm, wide_ref, current, routes, gain, sems):
    pairs = ((current_hbm, current), (routes_hbm, routes), (gain_hbm, gain))
    copies = [pltpu.make_async_copy(a, b, sems.at[k]) for k, (a, b) in enumerate(pairs)]
    for copy in copies:
        copy.start()
    for copy in copies:
        copy.wait()
    features = current.shape[-1]
    layers, batches, top, tokens = routes.shape
    columns = wide_ref.shape[1] - features
    wide_ref[:, :features] = normed_rows(current[...].astype(f32), gain[0:1])
    places = lax.broadcasted_iota(jnp.int32, (columns, tokens), 0)
    same = lax.broadcasted_iota(jnp.int32, (tokens, tokens), 0) == lax.broadcasted_iota(
        jnp.int32, (tokens, tokens), 1
    )
    for batch in range(batches):
        chosen = jnp.zeros(places.shape, f32)
        for layer_no in range(layers):
            named = routes[layer_no, batch] + layer_no * experts
            for k in range(top):
                chosen = jnp.where(places == named[k : k + 1], 1.0, chosen)
        turned = lax.dot_general(
            same.astype(bf16),
            chosen.astype(bf16),
            (((1,), (1,)), ((), ())),
            preferred_element_type=f32,
        )
        wide_ref[batch * tokens : (batch + 1) * tokens, features:] = turned.astype(bf16)


def total_rows(current, kept, sent):
    total = kept[...]
    for piece in sent:
        total = total + piece[...].astype(f32)
    return (current.astype(f32) + total * 0.125).astype(bf16)


def close_kernel(layer_no, current_ref, gain_ref, kept, *refs):
    *sent, out_ref, normed_ref = refs
    out = total_rows(current_ref[...], kept, sent)
    out_ref[...] = out
    normed_ref[...] = normed_rows(out.astype(f32), gain_ref[layer_no : layer_no + 1])


def end_kernel(earlier, current_ref, kept, *refs):
    sent, before, outs_ref = refs[: len(refs) - earlier - 1], refs[-earlier - 1 : -1], refs[-1]
    layers, batches, tokens, _ = outs_ref.shape
    done = [ref[...] for ref in before] + [total_rows(current_ref[...], kept, sent)]
    for layer_no in range(layers):
        for batch in range(batches):
            outs_ref[layer_no, batch] = done[layer_no][batch * tokens : (batch + 1) * tokens]


def load_kernel(layer_no, cuts, gate_up_hbm, down_hbm, gate_up_ref, down_ref, token, sems):
    token[...] = jnp.zeros_like(token)
    copies = []
    for source, target in ((gate_up_hbm, gate_up_ref), (down_hbm, down_ref)):
        rows = target.shape[0] // cuts
        for cut in range(cuts):
            span = pl.ds(cut * rows, rows)
            copies.append(
                pltpu.make_async_copy(
                    source.at[layer_no, 0, span], target.at[span], sems.at[len(copies)]
                )
            )
    for copy in copies:
        copy.start()
    for copy in copies:
        copy.wait()


def load_weights(layer_no, w_gate_up, w_down, after=()):
    cuts = 4
    return call(
        functools.partial(load_kernel, layer_no, cuts),
        [(w_gate_up.shape[2:], bf16), (w_down.shape[2:], bf16), ((8, LANES), f32)],
        [ANY] * 2,
        in_hbm(w_gate_up),
        in_hbm(w_down),
        scratch=[pltpu.SemaphoreType.DMA((2 * cuts,))],
        limit=12,
        after=after,
    )


def tile_of(extent, most):
    size = most
    while extent % size:
        size //= 2
    return size


def expert_kernel(count, first_column, wide, *refs):
    parts, refs = refs[:count], refs[count:]
    if wide:
        gate_up_ref, down_ref, *outs, routed_ref, rows_ref, hidden_ref = refs
    else:
        routed_ref, gate_up_ref, down_ref, *outs, rows_ref, hidden_ref = refs
    hidden_size, features = down_ref.shape
    first = 0
    for part in parts:
        span = slice(first, first + part.shape[0])
        first += part.shape[0]
        rows_ref[span] = part[:, :features]
        if wide:
            routed_ref[span] = part[:, features:]
    places = lax.broadcasted_iota(jnp.int32, routed_ref.shape, 1)
    column = first_column + lax.axis_index("expert")
    chosen = jnp.where(places == column, routed_ref[...].astype(f32), 0.0)
    share = jnp.sum(chosen, axis=1, keepdims=True)
    rows = rows_ref[...]
    size = tile_of(hidden_size, 256)
    for low in range(0, hidden_size, size):
        span, beside = slice(low, low + size), slice(hidden_size + low, hidden_size + low + size)
        gate = jnp.dot(rows, gate_up_ref[:, span], preferred_element_type=f32)
        up = jnp.dot(rows, gate_up_ref[:, beside], preferred_element_type=f32)
        hidden_ref[:, span] = (gate / (1.0 + jnp.exp(-gate)) * up).astype(bf16)
    hidden = hidden_ref[...]
    size = tile_of(features, 512)
    for low in range(0, features, size):
        span = slice(low, low + size)
        done = jnp.dot(hidden, down_ref[:, span], preferred_element_type=f32) * share
        first = 0
        for out in outs:
            out[:, span] = done[first : first + out.shape[0]].astype(out.dtype)
            first += out.shape[0]


def run_expert(parts, routed, first_column, weights, after):
    gate_up, down_proj, _ = weights
    hidden_size, features = down_proj.shape
    width = parts[0].shape[1]
    count = sum(part.shape[0] for part in parts)
    quarter = count // 4
    wide = routed is None
    outs = [((quarter, features), f32)] * 2 + [((quarter, features), bf16)]
    outs += [((quarter // 2, features), bf16)] * 2
    if wide:
        outs = outs + [((count, width - features), bf16)]
    found = call(
        functools.partial(expert_kernel, len(parts), first_column, wide),
        outs,
        [VMEM] * (len(parts) + (2 if wide else 3)),
        *parts,
        *([] if wide else [routed]),
        gate_up,
        down_proj,
        scratch=[pltpu.VMEM((count, features), bf16), pltpu.VMEM((count, hidden_size), bf16)],
        limit=24,
        after=after,
    )
    return found[:5], found[5] if wide else routed


def in_hbm(array):
    return pltpu.with_memory_space_constraint(array, pltpu.HBM)


def open_rows(current, routes, gain, experts):
    batches, tokens, features = current.shape
    rows = batches * tokens
    columns = routes.shape[0] * experts
    width = features + columns + -columns % LANES
    current, routes = current.reshape(rows, features), jnp.swapaxes(routes, 2, 3)
    (wide,) = call(
        functools.partial(open_kernel, experts),
        [((rows, width), bf16)],
        [ANY] * 3,
        in_hbm(current),
        in_hbm(routes),
        in_hbm(gain),
        scratch=[
            pltpu.VMEM(current.shape, bf16),
            pltpu.VMEM(routes.shape, jnp.int32),
            pltpu.VMEM(gain.shape, f32),
            pltpu.SemaphoreType.DMA((3,)),
        ],
    )
    return wide


def run_layer(rows, routed, first_column, weights, loaded=()):
    far = lax.axis_size("expert") // 4
    routed = routed or [None, None]
    half = far // 2
    sent = [rows] + [swap(rows, 4, k, far) for k in range(1, half)]
    first = join_rows(sent, loaded, 0)
    first_beside = swap(first, 2, 1, 2)
    crossed = join_rows([swap(rows, 4, half, far)], (first,), WAIT)
    second = [crossed] + [swap(crossed, 4, k, far) for k in range(1, half)]
    second_beside = [swap(crossed, 2, 1, 2)]
    for piece in second[1:]:
        second_beside.append(swap(held(piece, (second_beside[0], first_beside)), 2, 1, 2))

    def worked(near, beside, routed, after):
        parts = near + beside
        parts += [swap(piece, 1, 1, 2) for piece in parts]
        return run_expert(parts, routed, first_column, weights, after)

    first_beside = held(first_beside, (second[-1], second_beside[0]))
    outs, first_columns = worked([first], [first_beside], routed[0], (second[-1],))
    mine1, near1, leaving1 = leave_pair(outs, half, ())
    second_beside[-1] = held(second_beside[-1], outs[0])
    outs, second_columns = worked(second, second_beside, routed[1], tuple(leaving1))
    mine2, near2, leaving2 = leave_pair(outs, half, ())
    back2 = [swap(piece, 2, 1, 2, True) for piece in leaving2]
    crossed_back, hops = cross_rows(mine2, near2, back2)
    back1 = [swap(held(piece, hops), 2, 1, 2, True) for piece in leaving1]
    pieces = call(
        functools.partial(apart_kernel, 0, half),
        [(rows.shape[:1] + mine1.shape[1:], bf16 if k else f32) for k in range(half)],
        [VMEM] * (2 + len(back1)),
        mine1,
        near1,
        *back1,
        after=tuple(leaving2),
    )
    arrived = [swap(piece, 4, k, far, True) if k else piece for k, piece in enumerate(pieces)]
    return [*arrived, crossed_back], [first_columns, second_columns], (outs[0],)


def close_rows(layer_no, current, gain, returned, after=()):
    return call(
        functools.partial(close_kernel, layer_no),
        [(current.shape, bf16)] * 2,
        [VMEM] * (2 + len(returned)),
        current,
        gain,
        *returned,
        after=after,
    )


def on_device(inputs, routes, norm_gain, w_gate_up, w_down):
    experts = lax.axis_size("expert")
    sections = lax.axis_size("section")
    batches, tokens, features = inputs.shape
    layers = routes.shape[0]
    weights = load_weights(0, w_gate_up, w_down)
    if sections == 1:
        outs, routed = [], None
        current = inputs.reshape(batches * tokens, features)
        rows = open_rows(inputs, routes, norm_gain, experts)
        for layer_no in range(layers):
            returned, routed, worked = run_layer(
                rows, routed, layer_no * experts, weights, weights[2:]
            )
            if layer_no == layers - 1:
                (whole,) = call(
                    functools.partial(end_kernel, len(outs)),
                    [((layers, batches, tokens, features), bf16)],
                    [VMEM] * (1 + len(returned) + len(outs)),
                    current,
                    *returned,
                    *outs,
                )
                return whole
            weights = load_weights(layer_no + 1, w_gate_up, w_down, worked)
            current, rows = close_rows(layer_no + 1, current, norm_gain, returned, weights[2:])
            outs.append(current)
    segment_no = lax.axis_index("section")
    handed = jnp.zeros((tokens, features), bf16)
    finished = []
    for turn_no in range(batches + 1):
        if turn_no < batches:
            fresh_rows = inputs[turn_no]
        else:
            fresh_rows = jnp.zeros((tokens, features), bf16)
        current = jnp.where(segment_no == 0, fresh_rows, handed)
        batch_pick = jnp.clip(turn_no - segment_no, 0, batches - 1)
        turn_routes = lax.dynamic_slice_in_dim(routes, batch_pick, 1, 1)
        rows = open_rows(current[None], turn_routes, norm_gain, experts)
        returned, _, _ = run_layer(rows, None, 0, weights)
        result, _ = close_rows(0, current, norm_gain, returned)
        finished.append(result)
        if turn_no < batches:
            handed = from_behind(result, "section", 1)
    first_segment = jnp.stack(finished[:batches])
    second_segment = jnp.stack(finished[1:])
    return jnp.where(segment_no == 0, first_segment, second_segment)[None]


def solution(mesh):
    placed = (
        P(None, ("groups", "expert"), None),
        P("section", None, ("groups", "expert"), None),
        P("section", None),
        P("section", "expert", None, None),
        P("section", "expert", None, None),
    )
    return jax.shard_map(
        on_device,
        mesh=mesh,
        in_specs=placed,
        out_specs=P("section", None, ("groups", "expert"), None),
        check_vma=False,
    )
```

```python
import functools

import jax
import jax.numpy as jnp
from jax import lax
from jax.experimental import pallas as pl
from jax.experimental.pallas import tpu as pltpu
from jax.sharding import PartitionSpec as P

eps = 1e-06
LANES = 128
MIB = 2**20
WAIT = 6 * 10**9
VMEM = pl.BlockSpec(memory_space=pltpu.VMEM)
ANY = pl.BlockSpec(memory_space=pl.ANY)
bf16, f32 = jnp.bfloat16, jnp.float32


def from_behind(value, axis, steps):
    count = lax.axis_size(axis)
    initial, last = (max(0, -steps), min(count, count - steps))
    return lax.ppermute(value, axis, [(source, source + steps) for source in range(initial, last)])


def call(kernel, outs, specs, *operands, scratch=(), limit=8, after=(), weight=0):
    shapes = tuple(jax.ShapeDtypeStruct(shape, dtype) for shape, dtype in outs)
    operands = (*after, *operands)
    return pl.pallas_call(
        lambda *refs: kernel(*refs[len(after) :]),
        out_shape=shapes,
        in_specs=[ANY] * len(after) + specs,
        out_specs=(VMEM,) * len(outs),
        scratch_shapes=scratch,
        compiler_params=pltpu.CompilerParams(vmem_limit_bytes=limit * MIB),
        cost_estimate=pl.CostEstimate(flops=weight, bytes_accessed=0, transcendentals=0),
    )(*operands)


def swap(value, stride, step, radix, back=False):
    count = lax.axis_size("expert")

    def partner(index):
        digit = index // stride % radix
        if radix & (radix - 1) == 0:
            other = digit ^ step
        else:
            other = (digit + (step if back else radix - step)) % radix
        return index + (other - digit) * stride

    return lax.ppermute(value, "expert", [(i, partner(i)) for i in range(count)])


def join_kernel(*refs):
    *parts, whole = refs
    rows = parts[0].shape[0]
    for k, part in enumerate(parts):
        whole[k * rows : (k + 1) * rows] = part[...]


def join_rows(parts, after, weight):
    tokens, width = parts[0].shape
    return call(
        join_kernel,
        [((len(parts) * tokens, width), parts[0].dtype)],
        [VMEM] * len(parts),
        *parts,
        after=after,
        weight=weight,
    )[0]


def held(value, until):
    return lax.optimization_barrier((value, until))[0]


def sum_kernel(count, mine, *refs):
    parts, totals = refs[:count], refs[count:]
    size, rows = parts[0].shape[0], totals[0].shape[0]
    grain = min(size, rows)
    for low in range(0, mine.shape[0], grain):
        part, total = parts[low // size], totals[low // rows]
        inside = slice(low % size, low % size + grain)
        total[low % rows : low % rows + grain] = (
            mine[low : low + grain] + part[inside].astype(f32)
        ).astype(total.dtype)


def apart_kernel(first, count, mine, near, *refs):
    beside, pieces = refs[:-count], refs[-count:]
    rows = pieces[0].shape[0]
    for k, piece in enumerate(pieces):
        span = slice((first + k) * rows, (first + k + 1) * rows)
        part = beside[k][...] if len(beside) == count else beside[0][span]
        total = mine[span] + near[span].astype(f32) + part.astype(f32)
        piece[...] = total.astype(piece.dtype)


def cross_kernel(mine, near, beside, *refs):
    *arrived, out = refs
    rows = out.shape[0]
    total = mine[:rows] + near[:rows].astype(f32) + beside[...].astype(f32)
    for piece in arrived:
        total = total + piece[...].astype(f32)
    out[...] = total.astype(out.dtype)


def leave_pair(found, count, after):
    mine_near, mine_beside, other_near, *other_beside = found
    arrived_beside = [swap(half, 1, 1, 2, True) for half in other_beside]
    arrived_near = swap(other_near, 1, 1, 2, True)
    rows, width = mine_beside.shape
    leaving = call(
        functools.partial(sum_kernel, len(other_beside)),
        [((rows // count, width), bf16)] * count,
        [VMEM] * (1 + len(other_beside)),
        mine_beside,
        *arrived_beside,
        after=after,
    )
    return mine_near, arrived_near, leaving


def cross_rows(mine, near, beside):
    far, count = lax.axis_size("expert") // 4, len(beside)
    shape = beside[0].shape
    hops, arrived = [], []
    if count > 1:
        hops = call(
            functools.partial(apart_kernel, 1, count - 1),
            [(shape, bf16)] * (count - 1),
            [VMEM] * (count + 1),
            mine,
            near,
            *beside[1:],
        )
        arrived = [swap(piece, 4, k, far, True) for k, piece in enumerate(hops, 1)]
    (crossing,) = call(
        cross_kernel, [(shape, bf16)], [VMEM] * (3 + len(arrived)), mine, near, beside[0], *arrived
    )
    return swap(crossing, 4, count, far, True), tuple(hops)


def normed_rows(widened, gain_row):
    scale_inv = lax.rsqrt(jnp.mean(widened * widened, axis=-1, keepdims=True) + eps)
    return (widened * scale_inv * gain_row).astype(bf16)


def open_kernel(experts, current_hbm, routes_hbm, gain_hbm, wide_ref, current, routes, gain, sems):
    pairs = ((current_hbm, current), (routes_hbm, routes), (gain_hbm, gain))
    copies = [pltpu.make_async_copy(a, b, sems.at[k]) for k, (a, b) in enumerate(pairs)]
    for copy in copies:
        copy.start()
    for copy in copies:
        copy.wait()
    features = current.shape[-1]
    layers, batches, top, tokens = routes.shape
    columns = wide_ref.shape[1] - features
    wide_ref[:, :features] = normed_rows(current[...].astype(f32), gain[0:1])
    places = lax.broadcasted_iota(jnp.int32, (columns, tokens), 0)
    same = lax.broadcasted_iota(jnp.int32, (tokens, tokens), 0) == lax.broadcasted_iota(
        jnp.int32, (tokens, tokens), 1
    )
    for batch in range(batches):
        chosen = jnp.zeros(places.shape, f32)
        for layer_no in range(layers):
            named = routes[layer_no, batch] + layer_no * experts
            for k in range(top):
                chosen = jnp.where(places == named[k : k + 1], 1.0, chosen)
        turned = lax.dot_general(
            same.astype(bf16),
            chosen.astype(bf16),
            (((1,), (1,)), ((), ())),
            preferred_element_type=f32,
        )
        wide_ref[batch * tokens : (batch + 1) * tokens, features:] = turned.astype(bf16)


def total_rows(current, kept, sent):
    total = kept[...]
    for piece in sent:
        total = total + piece[...].astype(f32)
    return (current.astype(f32) + total * 0.125).astype(bf16)


def close_kernel(layer_no, current_ref, gain_ref, kept, *refs):
    *sent, out_ref, normed_ref = refs
    out = total_rows(current_ref[...], kept, sent)
    out_ref[...] = out
    normed_ref[...] = normed_rows(out.astype(f32), gain_ref[layer_no : layer_no + 1])


def end_kernel(earlier, current_ref, kept, *refs):
    sent, before, outs_ref = refs[: len(refs) - earlier - 1], refs[-earlier - 1 : -1], refs[-1]
    layers, batches, tokens, _ = outs_ref.shape
    done = [ref[...] for ref in before] + [total_rows(current_ref[...], kept, sent)]
    for layer_no in range(layers):
        for batch in range(batches):
            outs_ref[layer_no, batch] = done[layer_no][batch * tokens : (batch + 1) * tokens]


def load_kernel(layer_no, cuts, gate_up_hbm, down_hbm, gate_up_ref, down_ref, token, sems):
    token[...] = jnp.zeros_like(token)
    copies = []
    for source, target in ((gate_up_hbm, gate_up_ref), (down_hbm, down_ref)):
        rows = target.shape[0] // cuts
        for cut in range(cuts):
            span = pl.ds(cut * rows, rows)
            copies.append(
                pltpu.make_async_copy(
                    source.at[layer_no, 0, span], target.at[span], sems.at[len(copies)]
                )
            )
    for copy in copies:
        copy.start()
    for copy in copies:
        copy.wait()


def load_weights(layer_no, w_gate_up, w_down, after=()):
    cuts = 4
    return call(
        functools.partial(load_kernel, layer_no, cuts),
        [(w_gate_up.shape[2:], bf16), (w_down.shape[2:], bf16), ((8, LANES), f32)],
        [ANY] * 2,
        in_hbm(w_gate_up),
        in_hbm(w_down),
        scratch=[pltpu.SemaphoreType.DMA((2 * cuts,))],
        limit=12,
        after=after,
    )


def tile_of(extent, most):
    size = most
    while extent % size:
        size //= 2
    return size


def expert_kernel(count, first_column, wide, *refs):
    parts, refs = refs[:count], refs[count:]
    if wide:
        gate_up_ref, down_ref, *outs, routed_ref, rows_ref, hidden_ref = refs
    else:
        routed_ref, gate_up_ref, down_ref, *outs, rows_ref, hidden_ref = refs
    hidden_size, features = down_ref.shape
    first = 0
    for part in parts:
        span = slice(first, first + part.shape[0])
        first += part.shape[0]
        rows_ref[span] = part[:, :features]
        if wide:
            routed_ref[span] = part[:, features:]
    places = lax.broadcasted_iota(jnp.int32, routed_ref.shape, 1)
    column = first_column + lax.axis_index("expert")
    chosen = jnp.where(places == column, routed_ref[...].astype(f32), 0.0)
    share = jnp.sum(chosen, axis=1, keepdims=True)
    rows = rows_ref[...]
    size = tile_of(hidden_size, 256)
    for low in range(0, hidden_size, size):
        span, beside = slice(low, low + size), slice(hidden_size + low, hidden_size + low + size)
        gate = jnp.dot(rows, gate_up_ref[:, span], preferred_element_type=f32)
        up = jnp.dot(rows, gate_up_ref[:, beside], preferred_element_type=f32)
        hidden_ref[:, span] = (gate / (1.0 + jnp.exp(-gate)) * up).astype(bf16)
    hidden = hidden_ref[...]
    size = tile_of(features, 512)
    for low in range(0, features, size):
        span = slice(low, low + size)
        done = jnp.dot(hidden, down_ref[:, span], preferred_element_type=f32) * share
        first = 0
        for out in outs:
            out[:, span] = done[first : first + out.shape[0]].astype(out.dtype)
            first += out.shape[0]


def run_expert(parts, routed, first_column, weights, after):
    gate_up, down_proj, _ = weights
    hidden_size, features = down_proj.shape
    width = parts[0].shape[1]
    count = sum(part.shape[0] for part in parts)
    quarter = count // 4
    wide = routed is None
    outs = [((quarter, features), f32)] * 2 + [((quarter, features), bf16)]
    outs += [((quarter // 2, features), bf16)] * 2
    if wide:
        outs = outs + [((count, width - features), bf16)]
    found = call(
        functools.partial(expert_kernel, len(parts), first_column, wide),
        outs,
        [VMEM] * (len(parts) + (2 if wide else 3)),
        *parts,
        *([] if wide else [routed]),
        gate_up,
        down_proj,
        scratch=[pltpu.VMEM((count, features), bf16), pltpu.VMEM((count, hidden_size), bf16)],
        limit=24,
        after=after,
    )
    return found[:5], found[5] if wide else routed


def in_hbm(array):
    return pltpu.with_memory_space_constraint(array, pltpu.HBM)


def open_rows(current, routes, gain, experts):
    batches, tokens, features = current.shape
    rows = batches * tokens
    columns = routes.shape[0] * experts
    width = features + columns + -columns % LANES
    current, routes = current.reshape(rows, features), jnp.swapaxes(routes, 2, 3)
    (wide,) = call(
        functools.partial(open_kernel, experts),
        [((rows, width), bf16)],
        [ANY] * 3,
        in_hbm(current),
        in_hbm(routes),
        in_hbm(gain),
        scratch=[
            pltpu.VMEM(current.shape, bf16),
            pltpu.VMEM(routes.shape, jnp.int32),
            pltpu.VMEM(gain.shape, f32),
            pltpu.SemaphoreType.DMA((3,)),
        ],
    )
    return wide


def run_layer(rows, routed, first_column, weights, loaded=()):
    far = lax.axis_size("expert") // 4
    routed = routed or [None, None]
    half = far // 2
    sent = [rows] + [swap(rows, 4, k, far) for k in range(1, half)]
    first = join_rows(sent, (), 0)
    first_beside = swap(first, 2, 1, 2)
    crossed = join_rows([swap(rows, 4, half, far)], (first,), WAIT)
    second = [crossed] + [swap(crossed, 4, k, far) for k in range(1, half)]
    second_beside = [swap(crossed, 2, 1, 2)]
    for piece in second[1:]:
        second_beside.append(swap(held(piece, (second_beside[0], first_beside, *loaded)), 2, 1, 2))

    def worked(near, beside, routed, after):
        parts = near + beside
        parts += [swap(piece, 1, 1, 2) for piece in parts]
        return run_expert(parts, routed, first_column, weights, after)

    first_beside = held(first_beside, (second[-1], second_beside[0]))
    outs, first_columns = worked([first], [first_beside], routed[0], (second[-1],))
    mine1, near1, leaving1 = leave_pair(outs, half, ())
    second_beside[-1] = held(second_beside[-1], outs[0])
    outs, second_columns = worked(second, second_beside, routed[1], tuple(leaving1))
    mine2, near2, leaving2 = leave_pair(outs, half, ())
    back2 = [swap(piece, 2, 1, 2, True) for piece in leaving2]
    crossed_back, hops = cross_rows(mine2, near2, back2)
    back1 = [swap(held(piece, hops), 2, 1, 2, True) for piece in leaving1]
    pieces = call(
        functools.partial(apart_kernel, 0, half),
        [(rows.shape[:1] + mine1.shape[1:], bf16 if k else f32) for k in range(half)],
        [VMEM] * (2 + len(back1)),
        mine1,
        near1,
        *back1,
        after=tuple(leaving2),
    )
    arrived = [swap(piece, 4, k, far, True) if k else piece for k, piece in enumerate(pieces)]
    return [*arrived, crossed_back], [first_columns, second_columns], (outs[0],)


def close_rows(layer_no, current, gain, returned, after=()):
    return call(
        functools.partial(close_kernel, layer_no),
        [(current.shape, bf16)] * 2,
        [VMEM] * (2 + len(returned)),
        current,
        gain,
        *returned,
        after=after,
    )


def on_device(inputs, routes, norm_gain, w_gate_up, w_down):
    experts = lax.axis_size("expert")
    sections = lax.axis_size("section")
    batches, tokens, features = inputs.shape
    layers = routes.shape[0]
    weights = load_weights(0, w_gate_up, w_down)
    if sections == 1:
        outs, routed = [], None
        current = inputs.reshape(batches * tokens, features)
        rows = open_rows(inputs, routes, norm_gain, experts)
        for layer_no in range(layers):
            returned, routed, worked = run_layer(
                rows, routed, layer_no * experts, weights, weights[2:]
            )
            if layer_no == layers - 1:
                (whole,) = call(
                    functools.partial(end_kernel, len(outs)),
                    [((layers, batches, tokens, features), bf16)],
                    [VMEM] * (1 + len(returned) + len(outs)),
                    current,
                    *returned,
                    *outs,
                )
                return whole
            weights = load_weights(layer_no + 1, w_gate_up, w_down, worked)
            current, rows = close_rows(layer_no + 1, current, norm_gain, returned, weights[2:])
            outs.append(current)
    segment_no = lax.axis_index("section")
    handed = jnp.zeros((tokens, features), bf16)
    finished = []
    for turn_no in range(batches + 1):
        if turn_no < batches:
            fresh_rows = inputs[turn_no]
        else:
            fresh_rows = jnp.zeros((tokens, features), bf16)
        current = jnp.where(segment_no == 0, fresh_rows, handed)
        batch_pick = jnp.clip(turn_no - segment_no, 0, batches - 1)
        turn_routes = lax.dynamic_slice_in_dim(routes, batch_pick, 1, 1)
        rows = open_rows(current[None], turn_routes, norm_gain, experts)
        returned, _, _ = run_layer(rows, None, 0, weights)
        result, _ = close_rows(0, current, norm_gain, returned)
        finished.append(result)
        if turn_no < batches:
            handed = from_behind(result, "section", 1)
    first_segment = jnp.stack(finished[:batches])
    second_segment = jnp.stack(finished[1:])
    return jnp.where(segment_no == 0, first_segment, second_segment)[None]


def solution(mesh):
    placed = (
        P(None, ("groups", "expert"), None),
        P("section", None, ("groups", "expert"), None),
        P("section", None),
        P("section", "expert", None, None),
        P("section", "expert", None, None),
    )
    return jax.shard_map(
        on_device,
        mesh=mesh,
        in_specs=placed,
        out_specs=P("section", None, ("groups", "expert"), None),
        check_vma=False,
    )
```

```python
import functools

import jax
import jax.numpy as jnp
from jax import lax
from jax.experimental import pallas as pl
from jax.experimental.pallas import tpu as pltpu
from jax.sharding import PartitionSpec as P

eps = 1e-06
LANES = 128
MIB = 2**20
WAIT = 6 * 10**9
VMEM = pl.BlockSpec(memory_space=pltpu.VMEM)
ANY = pl.BlockSpec(memory_space=pl.ANY)
bf16, f32 = jnp.bfloat16, jnp.float32


def from_behind(value, axis, steps):
    count = lax.axis_size(axis)
    initial, last = (max(0, -steps), min(count, count - steps))
    return lax.ppermute(value, axis, [(source, source + steps) for source in range(initial, last)])


def call(kernel, outs, specs, *operands, scratch=(), limit=8, after=(), weight=0):
    shapes = tuple(jax.ShapeDtypeStruct(shape, dtype) for shape, dtype in outs)
    operands = (*after, *operands)
    return pl.pallas_call(
        lambda *refs: kernel(*refs[len(after) :]),
        out_shape=shapes,
        in_specs=[ANY] * len(after) + specs,
        out_specs=(VMEM,) * len(outs),
        scratch_shapes=scratch,
        compiler_params=pltpu.CompilerParams(vmem_limit_bytes=limit * MIB),
        cost_estimate=pl.CostEstimate(flops=weight, bytes_accessed=0, transcendentals=0),
    )(*operands)


def swap(value, stride, step, radix, back=False):
    count = lax.axis_size("expert")

    def partner(index):
        digit = index // stride % radix
        if radix & (radix - 1) == 0:
            other = digit ^ step
        else:
            other = (digit + (step if back else radix - step)) % radix
        return index + (other - digit) * stride

    return lax.ppermute(value, "expert", [(i, partner(i)) for i in range(count)])


def join_kernel(*refs):
    *parts, whole = refs
    rows = parts[0].shape[0]
    for k, part in enumerate(parts):
        whole[k * rows : (k + 1) * rows] = part[...]


def join_rows(parts, after, weight):
    tokens, width = parts[0].shape
    return call(
        join_kernel,
        [((len(parts) * tokens, width), parts[0].dtype)],
        [VMEM] * len(parts),
        *parts,
        after=after,
        weight=weight,
    )[0]


def held(value, until):
    return lax.optimization_barrier((value, until))[0]


def sum_kernel(count, mine, *refs):
    parts, totals = refs[:count], refs[count:]
    size, rows = parts[0].shape[0], totals[0].shape[0]
    grain = min(size, rows)
    for low in range(0, mine.shape[0], grain):
        part, total = parts[low // size], totals[low // rows]
        inside = slice(low % size, low % size + grain)
        total[low % rows : low % rows + grain] = (
            mine[low : low + grain] + part[inside].astype(f32)
        ).astype(total.dtype)


def apart_kernel(first, count, mine, near, *refs):
    beside, pieces = refs[:-count], refs[-count:]
    rows = pieces[0].shape[0]
    for k, piece in enumerate(pieces):
        span = slice((first + k) * rows, (first + k + 1) * rows)
        part = beside[k][...] if len(beside) == count else beside[0][span]
        total = mine[span] + near[span].astype(f32) + part.astype(f32)
        piece[...] = total.astype(piece.dtype)


def cross_kernel(mine, near, beside, *refs):
    *arrived, out = refs
    rows = out.shape[0]
    total = mine[:rows] + near[:rows].astype(f32) + beside[...].astype(f32)
    for piece in arrived:
        total = total + piece[...].astype(f32)
    out[...] = total.astype(out.dtype)


def part_kernel(k):
    def kernel(mine, part, total):
        rows = part.shape[0]
        summed = mine[k * rows : (k + 1) * rows] + part[...].astype(f32)
        total[...] = summed.astype(total.dtype)

    return kernel


def leave_pair(found, count, after, apart=False):
    mine_near, mine_beside, other_near, *other_beside = found
    arrived_beside = [swap(half, 1, 1, 2, True) for half in other_beside]
    arrived_near = swap(other_near, 1, 1, 2, True)
    rows, width = mine_beside.shape
    if count == len(other_beside) and apart:
        shape = (rows // count, width)
        leaving = [
            call(part_kernel(k), [(shape, bf16)], [VMEM] * 2, mine_beside, part, after=after)[0]
            for k, part in enumerate(arrived_beside)
        ]
        return mine_near, arrived_near, leaving
    leaving = call(
        functools.partial(sum_kernel, len(other_beside)),
        [((rows // count, width), bf16)] * count,
        [VMEM] * (1 + len(other_beside)),
        mine_beside,
        *arrived_beside,
        after=after,
    )
    return mine_near, arrived_near, leaving


def cross_rows(mine, near, beside):
    far, count = lax.axis_size("expert") // 4, len(beside)
    shape = beside[0].shape
    hops, arrived = [], []
    if count > 1:
        hops = call(
            functools.partial(apart_kernel, 1, count - 1),
            [(shape, bf16)] * (count - 1),
            [VMEM] * (count + 1),
            mine,
            near,
            *beside[1:],
        )
        arrived = [swap(piece, 4, k, far, True) for k, piece in enumerate(hops, 1)]
    (crossing,) = call(
        cross_kernel, [(shape, bf16)], [VMEM] * (3 + len(arrived)), mine, near, beside[0], *arrived
    )
    return swap(crossing, 4, count, far, True), tuple(hops)


def normed_rows(widened, gain_row):
    scale_inv = lax.rsqrt(jnp.mean(widened * widened, axis=-1, keepdims=True) + eps)
    return (widened * scale_inv * gain_row).astype(bf16)


def open_kernel(experts, current_hbm, routes_hbm, gain_hbm, wide_ref, current, routes, gain, sems):
    pairs = ((current_hbm, current), (routes_hbm, routes), (gain_hbm, gain))
    copies = [pltpu.make_async_copy(a, b, sems.at[k]) for k, (a, b) in enumerate(pairs)]
    for copy in copies:
        copy.start()
    for copy in copies:
        copy.wait()
    features = current.shape[-1]
    layers, batches, top, tokens = routes.shape
    columns = wide_ref.shape[1] - features
    wide_ref[:, :features] = normed_rows(current[...].astype(f32), gain[0:1])
    places = lax.broadcasted_iota(jnp.int32, (columns, tokens), 0)
    same = lax.broadcasted_iota(jnp.int32, (tokens, tokens), 0) == lax.broadcasted_iota(
        jnp.int32, (tokens, tokens), 1
    )
    for batch in range(batches):
        chosen = jnp.zeros(places.shape, f32)
        for layer_no in range(layers):
            named = routes[layer_no, batch] + layer_no * experts
            for k in range(top):
                chosen = jnp.where(places == named[k : k + 1], 1.0, chosen)
        turned = lax.dot_general(
            same.astype(bf16),
            chosen.astype(bf16),
            (((1,), (1,)), ((), ())),
            preferred_element_type=f32,
        )
        wide_ref[batch * tokens : (batch + 1) * tokens, features:] = turned.astype(bf16)


def total_rows(current, kept, sent):
    total = kept[...]
    for piece in sent:
        total = total + piece[...].astype(f32)
    return (current.astype(f32) + total * 0.125).astype(bf16)


def close_kernel(layer_no, current_ref, gain_ref, kept, *refs):
    *sent, out_ref, normed_ref = refs
    out = total_rows(current_ref[...], kept, sent)
    out_ref[...] = out
    normed_ref[...] = normed_rows(out.astype(f32), gain_ref[layer_no : layer_no + 1])


def end_kernel(earlier, current_ref, kept, *refs):
    sent, before, outs_ref = refs[: len(refs) - earlier - 1], refs[-earlier - 1 : -1], refs[-1]
    layers, batches, tokens, _ = outs_ref.shape
    done = [ref[...] for ref in before] + [total_rows(current_ref[...], kept, sent)]
    for layer_no in range(layers):
        for batch in range(batches):
            outs_ref[layer_no, batch] = done[layer_no][batch * tokens : (batch + 1) * tokens]


def load_kernel(layer_no, cuts, gate_up_hbm, down_hbm, gate_up_ref, down_ref, token, sems):
    token[...] = jnp.zeros_like(token)
    copies = []
    for source, target in ((gate_up_hbm, gate_up_ref), (down_hbm, down_ref)):
        rows = target.shape[0] // cuts
        for cut in range(cuts):
            span = pl.ds(cut * rows, rows)
            copies.append(
                pltpu.make_async_copy(
                    source.at[layer_no, 0, span], target.at[span], sems.at[len(copies)]
                )
            )
    for copy in copies:
        copy.start()
    for copy in copies:
        copy.wait()


def load_weights(layer_no, w_gate_up, w_down, after=()):
    cuts = 4
    return call(
        functools.partial(load_kernel, layer_no, cuts),
        [(w_gate_up.shape[2:], bf16), (w_down.shape[2:], bf16), ((8, LANES), f32)],
        [ANY] * 2,
        in_hbm(w_gate_up),
        in_hbm(w_down),
        scratch=[pltpu.SemaphoreType.DMA((2 * cuts,))],
        limit=12,
        after=after,
    )


def tile_of(extent, most):
    size = most
    while extent % size:
        size //= 2
    return size


def expert_kernel(count, first_column, wide, *refs):
    parts, refs = refs[:count], refs[count:]
    if wide:
        gate_up_ref, down_ref, *outs, routed_ref, rows_ref, hidden_ref = refs
    else:
        routed_ref, gate_up_ref, down_ref, *outs, rows_ref, hidden_ref = refs
    hidden_size, features = down_ref.shape
    first = 0
    for part in parts:
        span = slice(first, first + part.shape[0])
        first += part.shape[0]
        rows_ref[span] = part[:, :features]
        if wide:
            routed_ref[span] = part[:, features:]
    places = lax.broadcasted_iota(jnp.int32, routed_ref.shape, 1)
    column = first_column + lax.axis_index("expert")
    chosen = jnp.where(places == column, routed_ref[...].astype(f32), 0.0)
    share = jnp.sum(chosen, axis=1, keepdims=True)
    rows = rows_ref[...]
    size = tile_of(hidden_size, 256)
    for low in range(0, hidden_size, size):
        span, beside = slice(low, low + size), slice(hidden_size + low, hidden_size + low + size)
        gate = jnp.dot(rows, gate_up_ref[:, span], preferred_element_type=f32)
        up = jnp.dot(rows, gate_up_ref[:, beside], preferred_element_type=f32)
        hidden_ref[:, span] = (gate / (1.0 + jnp.exp(-gate)) * up).astype(bf16)
    hidden = hidden_ref[...]
    size = tile_of(features, 512)
    for low in range(0, features, size):
        span = slice(low, low + size)
        done = jnp.dot(hidden, down_ref[:, span], preferred_element_type=f32) * share
        first = 0
        for out in outs:
            out[:, span] = done[first : first + out.shape[0]].astype(out.dtype)
            first += out.shape[0]


def run_expert(parts, routed, first_column, weights, after):
    gate_up, down_proj, _ = weights
    hidden_size, features = down_proj.shape
    width = parts[0].shape[1]
    count = sum(part.shape[0] for part in parts)
    quarter = count // 4
    wide = routed is None
    outs = [((quarter, features), f32)] * 2 + [((quarter, features), bf16)]
    outs += [((quarter // 2, features), bf16)] * 2
    if wide:
        outs = outs + [((count, width - features), bf16)]
    found = call(
        functools.partial(expert_kernel, len(parts), first_column, wide),
        outs,
        [VMEM] * (len(parts) + (2 if wide else 3)),
        *parts,
        *([] if wide else [routed]),
        gate_up,
        down_proj,
        scratch=[pltpu.VMEM((count, features), bf16), pltpu.VMEM((count, hidden_size), bf16)],
        limit=24,
        after=after,
    )
    return found[:5], found[5] if wide else routed


def in_hbm(array):
    return pltpu.with_memory_space_constraint(array, pltpu.HBM)


def open_rows(current, routes, gain, experts):
    batches, tokens, features = current.shape
    rows = batches * tokens
    columns = routes.shape[0] * experts
    width = features + columns + -columns % LANES
    current, routes = current.reshape(rows, features), jnp.swapaxes(routes, 2, 3)
    (wide,) = call(
        functools.partial(open_kernel, experts),
        [((rows, width), bf16)],
        [ANY] * 3,
        in_hbm(current),
        in_hbm(routes),
        in_hbm(gain),
        scratch=[
            pltpu.VMEM(current.shape, bf16),
            pltpu.VMEM(routes.shape, jnp.int32),
            pltpu.VMEM(gain.shape, f32),
            pltpu.SemaphoreType.DMA((3,)),
        ],
    )
    return wide


def run_layer(rows, routed, first_column, weights, loaded=()):
    far = lax.axis_size("expert") // 4
    routed = routed or [None, None]
    half = far // 2
    sent = [rows] + [swap(rows, 4, k, far) for k in range(1, half)]
    first = join_rows(sent, loaded, 0)
    first_beside = swap(first, 2, 1, 2)
    crossed = join_rows([swap(rows, 4, half, far)], (first,), WAIT)
    second = [crossed] + [swap(crossed, 4, k, far) for k in range(1, half)]
    second_beside = [swap(crossed, 2, 1, 2)]
    for piece in second[1:]:
        second_beside.append(swap(held(piece, (second_beside[0], first_beside)), 2, 1, 2))

    def worked(near, beside, routed, after):
        parts = near + beside
        parts += [swap(piece, 1, 1, 2) for piece in parts]
        return run_expert(parts, routed, first_column, weights, after)

    first_beside = held(first_beside, (second[-1], second_beside[0]))
    outs, first_columns = worked([first], [first_beside], routed[0], (second[-1],))
    mine1, near1, leaving1 = leave_pair(outs, half, ())
    second_beside[-1] = held(second_beside[-1], outs[0])
    outs, second_columns = worked(second, second_beside, routed[1], tuple(leaving1))
    mine2, near2, leaving2 = leave_pair(outs, half, (), True)
    back2 = [swap(piece, 2, 1, 2, True) for piece in leaving2]
    crossed_back, hops = cross_rows(mine2, near2, back2)
    back1 = [swap(held(piece, hops), 2, 1, 2, True) for piece in leaving1]
    pieces = call(
        functools.partial(apart_kernel, 0, half),
        [(rows.shape[:1] + mine1.shape[1:], bf16 if k else f32) for k in range(half)],
        [VMEM] * (2 + len(back1)),
        mine1,
        near1,
        *back1,
        after=tuple(leaving2),
    )
    arrived = [swap(piece, 4, k, far, True) if k else piece for k, piece in enumerate(pieces)]
    return [*arrived, crossed_back], [first_columns, second_columns], (outs[0],)


def close_rows(layer_no, current, gain, returned, after=()):
    return call(
        functools.partial(close_kernel, layer_no),
        [(current.shape, bf16)] * 2,
        [VMEM] * (2 + len(returned)),
        current,
        gain,
        *returned,
        after=after,
    )


def on_device(inputs, routes, norm_gain, w_gate_up, w_down):
    experts = lax.axis_size("expert")
    sections = lax.axis_size("section")
    batches, tokens, features = inputs.shape
    layers = routes.shape[0]
    weights = load_weights(0, w_gate_up, w_down)
    if sections == 1:
        outs, routed = [], None
        current = inputs.reshape(batches * tokens, features)
        rows = open_rows(inputs, routes, norm_gain, experts)
        for layer_no in range(layers):
            returned, routed, worked = run_layer(
                rows, routed, layer_no * experts, weights, weights[2:]
            )
            if layer_no == layers - 1:
                (whole,) = call(
                    functools.partial(end_kernel, len(outs)),
                    [((layers, batches, tokens, features), bf16)],
                    [VMEM] * (1 + len(returned) + len(outs)),
                    current,
                    *returned,
                    *outs,
                )
                return whole
            weights = load_weights(layer_no + 1, w_gate_up, w_down, worked)
            current, rows = close_rows(layer_no + 1, current, norm_gain, returned, weights[2:])
            outs.append(current)
    segment_no = lax.axis_index("section")
    handed = jnp.zeros((tokens, features), bf16)
    finished = []
    for turn_no in range(batches + 1):
        if turn_no < batches:
            fresh_rows = inputs[turn_no]
        else:
            fresh_rows = jnp.zeros((tokens, features), bf16)
        current = jnp.where(segment_no == 0, fresh_rows, handed)
        batch_pick = jnp.clip(turn_no - segment_no, 0, batches - 1)
        turn_routes = lax.dynamic_slice_in_dim(routes, batch_pick, 1, 1)
        rows = open_rows(current[None], turn_routes, norm_gain, experts)
        returned, _, _ = run_layer(rows, None, 0, weights)
        result, _ = close_rows(0, current, norm_gain, returned)
        finished.append(result)
        if turn_no < batches:
            handed = from_behind(result, "section", 1)
    first_segment = jnp.stack(finished[:batches])
    second_segment = jnp.stack(finished[1:])
    return jnp.where(segment_no == 0, first_segment, second_segment)[None]


def solution(mesh):
    placed = (
        P(None, ("groups", "expert"), None),
        P("section", None, ("groups", "expert"), None),
        P("section", None),
        P("section", "expert", None, None),
        P("section", "expert", None, None),
    )
    return jax.shard_map(
        on_device,
        mesh=mesh,
        in_specs=placed,
        out_specs=P("section", None, ("groups", "expert"), None),
        check_vma=False,
    )
```
